512 devices in a mesh: gx: 8 (over y, core), gy: 4 (over x), gz: 16 (over z).
Axes of the slice: x: 4, y: 4, z: 16, core: 2. Of those that a mesh axis runs over, the one named last changes fastest.
Arguments:
- jump_rhs: float32 [8, 4, 16, 3, 16, 128], P('gx', 'gy', 'gz'), may hold values from -40 to 40
- flex_diag: float32 [8, 4, 16, 6, 128, 128], P('gx', 'gy', 'gz'), may hold values from -0.5 to 4.5, as said below
- flex_couple: float32 [8, 4, 16, 6, 128, 128], P('gx', 'gy', 'gz'), may hold values from -0.2 to 0.2
- dirichlet_diag: float32 [8, 4, 16, 6, 128, 128], P('gx', 'gy', 'gz'), may hold values from -0.5 to 4.5, as said below
- dirichlet_couple: float32 [8, 4, 16, 6, 128, 128], P('gx', 'gy', 'gz'), may hold values from -0.2 to 0.2
- face_pairs: int32 [8, 4, 16, 6, 2], P('gx', 'gy', 'gz'), may hold values from 0 to 5, as said below
- corner_coupling: float32 [8, 4, 16, 24, 768], P('gx', 'gy', 'gz'), may hold values from -0.21875 to 0.21875
- coarse_ids: int32 [8, 4, 16, 8], P('gx', 'gy', 'gz'), may hold values from 0 to 191, as said below
- partner: int32 [8, 4, 16, 3, 128], P('gx', 'gy', 'gz'), may hold values from 0 to 127, as said below
- coarse_inverse: float32 [576, 576], replicated, may hold values from -0.5 to 3.5, as said below
Outputs:
- multipliers: float32 [8, 4, 16, 3, 16, 128], P('gx', 'gy', 'gz')
- residual: float32 [8, 4, 16, 3, 16, 128], P('gx', 'gy', 'gz')
The draws below stay inside these ranges and needn't reach their ends.
Inputs may be any that keep to these rules, and one draw needn't show every extreme that they name: Each row of 128 entries is a permutation: dof k of a subdomain's upper face along d matches dof partner[k] of the next subdomain's lower face. `face_pairs`: each subdomain lists 6 different pairs of its 6 faces, the first number below the second. `coarse_ids`: corners of neighbouring subdomains that coincide carry the same aggregate. `flex_diag`: each block is symmetric, and each subdomain's assembled face operator is symmetric positive definite. `dirichlet_diag`: each block is symmetric, and each subdomain's assembled face operator is symmetric positive definite. `coarse_inverse`: symmetric positive definite.
All inputs are finite; a program needn't handle non-finite values.
Results may differ from the reference program's by a relative error of at most 0.0003.
Values sent between devices are 32-bit elements; how exact they have to be, the bound alone decides.
No kernel may reach another device: no remote copies, remote signals or barrier semaphores. Data moves between devices by JAX's collectives and lax.ppermute only.
A program may use at most 64 MiB of HBM per device.

```python
import math
import jax
import jax.numpy as jnp
import numpy as np
from jax import lax

FD = 128
CASES = 16
NOFF = 6
CORN = 24
NCP = 192
ITERS = 3
NX = 8
NY = 4
NZ = 16
CDOF = 576


def signed_orders(key, block_count, block_width):
    key_list = jax.random.split(key, block_count)
    orders = jax.vmap(lambda single: jax.random.permutation(single, block_width))(key_list)
    flip_bits = jax.random.bernoulli(jax.random.fold_in(key, 7), 0.5, (block_count, block_width))
    sign_values = jnp.where(flip_bits, 1.0, -1.0).astype(jnp.float32)
    columns = jnp.arange(block_width)
    return sign_values[:, :, None] * (orders[:, :, None] == columns[None, None, :]).astype(jnp.float32)


def symmetric_blocks(key, block_count, block_width, diag_low, diag_high, mix_low, mix_high, noise_bound):
    signed = signed_orders(jax.random.fold_in(key, 1), block_count, block_width)
    symmetric = 0.5 * (signed + jnp.swapaxes(signed, 1, 2))
    raw_noise = jax.random.uniform(jax.random.fold_in(key, 2), (block_count, block_width, block_width), jnp.float32, -noise_bound, noise_bound)
    small_noise = 0.5 * (raw_noise + jnp.swapaxes(raw_noise, 1, 2))
    mix_scale = jax.random.uniform(jax.random.fold_in(key, 3), (block_count, 1, 1), jnp.float32, mix_low, mix_high)
    diagonal = jnp.exp(jax.random.uniform(jax.random.fold_in(key, 4), (block_count, block_width), jnp.float32, math.log(diag_low), math.log(diag_high)))
    identity = (jnp.arange(block_width)[:, None] == jnp.arange(block_width)[None, :]).astype(jnp.float32)
    return identity[None, :, :] * diagonal[:, :, None] + mix_scale * symmetric + small_noise


def coupling_blocks(key, block_count, block_width):
    signed = signed_orders(jax.random.fold_in(key, 1), block_count, block_width)
    mix_scale = jax.random.uniform(jax.random.fold_in(key, 3), (block_count, 1, 1), jnp.float32, 0.08, 0.15)
    raw_noise = jax.random.uniform(jax.random.fold_in(key, 2), (block_count, block_width, block_width), jnp.float32, -1.0 / 2048, 1.0 / 2048)
    return mix_scale * signed + raw_noise


def draw_jump_rhs(key, part):
    key = jax.random.fold_in(key, 11)
    shape = (NX, NY, NZ, 3, CASES, FD)
    depth_ramp = 0.5 + jnp.arange(NZ, dtype=jnp.float32) / max(NZ - 1, 1)
    depth_ramp = depth_ramp[None, None, :, None, None, None]
    case_scale = jnp.exp(jax.random.uniform(jax.random.fold_in(key, 1), (CASES,), jnp.float32, math.log(0.3), math.log(3.0)))
    case_scale = case_scale[:, None]
    base_values = jnp.clip(jax.random.normal(jax.random.fold_in(key, 2), shape, jnp.float32), -5.0, 5.0)
    values = base_values * depth_ramp * case_scale
    return values


def draw_flex_diag(key, part):
    key = jax.random.fold_in(key, 31)
    return symmetric_blocks(key, NX * NY * NZ * 6, FD, 1.5, 4.0, 0.15, 0.25, 1.0 / 2048).reshape(NX, NY, NZ, 6, FD, FD)


def draw_flex_couple(key, part):
    key = jax.random.fold_in(key, 32)
    return coupling_blocks(key, NX * NY * NZ * NOFF, FD).reshape(NX, NY, NZ, NOFF, FD, FD)


def draw_dirichlet_diag(key, part):
    key = jax.random.fold_in(key, 41)
    return symmetric_blocks(key, NX * NY * NZ * 6, FD, 1.5, 4.0, 0.15, 0.25, 1.0 / 2048).reshape(NX, NY, NZ, 6, FD, FD)


def draw_dirichlet_couple(key, part):
    key = jax.random.fold_in(key, 42)
    return coupling_blocks(key, NX * NY * NZ * NOFF, FD).reshape(NX, NY, NZ, NOFF, FD, FD)


def draw_coarse_inverse(key, part):
    key = jax.random.fold_in(key, 51)
    return symmetric_blocks(key, 1, CDOF, 1.0, 3.0, 0.2, 0.3, 1.0 / 8192).reshape(CDOF, CDOF)


def draw_face_pairs(key, part):
    key = jax.random.fold_in(key, 61)
    pair_table = jnp.asarray(np.array([[a, b] for a in range(6) for b in range(a + 1, 6)], dtype=np.int32))
    key_list = jax.random.split(key, NX * NY * NZ)
    chosen = jax.vmap(lambda single: jax.random.permutation(single, 15)[:NOFF])(key_list)
    return pair_table[chosen].reshape(NX, NY, NZ, NOFF, 2).astype(jnp.int32)


def draw_partner(key, part):
    key = jax.random.fold_in(key, 71)
    key_list = jax.random.split(key, NX * NY * NZ * 3)
    orders = jax.vmap(lambda single: jax.random.permutation(single, FD))(key_list)
    return orders.reshape(NX, NY, NZ, 3, FD).astype(jnp.int32)


def draw_coarse_ids(key, part):
    key = jax.random.fold_in(key, 81)
    points = (NX + 1) * (NY + 1) * (NZ + 1)
    shuffled = jax.random.permutation(key, points).astype(jnp.int32)
    aggregate_table = (shuffled % NCP).astype(jnp.int32).reshape(NX + 1, NY + 1, NZ + 1)
    corners = []
    for lift_z in range(2):
        for lift_y in range(2):
            for lift_x in range(2):
                corners.append(aggregate_table[lift_x:lift_x + NX, lift_y:lift_y + NY, lift_z:lift_z + NZ])
    return jnp.stack(corners, axis=-1).astype(jnp.int32)


def shard_levels(stream_key, dims, shards, low, high):
    def one(position, parts):
        heights = jax.random.uniform(jax.random.fold_in(jax.random.fold_in(stream_key, 6), position), (parts,), jnp.float32, low / len(shards), high / len(shards))
        return jnp.repeat(jnp.exp(heights), dims[position] // parts).reshape((-1,) + (1,) * (len(dims) - position - 1))

    loudness = one(*shards[0])
    for cut in shards[1:]:
        loudness = loudness * one(*cut)
    return loudness


def normal_values(own_key, dims, deviation, most, cuts=(), kind=jnp.bfloat16):
    gain = shard_levels(own_key, dims, cuts, -0.22, 0.18) if cuts else 1.0
    entries = jax.random.normal(own_key, dims, jnp.float32) * deviation * gain
    return jnp.minimum(jnp.maximum(entries, -most), most).astype(kind)


def setup_inputs(seed: int = 0) -> dict:
    splits = jax.random.split(jax.random.key(seed), 11)
    jump_rhs = draw_jump_rhs(jax.random.fold_in(splits[10], 71), 0)
    flex_diag = draw_flex_diag(jax.random.fold_in(splits[10], 71), 0)
    flex_couple = draw_flex_couple(jax.random.fold_in(splits[10], 71), 0)
    dirichlet_diag = draw_dirichlet_diag(jax.random.fold_in(splits[10], 71), 0)
    dirichlet_couple = draw_dirichlet_couple(jax.random.fold_in(splits[10], 71), 0)
    face_pairs = draw_face_pairs(jax.random.fold_in(splits[10], 71), 0)
    corner_coupling = normal_values(splits[6], (NX, NY, NZ, CORN, 6 * FD), (6 * FD) ** -0.5, 0.21875, ((0, 8), (1, 4), (2, 16)), jnp.float32)
    coarse_ids = draw_coarse_ids(jax.random.fold_in(splits[10], 71), 0)
    partner = draw_partner(jax.random.fold_in(splits[10], 71), 0)
    coarse_inverse = draw_coarse_inverse(jax.random.fold_in(splits[10], 71), 0)
    return {"jump_rhs": jump_rhs, "flex_diag": flex_diag, "flex_couple": flex_couple, "dirichlet_diag": dirichlet_diag, "dirichlet_couple": dirichlet_couple, "face_pairs": face_pairs, "corner_coupling": corner_coupling, "coarse_ids": coarse_ids, "partner": partner, "coarse_inverse": coarse_inverse}


HIGHEST = lax.Precision.HIGHEST


def lower_shift(values, direction):
    extent = values.shape[direction]
    zero_rim = jnp.zeros_like(lax.slice_in_dim(values, 0, 1, axis=direction))
    return jnp.concatenate([zero_rim, lax.slice_in_dim(values, 0, extent - 1, axis=direction)], axis=direction)


def upper_shift(values, direction):
    extent = values.shape[direction]
    zero_rim = jnp.zeros_like(lax.slice_in_dim(values, 0, 1, axis=direction))
    return jnp.concatenate([lax.slice_in_dim(values, 1, extent, axis=direction), zero_rim], axis=direction)


def inner_mask():
    along_x = jnp.broadcast_to(jnp.arange(NX)[:, None, None] < NX - 1, (NX, NY, NZ))
    along_y = jnp.broadcast_to(jnp.arange(NY)[None, :, None] < NY - 1, (NX, NY, NZ))
    along_z = jnp.broadcast_to(jnp.arange(NZ)[None, None, :] < NZ - 1, (NX, NY, NZ))
    return jnp.stack([along_x, along_y, along_z], axis=3).astype(jnp.float32)[:, :, :, :, None, None]


def spread(field, partner):
    inverse = jnp.argsort(partner, axis=-1).astype(jnp.int32)
    gather_index = jnp.broadcast_to(inverse[:, :, :, :, None, :], field.shape)
    permuted = jnp.take_along_axis(field, gather_index, axis=-1)
    faces = []
    for direction in range(3):
        faces.append(-lower_shift(permuted[:, :, :, direction], direction))
        faces.append(field[:, :, :, direction])
    return jnp.stack(faces, axis=3)


def jump_trace(displaced, partner):
    jump_parts = []
    for direction in range(3):
        from_above = upper_shift(displaced[:, :, :, 2 * direction], direction)
        gather_index = jnp.broadcast_to(partner[:, :, :, direction][:, :, :, None, :], from_above.shape).astype(jnp.int32)
        matched = jnp.take_along_axis(from_above, gather_index, axis=-1)
        jump_parts.append(displaced[:, :, :, 2 * direction + 1] - matched)
    return jnp.stack(jump_parts, axis=3)


def apply_blocks(face_loads, diagonal, couple, pairs):
    result = jnp.einsum('nfcm,nfmk->nfck', face_loads, diagonal, precision=HIGHEST)
    first_face = pairs[:, :, 0]
    second_face = pairs[:, :, 1]
    target = (pairs.shape[0], pairs.shape[1]) + face_loads.shape[2:]
    take_first = jnp.take_along_axis(face_loads, jnp.broadcast_to(first_face[:, :, None, None], target), axis=1)
    take_second = jnp.take_along_axis(face_loads, jnp.broadcast_to(second_face[:, :, None, None], target), axis=1)
    to_first = jnp.einsum('nkcm,nkml->nkcl', take_second, couple, precision=HIGHEST)
    to_second = jnp.einsum('nkcl,nkml->nkcm', take_first, couple, precision=HIGHEST)
    face_range = jnp.arange(face_loads.shape[1])
    hit_first = (first_face[:, :, None] == face_range[None, None, :]).astype(jnp.float32)
    hit_second = (second_face[:, :, None] == face_range[None, None, :]).astype(jnp.float32)
    result = result + jnp.einsum('nkf,nkcl->nfcl', hit_first, to_first, precision=HIGHEST)
    result = result + jnp.einsum('nkf,nkcl->nfcl', hit_second, to_second, precision=HIGHEST)
    return result


def column_blocks(face_loads, diagonal, couple, pairs):
    def one_column(packed):
        return apply_blocks(packed[0], packed[1], packed[2], packed[3])

    shaped = (face_loads.reshape((NX * NY, NZ) + face_loads.shape[3:]),
              diagonal.reshape((NX * NY, NZ) + diagonal.shape[3:]),
              couple.reshape((NX * NY, NZ) + couple.shape[3:]),
              pairs.reshape((NX * NY, NZ) + pairs.shape[3:]))
    return lax.map(one_column, shaped).reshape(face_loads.shape)


def coarse_correction(face_loads, corner_coupling, coarse_ids, coarse_inverse):
    sub_total = NX * NY * NZ
    coupling = corner_coupling.reshape(sub_total, CORN, 6, FD)
    flat_loads = face_loads.reshape((sub_total,) + face_loads.shape[3:])
    corner_load = jnp.einsum('nrfm,nfcm->nrc', coupling, flat_loads, precision=HIGHEST)
    corner_ids = coarse_ids.reshape(sub_total, 8).astype(jnp.int32)
    one_hot = (corner_ids[:, :, None] == jnp.arange(NCP)[None, None, :]).astype(jnp.float32)
    grouped = corner_load.reshape(sub_total, 8, 3, CASES)
    gathered = jnp.einsum('njdc,njp->cdp', grouped, one_hot, precision=HIGHEST).reshape(CASES, 3 * NCP)
    coarse_values = jnp.dot(gathered, coarse_inverse, precision=HIGHEST)
    column_index = (jnp.arange(3)[None, None, :] * NCP + corner_ids[:, :, None]).astype(jnp.int32)
    picked = jnp.take(coarse_values, column_index.reshape(-1), axis=1).reshape(CASES, sub_total, 8, 3)
    corner_values = jnp.transpose(picked, (1, 2, 3, 0)).reshape(sub_total, CORN, CASES)
    correction = jnp.einsum('nrc,nrfm->nfcm', corner_values, coupling, precision=HIGHEST)
    return correction.reshape(face_loads.shape)


def case_sums(left, right):
    return jnp.sum(left * right, axis=(0, 1, 2, 3, 5))


def reference(jump_rhs, flex_diag, flex_couple, dirichlet_diag, dirichlet_couple, face_pairs, corner_coupling, coarse_ids, partner, coarse_inverse):
    inner = inner_mask()

    def flexibility(field):
        face_loads = spread(field, partner)
        displaced = column_blocks(face_loads, flex_diag, flex_couple, face_pairs)
        displaced = displaced + coarse_correction(face_loads, corner_coupling, coarse_ids, coarse_inverse)
        return jump_trace(displaced, partner) * inner

    def dirichlet(field):
        face_loads = spread(field, partner)
        answer = column_blocks(face_loads, dirichlet_diag, dirichlet_couple, face_pairs)
        return 0.25 * jump_trace(answer, partner) * inner

    residual = jump_rhs * inner
    multipliers = jnp.zeros_like(residual)
    preconditioned = dirichlet(residual)
    search = preconditioned
    norm_now = case_sums(residual, preconditioned)
    for iteration in range(ITERS):
        applied = flexibility(search)
        step_size = (norm_now / case_sums(search, applied))[:, None]
        multipliers = multipliers + step_size * search
        residual = residual - step_size * applied
        if iteration + 1 < ITERS:
            preconditioned = dirichlet(residual)
            norm_next = case_sums(residual, preconditioned)
            search = preconditioned + (norm_next / norm_now)[:, None] * search
            norm_now = norm_next
    return multipliers, residual
```

```python
import functools

import jax
import jax.numpy as jnp
from jax import lax
from jax.experimental import pallas as pl
from jax.experimental.pallas import tpu as pltpu
from jax.sharding import PartitionSpec as P

ITERS = 3
CASES = 16
FD = 128
WIDE = 6 * FD
QPAD = 256
SUBS = 32
PLANE = ("gx", "gy")
F32 = jnp.float32
BF16 = jnp.bfloat16
VMEM = pl.BlockSpec(memory_space=pltpu.VMEM)
SMEM = pl.BlockSpec(memory_space=pltpu.SMEM)


def call(kernel, outs, *args, smem=0, scratch=()):
    return pl.pallas_call(
        kernel,
        out_shape=[jax.ShapeDtypeStruct(shape, dtype) for shape, dtype in outs],
        in_specs=[SMEM] * smem + [VMEM] * (len(args) - smem),
        out_specs=[VMEM] * len(outs),
        scratch_shapes=list(scratch),
        compiler_params=pltpu.CompilerParams(vmem_limit_bytes=40 * 1024 * 1024),
    )(*args)


def halves(x):
    high = x.astype(BF16)
    return high, (x - high.astype(F32)).astype(BF16)


def dot_exact(x, selector):
    rows = x.shape[0]
    high, low = halves(x)
    both = jnp.dot(jnp.concatenate([high, low], 0), selector, preferred_element_type=F32)
    return both[:rows] + both[rows:]


def dot_split(x, high_ref, low_ref):
    rows = x.shape[0]
    high, low = halves(x)
    both = jnp.dot(jnp.concatenate([high, low], 0), high_ref[...], preferred_element_type=F32)
    rest = jnp.dot(high, low_ref[...], preferred_element_type=F32)
    return both[:rows] + both[rows:] + rest


def face(x, f):
    return x[:, f * FD:(f + 1) * FD]


def take(x, row):
    index = jnp.broadcast_to(row.astype(jnp.int32), x.shape)
    return jnp.take_along_axis(x, index, axis=1, mode="promise_in_bounds")


def lower_changed(x, rows):
    parts = []
    for d in range(3):
        parts.append(-take(face(x, 2 * d), rows[d]))
        parts.append(face(x, 2 * d + 1))
    return jnp.concatenate(parts, axis=1)


def partner_rows(messages):
    return [m[CASES:CASES + 1, :] for m in messages]


def inverse_rows(messages):
    return [m[CASES + 1:CASES + 2, :] for m in messages]


def apply_dense(field, messages, high_ref, low_ref):
    loads = lower_changed(field, inverse_rows(messages))
    return loads, lower_changed(dot_split(loads, high_ref, low_ref), partner_rows(messages))


def put_plane(spots, slots_ref, piece, gy):
    here = spots[0]
    for f, by in ((0, -gy), (1, gy), (2, -1), (3, 1)):
        @pl.when(spots[2 + f] > 0)
        def _():
            value = piece(f)
            slots_ref[here + by, 0:value.shape[0], :] = value


def take_plane(spots, slots_ref, f, gy, rows):
    here = spots[0]
    by = (-gy, gy, -1, 1)[f]
    spot = jnp.where(spots[2 + f] > 0, here + by, here)
    return slots_ref[spot, rows, :]


def prep_kernel(spots, rhs_ref, partner_ref, message_ref):
    for d in range(3):
        inner = spots[3 + 2 * d].astype(F32)
        row = partner_ref[d:d + 1, :]
        message_ref[d, 0:CASES, :] = rhs_ref[d] * inner
        wanted = lax.broadcasted_iota(jnp.int32, (FD, FD), 0)
        hits = (wanted == jnp.broadcast_to(row, (FD, FD))).astype(F32).astype(BF16)
        count = lax.broadcasted_iota(jnp.int32, (16, FD), 1).astype(F32).astype(BF16)
        inverse = lax.dot_general(
            count, hits, (((1,), (1,)), ((), ())), preferred_element_type=F32
        )
        message_ref[d, CASES:CASES + 1, :] = row.astype(F32)
        message_ref[d, CASES + 1:CASES + 2, :] = inverse[0:1, :]
        message_ref[d, CASES + 2:CASES + 8, :] = jnp.zeros((6, FD), F32)


def build_kernel(pairs, diag_ref, couple_ref, high_ref, low_ref):
    high_ref[...] = jnp.zeros_like(high_ref)
    low_ref[...] = jnp.zeros_like(low_ref)

    def put(row_face, col_face, block):
        high, low = halves(block)
        if isinstance(row_face, int):
            rows, cols = row_face * FD, col_face * FD
        else:
            rows = pl.multiple_of(row_face * FD, FD)
            cols = pl.multiple_of(col_face * FD, FD)
        high_ref[pl.ds(rows, FD), pl.ds(cols, FD)] = high
        low_ref[pl.ds(rows, FD), pl.ds(cols, FD)] = low

    for f in range(6):
        put(f, f, diag_ref[f])
    for k in range(6):
        first, second = pairs[2 * k], pairs[2 * k + 1]
        block = couple_ref[k]
        put(second, first, block)
        put(first, second, block.T)


def split_kernel(matrix_ref, high_ref, low_ref):
    high, low = halves(matrix_ref[...])
    high_ref[...] = high
    low_ref[...] = low


def corner_kernel(ids, coupling_ref, wh_ref, wl_ref, expand_ref, pad):
    pad[...] = jnp.zeros_like(pad)
    pad[0:24, :] = coupling_ref[...]
    for f in range(6):
        high, low = halves(pad[:, f * FD:(f + 1) * FD].T)
        wh_ref[f * FD:(f + 1) * FD, :] = high
        wl_ref[f * FD:(f + 1) * FD, :] = low
    pad[...] = jnp.zeros_like(pad)
    lanes = lax.broadcasted_iota(jnp.int32, (1, 3 * QPAD), 1)
    for r in range(24):
        spot = (r % 3) * QPAD + ids[r // 3]
        pad[r:r + 1, :] = (lanes == spot).astype(F32)
    expand_ref[...] = pad[...].astype(BF16)


def start_kernel(gy, spots, ids, rhs_ref, mx_ref, my_ref, mz_ref, dh_ref, dl_ref, coupling_ref,
                 field_ref, shown_ref, own_ref, slots_ref, up_ref, down_ref):
    messages = (mx_ref, my_ref, mz_ref)
    parts = []
    for d in range(3):
        parts.append(messages[d][0:CASES, :])
        parts.append(rhs_ref[d] * spots[3 + 2 * d].astype(F32))
    field = jnp.concatenate(parts, axis=1)
    field_ref[...] = field
    _, shown = apply_dense(field, messages, dh_ref, dl_ref)
    shown_ref[...] = shown
    own = lower_changed(coupling_ref[...], partner_rows(messages))
    own_ref[...] = own
    lanes = lax.broadcasted_iota(jnp.int32, (8, FD), 1) % SUBS
    target = jnp.full((8, FD), -1, jnp.int32)
    for r in range(24):
        target = jnp.where(lanes == r, (r % 3) * QPAD + ids[r // 3], target)
    target = target.astype(F32)

    def piece(f):
        return jnp.concatenate([face(shown, f), face(own, f), target], axis=0)

    slots_ref[...] = jnp.zeros_like(slots_ref)
    put_plane(spots, slots_ref, piece, gy)
    down_ref[...] = piece(4)
    up_ref[...] = piece(5)


def joint_kernel(gy, spots, ids, own_ref, slots_ref, low_ref, top_ref, gh_ref, gl_ref, pick_ref, whole):
    whole[...] = jnp.zeros_like(whole)
    whole[0:24, :] = own_ref[...]
    lanes = lax.broadcasted_iota(jnp.int32, (8, FD), 1)
    target = jnp.full((8, FD), -1, jnp.int32)
    for r in range(24):
        target = jnp.where(lanes % SUBS == r, (r % 3) * QPAD + ids[r // 3], target)
    targets = [target.astype(F32)]
    for f in range(6):
        if f < 4:
            other = take_plane(spots, slots_ref, f, gy, slice(CASES, CASES + 32))
        else:
            other = (low_ref, top_ref)[f - 4][CASES:CASES + 32, :]
        there = spots[2 + f].astype(F32)
        whole[SUBS * (f + 1):SUBS * (f + 1) + 24, f * FD:(f + 1) * FD] = other[0:24, :] * there
        targets.append(other[24:32, :] * there)
    high, low = halves(whole[...])
    gh_ref[...] = high
    gl_ref[...] = low
    rows = lax.broadcasted_iota(jnp.int32, (3 * QPAD, FD), 0)
    for half in range(2):
        wanted = jnp.full((8, FD), -1.0, F32)
        for n in range(4 * half, min(4 * half + 4, 7)):
            wanted = jnp.where(lanes // SUBS == n % 4, targets[n], wanted)
        wanted = jnp.broadcast_to(wanted[0:1, :].astype(jnp.int32), (3 * QPAD, FD))
        pick_ref[:, half * FD:(half + 1) * FD] = (rows == wanted).astype(F32).astype(BF16)


def load_kernel(gy, first, spots, mask_ref, mx_ref, my_ref, mz_ref, shown_ref, slots_ref, low_ref,
                top_ref, residual_ref, fh_ref, fl_ref, wh_ref, wl_ref, expand_ref, *rest):
    if first:
        z_ref, flexed_ref, out_ref = rest
    else:
        search_ref, applied_ref, z_ref, flexed_ref, out_ref = rest
    messages = (mx_ref, my_ref, mz_ref)
    head = slice(0, CASES)
    across = [take_plane(spots, slots_ref, f, gy, head) for f in range(4)]
    across += [low_ref[head, :], top_ref[head, :]]
    mask = mask_ref[...]
    z = 0.25 * (shown_ref[...] + jnp.concatenate(across, axis=1)) * mask
    z_ref[...] = z
    loads, flexed = apply_dense(z, messages, fh_ref, fl_ref)
    flexed_ref[...] = flexed
    corner = dot_split(loads, wh_ref, wl_ref)
    gathered = dot_exact(corner, expand_ref[...])

    def upper_sum(a):
        return jnp.sum(face(a, 1) + face(a, 3) + face(a, 5), axis=1, keepdims=True)

    sums = [upper_sum(z * residual_ref[...]), jnp.sum(z * flexed, axis=1, keepdims=True)]
    if not first:
        sums.append(
            upper_sum(z * applied_ref[...])
            + jnp.sum(search_ref[...] * flexed, axis=1, keepdims=True)
        )
    lanes = lax.broadcasted_iota(jnp.int32, (CASES, FD), 1)
    out_ref[...] = jnp.zeros_like(out_ref)
    for b in range(6):
        block = face(gathered, b)
        if b == 1:
            for t, value in enumerate(sums):
                block = jnp.where(lanes == 64 + t, value, block)
        for h in range(2):
            out_ref[2 * b + h, CASES:CASES + 8, :] = block[8 * h:8 * h + 8, :]
    put_plane(spots, out_ref, lambda f: face(flexed, f), gy)


def layer_kernel(spots, slots_ref, flexed_ref, out_ref):
    total = jnp.sum(slots_ref[:, CASES:CASES + 8, :], axis=0)
    out_ref[...] = jnp.zeros_like(out_ref)
    for i in range(out_ref.shape[0]):
        out_ref[i, CASES:CASES + 8, :] = total
    for f, by in ((4, -1), (5, 1)):
        @pl.when(spots[2 + f] > 0)
        def _():
            out_ref[spots[1] + by, 0:CASES, :] = flexed_ref[:, f * FD:(f + 1) * FD]


def spread_kernel(slots_ref, out_ref):
    total = jnp.sum(slots_ref[:, CASES:CASES + 8, :], axis=0)
    for i in range(out_ref.shape[0]):
        out_ref[i] = total


def step_kernel(gy, first, last, spots, mask_ref, total_ref, slots_ref, layers_ref, flexed_ref,
                z_ref, residual_ref, kh_ref, kl_ref, gh_ref, gl_ref, pick_ref, *rest):
    rest = list(rest)
    if not last:
        mx_ref, my_ref, mz_ref, dh_ref, dl_ref = rest[:5]
        rest = rest[5:]
    if not first:
        search_ref, applied_ref, load_ref, scale_ref, iterate_ref = rest[:5]
        rest = rest[5:]
    head = slice(0, CASES)
    across = [take_plane(spots, slots_ref, f, gy, head) for f in range(4)]
    for f, by in ((4, -1), (5, 1)):
        spot = jnp.where(spots[2 + f] > 0, spots[1] + by, spots[1])
        across.append(layers_ref[spot, head, :])
    mask = mask_ref[...]
    applied = (flexed_ref[...] + jnp.concatenate(across, axis=1)) * mask
    search = z_ref[...]
    blocks = []
    for b in range(6):
        blocks.append(jnp.concatenate([total_ref[2 * b], total_ref[2 * b + 1]], axis=0))
    norm = blocks[1][:, 64:65]
    energy = blocks[1][:, 65:66]
    load = jnp.concatenate(blocks, axis=1)
    lanes = lax.broadcasted_iota(jnp.int32, load.shape, 1) % QPAD
    load = jnp.where(lanes < 192, load, 0.0)
    if not first:
        beta = norm / scale_ref[:, 0:1]
        cross = blocks[1][:, 66:67]
        energy = energy + beta * cross + beta * beta * scale_ref[:, 1:2]
        applied = applied + beta * applied_ref[...]
        search = search + beta * search_ref[...]
        load = load + beta * load_ref[...]
    coarse = dot_split(load, kh_ref, kl_ref)
    step = norm / (energy + jnp.sum(load * coarse, axis=1, keepdims=True))
    corner = dot_exact(coarse, pick_ref[...])
    correction = dot_split(corner, gh_ref, gl_ref) * mask
    residual = residual_ref[...] - step * (applied + correction)
    moved = step * search
    if last:
        multipliers_ref, left_ref = rest
        for d in range(3):
            multipliers_ref[d] = iterate_ref[d] + face(moved, 2 * d + 1)
            left_ref[d] = face(residual, 2 * d + 1)
        return
    (search_out, applied_out, load_out, scale_out, iterate_out, residual_out, shown_ref, out_ref,
     up_ref, down_ref) = rest
    search_out[...] = search
    applied_out[...] = applied
    load_out[...] = load
    residual_out[...] = residual
    lanes = lax.broadcasted_iota(jnp.int32, (CASES, FD), 1)
    scale_out[...] = jnp.where(lanes == 0, norm, energy)
    for d in range(3):
        moved_face = face(moved, 2 * d + 1)
        iterate_out[d] = moved_face if first else iterate_ref[d] + moved_face
    _, shown = apply_dense(residual, (mx_ref, my_ref, mz_ref), dh_ref, dl_ref)
    shown_ref[...] = shown
    out_ref[...] = jnp.zeros_like(out_ref)
    put_plane(spots, out_ref, lambda f: face(shown, f), gy)
    down_ref[...] = face(shown, 4)
    up_ref[...] = face(shown, 5)


def passed_along(shard, axis, by):
    peers = lax.axis_size(axis)
    pairs = [(i, i + by) for i in range(peers) if 0 <= i + by < peers]
    return lax.ppermute(shard, axis, pairs)


def swapped(slots, axes):
    return lax.all_to_all(slots, axes, 0, 0)


def body(
    jump_rhs,
    flex_diag,
    flex_couple,
    dirichlet_diag,
    dirichlet_couple,
    face_pairs,
    corner_coupling,
    coarse_ids,
    partner,
    coarse_inverse,
):
    gx, gy, gz = (lax.axis_size(a) for a in ("gx", "gy", "gz"))
    ix, iy, iz = (lax.axis_index(a) for a in ("gx", "gy", "gz"))
    plane = gx * gy
    spots = jnp.stack(
        [ix * gy + iy, iz]
        + [v.astype(jnp.int32) for v in (ix > 0, ix < gx - 1, iy > 0, iy < gy - 1, iz > 0, iz < gz - 1)]
    ).astype(jnp.int32)
    mask = jnp.repeat(spots[2:].astype(F32), FD)[None, :]
    rhs = jump_rhs.reshape(3, CASES, FD)
    pairs = face_pairs.reshape(12)
    coupling = corner_coupling.reshape(24, WIDE)
    ids = coarse_ids.reshape(8)
    square = (WIDE, WIDE)
    wide = (CASES, WIDE)

    (message,) = call(
        prep_kernel, [((3, CASES + 8, FD), F32)], spots, rhs, partner.reshape(3, FD), smem=1
    )
    messages = [passed_along(message[d], a, 1) for d, a in enumerate(("gx", "gy", "gz"))]

    def build(diag, couple):
        return call(
            build_kernel, [(square, BF16)] * 2, pairs, diag.reshape(6, FD, FD),
            couple.reshape(6, FD, FD), smem=1
        )

    dirichlet = build(dirichlet_diag, dirichlet_couple)
    flex = build(flex_diag, flex_couple)
    padded = jnp.pad(
        coarse_inverse.reshape(3, 192, 3, 192), ((0, 0), (0, 64), (0, 0), (0, 64))
    ).reshape(square)
    inverse = call(split_kernel, [(square, BF16)] * 2, padded)
    weight_high, weight_low, expand = call(
        corner_kernel,
        [((WIDE, FD), BF16), ((WIDE, FD), BF16), ((FD, WIDE), BF16)],
        ids, coupling, smem=1, scratch=[pltpu.VMEM((FD, WIDE), F32)],
    )

    long = CASES + 32
    residual, shown, own, slots, up, down = call(
        functools.partial(start_kernel, gy),
        [(wide, F32), (wide, F32), ((24, WIDE), F32), ((plane, long, FD), F32), ((long, FD), F32),
         ((long, FD), F32)],
        spots, ids, rhs, *messages, *dirichlet, coupling, smem=2,
    )
    top = passed_along(down, "gz", -1)
    low = passed_along(up, "gz", 1)
    slots = swapped(slots, PLANE)
    joint = call(
        functools.partial(joint_kernel, gy),
        [((QPAD, WIDE), BF16), ((QPAD, WIDE), BF16), ((3 * QPAD, QPAD), BF16)],
        spots, ids, own, slots, low, top, smem=2, scratch=[pltpu.VMEM((QPAD, WIDE), F32)],
    )

    kept = ()
    for iteration in range(ITERS):
        first, last = iteration == 0, iteration + 1 == ITERS
        z, flexed, out = call(
            functools.partial(load_kernel, gy, first),
            [(wide, F32), (wide, F32), ((plane, CASES + 8, FD), F32)],
            spots, mask, *messages, shown, slots, low, top, residual, *flex, weight_high,
            weight_low, expand, *kept[:2], smem=1,
        )
        across = swapped(out, PLANE)
        (layers,) = call(
            layer_kernel, [((gz, CASES + 8, FD), F32)], spots, across, flexed, smem=1
        )
        layers = swapped(layers, "gz")
        (total,) = call(spread_kernel, [((plane, 8, FD), F32)], layers)
        total = swapped(total, PLANE)
        common = (spots, mask, total, across, layers, flexed, z, residual, *inverse, *joint)
        kernel = functools.partial(step_kernel, gy, first, last)
        if last:
            multipliers, left = call(
                kernel, [((3, CASES, FD), F32)] * 2, *common, *kept, smem=1
            )
            break
        search, applied, load, scale, iterate, residual, shown, slots, up, down = call(
            kernel,
            [(wide, F32)] * 3 + [((CASES, FD), F32), ((3, CASES, FD), F32), (wide, F32), (wide, F32),
             ((plane, CASES, FD), F32), ((CASES, FD), F32), ((CASES, FD), F32)],
            *common, *messages, *dirichlet, *kept, smem=1,
        )
        kept = (search, applied, load, scale, iterate)
        top = passed_along(down, "gz", -1)
        low = passed_along(up, "gz", 1)
        slots = swapped(slots, PLANE)
    return multipliers.reshape(jump_rhs.shape), left.reshape(jump_rhs.shape)


def solution(mesh):
    placed = (
        P("gx", "gy", "gz", None, None, None),
        P("gx", "gy", "gz", None, None, None),
        P("gx", "gy", "gz", None, None, None),
        P("gx", "gy", "gz", None, None, None),
        P("gx", "gy", "gz", None, None, None),
        P("gx", "gy", "gz", None, None),
        P("gx", "gy", "gz", None, None),
        P("gx", "gy", "gz", None),
        P("gx", "gy", "gz", None, None),
        P(),
    )
    return jax.shard_map(
        body,
        mesh=mesh,
        in_specs=placed,
        out_specs=(P("gx", "gy", "gz", None, None, None), P("gx", "gy", "gz", None, None, None)),
        check_vma=False,
    )
```

```python
import functools

import jax
import jax.numpy as jnp
from jax import lax
from jax.experimental import pallas as pl
from jax.experimental.pallas import tpu as pltpu
from jax.sharding import PartitionSpec as P

ITERS = 3
CASES = 16
FD = 128
WIDE = 6 * FD
QPAD = 256
SUBS = 32
PLANE = ("gx", "gy")
F32 = jnp.float32
BF16 = jnp.bfloat16
VMEM = pl.BlockSpec(memory_space=pltpu.VMEM)
SMEM = pl.BlockSpec(memory_space=pltpu.SMEM)


def call(kernel, outs, *args, smem=0, scratch=()):
    return pl.pallas_call(
        kernel,
        out_shape=[jax.ShapeDtypeStruct(shape, dtype) for shape, dtype in outs],
        in_specs=[SMEM] * smem + [VMEM] * (len(args) - smem),
        out_specs=[VMEM] * len(outs),
        scratch_shapes=list(scratch),
        compiler_params=pltpu.CompilerParams(vmem_limit_bytes=40 * 1024 * 1024),
    )(*args)


def halves(x):
    high = x.astype(BF16)
    return high, (x - high.astype(F32)).astype(BF16)


def dot_exact(x, selector):
    rows = x.shape[0]
    high, low = halves(x)
    both = jnp.dot(jnp.concatenate([high, low], 0), selector, preferred_element_type=F32)
    return both[:rows] + both[rows:]


def dot_split(x, high_ref, low_ref):
    rows = x.shape[0]
    high, low = halves(x)
    both = jnp.dot(jnp.concatenate([high, low], 0), high_ref[...], preferred_element_type=F32)
    rest = jnp.dot(high, low_ref[...], preferred_element_type=F32)
    return both[:rows] + both[rows:] + rest


def face(x, f):
    return x[:, f * FD:(f + 1) * FD]


def take(x, row):
    index = jnp.broadcast_to(row.astype(jnp.int32), x.shape)
    return jnp.take_along_axis(x, index, axis=1, mode="promise_in_bounds")


def lower_changed(x, rows):
    parts = []
    for d in range(3):
        parts.append(-take(face(x, 2 * d), rows[d]))
        parts.append(face(x, 2 * d + 1))
    return jnp.concatenate(parts, axis=1)


def partner_rows(messages):
    return [m[CASES:CASES + 1, :] for m in messages]


def inverse_rows(messages):
    return [m[CASES + 1:CASES + 2, :] for m in messages]


def apply_dense(field, messages, high_ref, low_ref):
    loads = lower_changed(field, inverse_rows(messages))
    return loads, lower_changed(dot_split(loads, high_ref, low_ref), partner_rows(messages))


def put_plane(spots, slots_ref, piece, gy):
    here = spots[0]
    for f, by in ((0, -gy), (1, gy), (2, -1), (3, 1)):
        @pl.when(spots[2 + f] > 0)
        def _():
            value = piece(f)
            slots_ref[here + by, 0:value.shape[0], :] = value


def take_plane(spots, slots_ref, f, gy, rows):
    here = spots[0]
    by = (-gy, gy, -1, 1)[f]
    spot = jnp.where(spots[2 + f] > 0, here + by, here)
    return slots_ref[spot, rows, :]


def prep_kernel(spots, rhs_ref, partner_ref, message_ref):
    for d in range(3):
        inner = spots[3 + 2 * d].astype(F32)
        row = partner_ref[d:d + 1, :]
        message_ref[d, 0:CASES, :] = rhs_ref[d] * inner
        wanted = lax.broadcasted_iota(jnp.int32, (FD, FD), 0)
        hits = (wanted == jnp.broadcast_to(row, (FD, FD))).astype(F32).astype(BF16)
        count = lax.broadcasted_iota(jnp.int32, (16, FD), 1).astype(F32).astype(BF16)
        inverse = lax.dot_general(
            count, hits, (((1,), (1,)), ((), ())), preferred_element_type=F32
        )
        message_ref[d, CASES:CASES + 1, :] = row.astype(F32)
        message_ref[d, CASES + 1:CASES + 2, :] = inverse[0:1, :]
        message_ref[d, CASES + 2:CASES + 8, :] = jnp.zeros((6, FD), F32)


def build_kernel(pairs, diag_ref, couple_ref, high_ref, low_ref):
    high_ref[...] = jnp.zeros_like(high_ref)
    low_ref[...] = jnp.zeros_like(low_ref)

    def put(row_face, col_face, block):
        high, low = halves(block)
        if isinstance(row_face, int):
            rows, cols = row_face * FD, col_face * FD
        else:
            rows = pl.multiple_of(row_face * FD, FD)
            cols = pl.multiple_of(col_face * FD, FD)
        high_ref[pl.ds(rows, FD), pl.ds(cols, FD)] = high
        low_ref[pl.ds(rows, FD), pl.ds(cols, FD)] = low

    for f in range(6):
        put(f, f, diag_ref[f])
    for k in range(6):
        first, second = pairs[2 * k], pairs[2 * k + 1]
        block = couple_ref[k]
        put(second, first, block)
        put(first, second, block.T)


def split_kernel(matrix_ref, high_ref, low_ref, pad):
    pad[...] = jnp.zeros_like(pad)
    for p in range(3):
        for q in range(3):
            pad[p * QPAD:p * QPAD + 192, q * QPAD:q * QPAD + 192] = matrix_ref[
                p * 192:(p + 1) * 192, q * 192:(q + 1) * 192
            ]
    high, low = halves(pad[...])
    high_ref[...] = high
    low_ref[...] = low


def corner_kernel(ids, coupling_ref, wh_ref, wl_ref, expand_ref, pad):
    pad[...] = jnp.zeros_like(pad)
    pad[0:24, :] = coupling_ref[...]
    for f in range(6):
        high, low = halves(pad[:, f * FD:(f + 1) * FD].T)
        wh_ref[f * FD:(f + 1) * FD, :] = high
        wl_ref[f * FD:(f + 1) * FD, :] = low
    pad[...] = jnp.zeros_like(pad)
    lanes = lax.broadcasted_iota(jnp.int32, (1, 3 * QPAD), 1)
    for r in range(24):
        spot = (r % 3) * QPAD + ids[r // 3]
        pad[r:r + 1, :] = (lanes == spot).astype(F32)
    expand_ref[...] = pad[...].astype(BF16)


def start_kernel(gy, spots, ids, rhs_ref, mx_ref, my_ref, mz_ref, dh_ref, dl_ref, coupling_ref,
                 field_ref, shown_ref, own_ref, slots_ref, up_ref, down_ref):
    messages = (mx_ref, my_ref, mz_ref)
    parts = []
    for d in range(3):
        parts.append(messages[d][0:CASES, :])
        parts.append(rhs_ref[d] * spots[3 + 2 * d].astype(F32))
    field = jnp.concatenate(parts, axis=1)
    field_ref[...] = field
    _, shown = apply_dense(field, messages, dh_ref, dl_ref)
    shown_ref[...] = shown
    own = lower_changed(coupling_ref[...], partner_rows(messages))
    own_ref[...] = own
    lanes = lax.broadcasted_iota(jnp.int32, (8, FD), 1) % SUBS
    target = jnp.full((8, FD), -1, jnp.int32)
    for r in range(24):
        target = jnp.where(lanes == r, (r % 3) * QPAD + ids[r // 3], target)
    target = target.astype(F32)

    def piece(f):
        return jnp.concatenate([face(shown, f), face(own, f), target], axis=0)

    slots_ref[...] = jnp.zeros_like(slots_ref)
    put_plane(spots, slots_ref, piece, gy)
    down_ref[...] = piece(4)
    up_ref[...] = piece(5)


def joint_kernel(gy, spots, ids, own_ref, slots_ref, low_ref, top_ref, gh_ref, gl_ref, pick_ref, whole):
    whole[...] = jnp.zeros_like(whole)
    whole[0:24, :] = own_ref[...]
    lanes = lax.broadcasted_iota(jnp.int32, (8, FD), 1)
    target = jnp.full((8, FD), -1, jnp.int32)
    for r in range(24):
        target = jnp.where(lanes % SUBS == r, (r % 3) * QPAD + ids[r // 3], target)
    targets = [target.astype(F32)]
    for f in range(6):
        if f < 4:
            other = take_plane(spots, slots_ref, f, gy, slice(CASES, CASES + 32))
        else:
            other = (low_ref, top_ref)[f - 4][CASES:CASES + 32, :]
        there = spots[2 + f].astype(F32)
        whole[SUBS * (f + 1):SUBS * (f + 1) + 24, f * FD:(f + 1) * FD] = other[0:24, :] * there
        targets.append(other[24:32, :] * there)
    high, low = halves(whole[...])
    gh_ref[...] = high
    gl_ref[...] = low
    rows = lax.broadcasted_iota(jnp.int32, (3 * QPAD, FD), 0)
    for half in range(2):
        wanted = jnp.full((8, FD), -1.0, F32)
        for n in range(4 * half, min(4 * half + 4, 7)):
            wanted = jnp.where(lanes // SUBS == n % 4, targets[n], wanted)
        wanted = jnp.broadcast_to(wanted[0:1, :].astype(jnp.int32), (3 * QPAD, FD))
        pick_ref[:, half * FD:(half + 1) * FD] = (rows == wanted).astype(F32).astype(BF16)


def load_kernel(gy, first, spots, mask_ref, mx_ref, my_ref, mz_ref, shown_ref, slots_ref, low_ref,
                top_ref, residual_ref, fh_ref, fl_ref, wh_ref, wl_ref, expand_ref, *rest):
    if first:
        z_ref, flexed_ref, out_ref = rest
    else:
        search_ref, applied_ref, z_ref, flexed_ref, out_ref = rest
    messages = (mx_ref, my_ref, mz_ref)
    head = slice(0, CASES)
    across = [take_plane(spots, slots_ref, f, gy, head) for f in range(4)]
    across += [low_ref[head, :], top_ref[head, :]]
    mask = mask_ref[...]
    z = 0.25 * (shown_ref[...] + jnp.concatenate(across, axis=1)) * mask
    z_ref[...] = z
    loads, flexed = apply_dense(z, messages, fh_ref, fl_ref)
    flexed_ref[...] = flexed
    corner = dot_split(loads, wh_ref, wl_ref)
    gathered = dot_exact(corner, expand_ref[...])

    def upper_sum(a):
        return jnp.sum(face(a, 1) + face(a, 3) + face(a, 5), axis=1, keepdims=True)

    sums = [upper_sum(z * residual_ref[...]), jnp.sum(z * flexed, axis=1, keepdims=True)]
    if not first:
        sums.append(
            upper_sum(z * applied_ref[...])
            + jnp.sum(search_ref[...] * flexed, axis=1, keepdims=True)
        )
    lanes = lax.broadcasted_iota(jnp.int32, (CASES, FD), 1)
    out_ref[...] = jnp.zeros_like(out_ref)
    for b in range(6):
        block = face(gathered, b)
        if b == 1:
            for t, value in enumerate(sums):
                block = jnp.where(lanes == 64 + t, value, block)
        for h in range(2):
            out_ref[2 * b + h, CASES:CASES + 8, :] = block[8 * h:8 * h + 8, :]
    put_plane(spots, out_ref, lambda f: face(flexed, f), gy)


def layer_kernel(spots, slots_ref, flexed_ref, out_ref):
    total = jnp.sum(slots_ref[:, CASES:CASES + 8, :], axis=0)
    out_ref[...] = jnp.zeros_like(out_ref)
    for i in range(out_ref.shape[0]):
        out_ref[i, CASES:CASES + 8, :] = total
    for f, by in ((4, -1), (5, 1)):
        @pl.when(spots[2 + f] > 0)
        def _():
            out_ref[spots[1] + by, 0:CASES, :] = flexed_ref[:, f * FD:(f + 1) * FD]


def spread_kernel(slots_ref, out_ref):
    total = jnp.sum(slots_ref[:, CASES:CASES + 8, :], axis=0)
    for i in range(out_ref.shape[0]):
        out_ref[i] = total


def step_kernel(gy, first, last, spots, mask_ref, total_ref, slots_ref, layers_ref, flexed_ref,
                z_ref, residual_ref, kh_ref, kl_ref, gh_ref, gl_ref, pick_ref, *rest):
    rest = list(rest)
    if not last:
        mx_ref, my_ref, mz_ref, dh_ref, dl_ref = rest[:5]
        rest = rest[5:]
    if not first:
        search_ref, applied_ref, load_ref, scale_ref, iterate_ref = rest[:5]
        rest = rest[5:]
    head = slice(0, CASES)
    across = [take_plane(spots, slots_ref, f, gy, head) for f in range(4)]
    for f, by in ((4, -1), (5, 1)):
        spot = jnp.where(spots[2 + f] > 0, spots[1] + by, spots[1])
        across.append(layers_ref[spot, head, :])
    mask = mask_ref[...]
    applied = (flexed_ref[...] + jnp.concatenate(across, axis=1)) * mask
    search = z_ref[...]
    blocks = []
    for b in range(6):
        blocks.append(jnp.concatenate([total_ref[2 * b], total_ref[2 * b + 1]], axis=0))
    norm = blocks[1][:, 64:65]
    energy = blocks[1][:, 65:66]
    load = jnp.concatenate(blocks, axis=1)
    lanes = lax.broadcasted_iota(jnp.int32, load.shape, 1) % QPAD
    load = jnp.where(lanes < 192, load, 0.0)
    if not first:
        beta = norm / scale_ref[:, 0:1]
        cross = blocks[1][:, 66:67]
        energy = energy + beta * cross + beta * beta * scale_ref[:, 1:2]
        applied = applied + beta * applied_ref[...]
        search = search + beta * search_ref[...]
        load = load + beta * load_ref[...]
    coarse = dot_split(load, kh_ref, kl_ref)
    step = norm / (energy + jnp.sum(load * coarse, axis=1, keepdims=True))
    corner = dot_exact(coarse, pick_ref[...])
    correction = dot_split(corner, gh_ref, gl_ref) * mask
    residual = residual_ref[...] - step * (applied + correction)
    moved = step * search
    if last:
        multipliers_ref, left_ref = rest
        for d in range(3):
            multipliers_ref[d] = iterate_ref[d] + face(moved, 2 * d + 1)
            left_ref[d] = face(residual, 2 * d + 1)
        return
    (search_out, applied_out, load_out, scale_out, iterate_out, residual_out, shown_ref, out_ref,
     up_ref, down_ref) = rest
    search_out[...] = search
    applied_out[...] = applied
    load_out[...] = load
    residual_out[...] = residual
    lanes = lax.broadcasted_iota(jnp.int32, (CASES, FD), 1)
    scale_out[...] = jnp.where(lanes == 0, norm, energy)
    for d in range(3):
        moved_face = face(moved, 2 * d + 1)
        iterate_out[d] = moved_face if first else iterate_ref[d] + moved_face
    _, shown = apply_dense(residual, (mx_ref, my_ref, mz_ref), dh_ref, dl_ref)
    shown_ref[...] = shown
    out_ref[...] = jnp.zeros_like(out_ref)
    put_plane(spots, out_ref, lambda f: face(shown, f), gy)
    down_ref[...] = face(shown, 4)
    up_ref[...] = face(shown, 5)


def passed_along(shard, axis, by):
    peers = lax.axis_size(axis)
    pairs = [(i, i + by) for i in range(peers) if 0 <= i + by < peers]
    return lax.ppermute(shard, axis, pairs)


def swapped(slots, axes):
    return lax.all_to_all(slots, axes, 0, 0)


def body(
    jump_rhs,
    flex_diag,
    flex_couple,
    dirichlet_diag,
    dirichlet_couple,
    face_pairs,
    corner_coupling,
    coarse_ids,
    partner,
    coarse_inverse,
):
    gx, gy, gz = (lax.axis_size(a) for a in ("gx", "gy", "gz"))
    ix, iy, iz = (lax.axis_index(a) for a in ("gx", "gy", "gz"))
    plane = gx * gy
    spots = jnp.stack(
        [ix * gy + iy, iz]
        + [v.astype(jnp.int32) for v in (ix > 0, ix < gx - 1, iy > 0, iy < gy - 1, iz > 0, iz < gz - 1)]
    ).astype(jnp.int32)
    mask = jnp.repeat(spots[2:].astype(F32), FD)[None, :]
    rhs = jump_rhs.reshape(3, CASES, FD)
    pairs = face_pairs.reshape(12)
    coupling = corner_coupling.reshape(24, WIDE)
    ids = coarse_ids.reshape(8)
    square = (WIDE, WIDE)
    wide = (CASES, WIDE)

    (message,) = call(
        prep_kernel, [((3, CASES + 8, FD), F32)], spots, rhs, partner.reshape(3, FD), smem=1
    )
    messages = [passed_along(message[d], a, 1) for d, a in enumerate(("gx", "gy", "gz"))]

    def build(diag, couple):
        return call(
            build_kernel, [(square, BF16)] * 2, pairs, diag.reshape(6, FD, FD),
            couple.reshape(6, FD, FD), smem=1
        )

    dirichlet = build(dirichlet_diag, dirichlet_couple)
    flex = build(flex_diag, flex_couple)
    inverse = call(
        split_kernel, [(square, BF16)] * 2, coarse_inverse, scratch=[pltpu.VMEM(square, F32)]
    )
    weight_high, weight_low, expand = call(
        corner_kernel,
        [((WIDE, FD), BF16), ((WIDE, FD), BF16), ((FD, WIDE), BF16)],
        ids, coupling, smem=1, scratch=[pltpu.VMEM((FD, WIDE), F32)],
    )

    setup = (messages, dirichlet, flex, inverse, weight_high, weight_low, expand)
    messages, dirichlet, flex, inverse, weight_high, weight_low, expand = lax.optimization_barrier(setup)
    long = CASES + 32
    residual, shown, own, slots, up, down = call(
        functools.partial(start_kernel, gy),
        [(wide, F32), (wide, F32), ((24, WIDE), F32), ((plane, long, FD), F32), ((long, FD), F32),
         ((long, FD), F32)],
        spots, ids, rhs, *messages, *dirichlet, coupling, smem=2,
    )
    top = passed_along(down, "gz", -1)
    low = passed_along(up, "gz", 1)
    slots, low, top = lax.optimization_barrier((slots, low, top))
    slots = swapped(slots, PLANE)
    joint = call(
        functools.partial(joint_kernel, gy),
        [((QPAD, WIDE), BF16), ((QPAD, WIDE), BF16), ((3 * QPAD, QPAD), BF16)],
        spots, ids, own, slots, low, top, smem=2, scratch=[pltpu.VMEM((QPAD, WIDE), F32)],
    )

    slots, low, top, joint = lax.optimization_barrier((slots, low, top, joint))
    kept = ()
    for iteration in range(ITERS):
        first, last = iteration == 0, iteration + 1 == ITERS
        z, flexed, out = call(
            functools.partial(load_kernel, gy, first),
            [(wide, F32), (wide, F32), ((plane, CASES + 8, FD), F32)],
            spots, mask, *messages, shown, slots, low, top, residual, *flex, weight_high,
            weight_low, expand, *kept[:2], smem=1,
        )
        across = swapped(out, PLANE)
        (layers,) = call(
            layer_kernel, [((gz, CASES + 8, FD), F32)], spots, across, flexed, smem=1
        )
        layers = swapped(layers, "gz")
        (total,) = call(spread_kernel, [((plane, 8, FD), F32)], layers)
        total = swapped(total, PLANE)
        common = (spots, mask, total, across, layers, flexed, z, residual, *inverse, *joint)
        kernel = functools.partial(step_kernel, gy, first, last)
        if last:
            multipliers, left = call(
                kernel, [((3, CASES, FD), F32)] * 2, *common, *kept, smem=1
            )
            break
        search, applied, load, scale, iterate, residual, shown, slots, up, down = call(
            kernel,
            [(wide, F32)] * 3 + [((CASES, FD), F32), ((3, CASES, FD), F32), (wide, F32), (wide, F32),
             ((plane, CASES, FD), F32), ((CASES, FD), F32), ((CASES, FD), F32)],
            *common, *messages, *dirichlet, *kept, smem=1,
        )
        kept = (search, applied, load, scale, iterate)
        top = passed_along(down, "gz", -1)
        low = passed_along(up, "gz", 1)
        slots, low, top = lax.optimization_barrier((slots, low, top))
        slots = swapped(slots, PLANE)
    return multipliers.reshape(jump_rhs.shape), left.reshape(jump_rhs.shape)


def solution(mesh):
    placed = (
        P("gx", "gy", "gz", None, None, None),
        P("gx", "gy", "gz", None, None, None),
        P("gx", "gy", "gz", None, None, None),
        P("gx", "gy", "gz", None, None, None),
        P("gx", "gy", "gz", None, None, None),
        P("gx", "gy", "gz", None, None),
        P("gx", "gy", "gz", None, None),
        P("gx", "gy", "gz", None),
        P("gx", "gy", "gz", None, None),
        P(),
    )
    return jax.shard_map(
        body,
        mesh=mesh,
        in_specs=placed,
        out_specs=(P("gx", "gy", "gz", None, None, None), P("gx", "gy", "gz", None, None, None)),
        check_vma=False,
    )
```

```python
import functools

import jax
import jax.numpy as jnp
from jax import lax
from jax.experimental import pallas as pl
from jax.experimental.pallas import tpu as pltpu
from jax.sharding import PartitionSpec as P

ITERS = 3
CASES = 16
FD = 128
WIDE = 6 * FD
QPAD = 256
SUBS = 32
AXES = ("gx", "gy", "gz")
PLANE = ("gx", "gy")
F32 = jnp.float32
BF16 = jnp.bfloat16
VMEM = pl.BlockSpec(memory_space=pltpu.VMEM)
SMEM = pl.BlockSpec(memory_space=pltpu.SMEM)


def call(kernel, outs, args, specs=(), scratch=()):
    return pl.pallas_call(
        kernel,
        out_shape=[jax.ShapeDtypeStruct(shape, dtype) for shape, dtype in outs],
        in_specs=list(specs) + [VMEM] * (len(args) - len(specs)),
        out_specs=[VMEM] * len(outs),
        scratch_shapes=list(scratch),
        compiler_params=pltpu.CompilerParams(vmem_limit_bytes=40 * 1024 * 1024),
    )(*args)


def halves(x):
    high = x.astype(BF16)
    return high, (x - high.astype(F32)).astype(BF16)


def dot_exact(x, selector):
    rows = x.shape[0]
    high, low = halves(x)
    both = jnp.dot(jnp.concatenate([high, low], 0), selector, preferred_element_type=F32)
    return both[:rows] + both[rows:]


def dot_split(x, high_ref, low_ref):
    rows = x.shape[0]
    high, low = halves(x)
    both = jnp.dot(jnp.concatenate([high, low], 0), high_ref[...], preferred_element_type=F32)
    rest = jnp.dot(high, low_ref[...], preferred_element_type=F32)
    return both[:rows] + both[rows:] + rest


def face(x, f):
    return x[:, f * FD:(f + 1) * FD]


def take(x, row):
    index = jnp.broadcast_to(row.astype(jnp.int32), x.shape)
    return jnp.take_along_axis(x, index, axis=1, mode="promise_in_bounds")


def lower_changed(x, rows):
    parts = []
    for d in range(3):
        parts.append(-take(face(x, 2 * d), rows[d]))
        parts.append(face(x, 2 * d + 1))
    return jnp.concatenate(parts, axis=1)


def partner_rows(messages):
    return [m[CASES:CASES + 1, :] for m in messages]


def inverse_rows(messages):
    return [m[CASES + 1:CASES + 2, :] for m in messages]


def apply_dense(field, messages, high_ref, low_ref):
    loads = lower_changed(field, inverse_rows(messages))
    return loads, lower_changed(dot_split(loads, high_ref, low_ref), partner_rows(messages))


def position():
    gy = lax.axis_size("gy")
    places = [(lax.axis_index(a), lax.axis_size(a)) for a in ("gx", "gy", "gz")]
    there = []
    for place, size in places:
        there += [place > 0, place < size - 1]
    return places[0][0] * gy + places[1][0], places[2][0], there


def steps():
    gy = lax.axis_size("gy")
    return (-gy, gy, -1, 1)


def mask_row(there):
    return jnp.concatenate([jnp.full((1, FD), t.astype(F32)) for t in there], axis=1)


def put_rows(slots_ref, spot, rows):
    for q in range(4):
        slots_ref[spot, q] = rows[4 * q:4 * q + 4, :]


def take_rows(slots_ref, spot):
    return jnp.concatenate([slots_ref[spot, q] for q in range(4)], axis=0)


def prep_kernel(rhs_ref, partner_ref, *message_refs):
    _, _, there = position()
    for d in range(3):
        message_ref = message_refs[d]
        row = partner_ref[d:d + 1, :]
        message_ref[0:CASES, :] = rhs_ref[d] * there[2 * d + 1].astype(F32)
        wanted = lax.broadcasted_iota(jnp.int32, (FD, FD), 0)
        hits = (wanted == jnp.broadcast_to(row, (FD, FD))).astype(F32).astype(BF16)
        count = lax.broadcasted_iota(jnp.int32, (16, FD), 1).astype(F32).astype(BF16)
        inverse = lax.dot_general(
            count, hits, (((1,), (1,)), ((), ())), preferred_element_type=F32
        )
        message_ref[CASES:CASES + 1, :] = row.astype(F32)
        message_ref[CASES + 1:CASES + 2, :] = inverse[0:1, :]
        message_ref[CASES + 2:CASES + 8, :] = jnp.zeros((6, FD), F32)


def put_dense(pairs, diag_ref, couple_ref, high_ref, low_ref):
    high_ref[...] = jnp.zeros_like(high_ref)
    low_ref[...] = jnp.zeros_like(low_ref)

    def put(rows, cols, block):
        high, low = halves(block)
        high_ref[pl.ds(rows, FD), pl.ds(cols, FD)] = high
        low_ref[pl.ds(rows, FD), pl.ds(cols, FD)] = low

    for f in range(6):
        put(f * FD, f * FD, diag_ref[f])
    for k in range(6):
        first = pl.multiple_of(pairs[k, 0] * FD, FD)
        second = pl.multiple_of(pairs[k, 1] * FD, FD)
        block = couple_ref[k]
        put(second, first, block)
        put(first, second, block.T)


def setup_kernel(pairs, ids, *rest):
    sources, rest = rest[:6], rest[6:]
    (dh_ref, dl_ref, fh_ref, fl_ref, kh_ref, kl_ref, wh_ref, wl_ref, expand_ref, target_ref) = rest[:10]
    held, (pad, square, sems) = rest[10:16], rest[16:]
    copies = [
        pltpu.make_async_copy(source, target, sems.at[i])
        for i, (source, target) in enumerate(zip(sources, held))
    ]
    for copy in copies:
        copy.start()
    lanes = lax.broadcasted_iota(jnp.int32, (8, FD), 1) % SUBS
    target = jnp.full((8, FD), -1, jnp.int32)
    for r in range(24):
        target = jnp.where(lanes == r, (r % 3) * QPAD + ids[0, r // 3], target)
    target_ref[...] = target.astype(F32)
    pad[...] = jnp.zeros_like(pad)
    lanes = lax.broadcasted_iota(jnp.int32, (1, 3 * QPAD), 1)
    for r in range(24):
        spot = (r % 3) * QPAD + ids[0, r // 3]
        pad[r:r + 1, :] = (lanes == spot).astype(F32)
    expand_ref[...] = pad[...].astype(BF16)
    copies[0].wait()
    copies[1].wait()
    put_dense(pairs, held[0], held[1], dh_ref, dl_ref)
    copies[2].wait()
    copies[3].wait()
    put_dense(pairs, held[2], held[3], fh_ref, fl_ref)
    square[...] = jnp.zeros_like(square)
    copies[4].wait()
    for p in range(3):
        for q in range(3):
            square[p * QPAD:p * QPAD + 192, q * QPAD:q * QPAD + 192] = held[4][
                p * 192:(p + 1) * 192, q * 192:(q + 1) * 192
            ]
    high, low = halves(square[...])
    kh_ref[...] = high
    kl_ref[...] = low
    pad[...] = jnp.zeros_like(pad)
    copies[5].wait()
    pad[0:24, :] = held[5][...]
    for f in range(6):
        high, low = halves(pad[:, f * FD:(f + 1) * FD].T)
        wh_ref[f * FD:(f + 1) * FD, :] = high
        wl_ref[f * FD:(f + 1) * FD, :] = low


def start_kernel(rhs_ref, mx_ref, my_ref, mz_ref, dh_ref, dl_ref, coupling_ref, target_ref,
                 field_ref, shown_ref, own_ref, *piece_refs):
    _, _, there = position()
    messages = (mx_ref, my_ref, mz_ref)
    parts = []
    for d in range(3):
        parts.append(messages[d][0:CASES, :])
        parts.append(rhs_ref[d] * there[2 * d + 1].astype(F32))
    field = jnp.concatenate(parts, axis=1)
    field_ref[...] = field
    _, shown = apply_dense(field, messages, dh_ref, dl_ref)
    shown_ref[...] = shown
    own = lower_changed(coupling_ref[...], partner_rows(messages))
    own_ref[...] = own
    for f in range(6):
        piece_refs[f][0:CASES, :] = face(shown, f)
        piece_refs[f][CASES:CASES + 24, :] = face(own, f)
        piece_refs[f][CASES + 24:CASES + 32, :] = target_ref[...]


def joint_kernel(own_ref, target_ref, *rest):
    others, (gh_ref, gl_ref, pick_ref, whole) = rest[:6], rest[6:]
    _, _, there = position()
    whole[...] = jnp.zeros_like(whole)
    whole[0:24, :] = own_ref[...]
    lanes = lax.broadcasted_iota(jnp.int32, (8, FD), 1)
    targets = [target_ref[...]]
    for f in range(6):
        exists = there[f].astype(F32)
        whole[SUBS * (f + 1):SUBS * (f + 1) + 24, f * FD:(f + 1) * FD] = (
            others[f][CASES:CASES + 24, :] * exists
        )
        targets.append(others[f][CASES + 24:CASES + 32, :] * exists)
    high, low = halves(whole[...])
    gh_ref[...] = high
    gl_ref[...] = low
    rows = lax.broadcasted_iota(jnp.int32, (3 * QPAD, FD), 0)
    for half in range(2):
        wanted = jnp.full((8, FD), -1.0, F32)
        for n in range(4 * half, min(4 * half + 4, 7)):
            wanted = jnp.where(lanes // SUBS == n % 4, targets[n], wanted)
        wanted = jnp.broadcast_to(wanted[0:1, :].astype(jnp.int32), (3 * QPAD, FD))
        pick_ref[:, half * FD:(half + 1) * FD] = (rows == wanted).astype(F32).astype(BF16)


def load_kernel(first, mx_ref, my_ref, mz_ref, shown_ref, *rest):
    others, rest = rest[:6], rest[6:]
    residual_ref, fh_ref, fl_ref, wh_ref, wl_ref, expand_ref = rest[:6]
    rest = rest[6:]
    if first:
        z_ref, flexed_ref, out_ref = rest
    else:
        search_ref, applied_ref, z_ref, flexed_ref, out_ref = rest
    messages = (mx_ref, my_ref, mz_ref)
    here, _, there = position()
    across = jnp.concatenate([other[0:CASES, :] for other in others], axis=1)
    z = 0.25 * (shown_ref[...] + across) * mask_row(there)
    z_ref[...] = z
    loads, flexed = apply_dense(z, messages, fh_ref, fl_ref)
    flexed_ref[...] = flexed
    corner = dot_split(loads, wh_ref, wl_ref)
    gathered = dot_exact(corner, expand_ref[...])

    def upper_sum(a):
        return jnp.sum(face(a, 1) + face(a, 3) + face(a, 5), axis=1, keepdims=True)

    sums = [upper_sum(z * residual_ref[...]), jnp.sum(z * flexed, axis=1, keepdims=True)]
    if not first:
        sums.append(
            upper_sum(z * applied_ref[...])
            + jnp.sum(search_ref[...] * flexed, axis=1, keepdims=True)
        )
    lanes = lax.broadcasted_iota(jnp.int32, (CASES, FD), 1)
    out_ref[...] = jnp.zeros_like(out_ref)
    for b in range(6):
        block = face(gathered, b)
        if b == 1:
            for t, value in enumerate(sums):
                block = jnp.where(lanes == 64 + t, value, block)
        for q in range(4):
            out_ref[4 * b + q, 4] = block[4 * q:4 * q + 4, :]
    for f, by in enumerate(steps()):
        @pl.when(there[f])
        def _():
            put_rows(out_ref, here + by, face(flexed, f))


def layer_kernel(slots_ref, flexed_ref, out_ref):
    _, layer, there = position()
    total = jnp.sum(slots_ref[:, 4], axis=0)
    out_ref[...] = jnp.zeros_like(out_ref)
    for i in range(out_ref.shape[0]):
        out_ref[i, 4] = total
    for f, by in ((4, -1), (5, 1)):
        @pl.when(there[f])
        def _():
            put_rows(out_ref, layer + by, flexed_ref[:, f * FD:(f + 1) * FD])


def spread_kernel(slots_ref, out_ref):
    total = jnp.sum(slots_ref[:, 4], axis=0)
    for i in range(out_ref.shape[0]):
        out_ref[i] = total


def step_kernel(first, last, total_ref, slots_ref, layers_ref, flexed_ref,
                z_ref, residual_ref, kh_ref, kl_ref, gh_ref, gl_ref, pick_ref, *rest):
    rest = list(rest)
    if not last:
        mx_ref, my_ref, mz_ref, dh_ref, dl_ref = rest[:5]
        rest = rest[5:]
    if not first:
        search_ref, applied_ref, load_ref, scale_ref, iterate_ref = rest[:5]
        rest = rest[5:]
    here, layer, there = position()
    across = []
    for f, by in enumerate(steps()):
        across.append(take_rows(slots_ref, jnp.where(there[f], here + by, here)))
    for f, by in ((4, -1), (5, 1)):
        across.append(take_rows(layers_ref, jnp.where(there[f], layer + by, layer)))
    mask = mask_row(there)
    applied = (flexed_ref[...] + jnp.concatenate(across, axis=1)) * mask
    search = z_ref[...]
    blocks = []
    for b in range(6):
        blocks.append(jnp.concatenate([total_ref[4 * b + q] for q in range(4)], axis=0))
    norm = blocks[1][:, 64:65]
    energy = blocks[1][:, 65:66]
    load = jnp.concatenate(blocks, axis=1)
    lanes = lax.broadcasted_iota(jnp.int32, load.shape, 1) % QPAD
    load = jnp.where(lanes < 192, load, 0.0)
    if not first:
        beta = norm / scale_ref[:, 0:1]
        cross = blocks[1][:, 66:67]
        energy = energy + beta * cross + beta * beta * scale_ref[:, 1:2]
        applied = applied + beta * applied_ref[...]
        search = search + beta * search_ref[...]
        load = load + beta * load_ref[...]
    coarse = dot_split(load, kh_ref, kl_ref)
    step = norm / (energy + jnp.sum(load * coarse, axis=1, keepdims=True))
    corner = dot_exact(coarse, pick_ref[...])
    correction = dot_split(corner, gh_ref, gl_ref) * mask
    residual = residual_ref[...] - step * (applied + correction)
    moved = step * search
    if last:
        multipliers_ref, left_ref = rest
        for d in range(3):
            multipliers_ref[d] = iterate_ref[d] + face(moved, 2 * d + 1)
            left_ref[d] = face(residual, 2 * d + 1)
        return
    search_out, applied_out, load_out, scale_out, iterate_out, residual_out, shown_ref = rest[:7]
    piece_refs = rest[7:]
    search_out[...] = search
    applied_out[...] = applied
    load_out[...] = load
    residual_out[...] = residual
    lanes = lax.broadcasted_iota(jnp.int32, (CASES, FD), 1)
    scale_out[...] = jnp.where(lanes == 0, norm, energy)
    for d in range(3):
        moved_face = face(moved, 2 * d + 1)
        iterate_out[d] = moved_face if first else iterate_ref[d] + moved_face
    _, shown = apply_dense(residual, (mx_ref, my_ref, mz_ref), dh_ref, dl_ref)
    shown_ref[...] = shown
    for f in range(6):
        piece_refs[f][...] = face(shown, f)


def passed_along(shard, axis, by):
    peers = lax.axis_size(axis)
    pairs = [(i, i + by) for i in range(peers) if 0 <= i + by < peers]
    return lax.ppermute(shard, axis, pairs)


def swapped(slots, axes):
    return lax.all_to_all(slots, axes, 0, 0)


def across_faces(pieces):
    got = [None] * 6
    for d in (2, 1, 0):
        got[2 * d] = passed_along(pieces[2 * d + 1], AXES[d], 1)
        got[2 * d + 1] = passed_along(pieces[2 * d], AXES[d], -1)
    return got


def body(
    jump_rhs,
    flex_diag,
    flex_couple,
    dirichlet_diag,
    dirichlet_couple,
    face_pairs,
    corner_coupling,
    coarse_ids,
    partner,
    coarse_inverse,
):
    gx, gy, gz = (lax.axis_size(a) for a in AXES)
    plane = gx * gy
    rhs = jump_rhs.reshape(3, CASES, FD)
    pairs = face_pairs.reshape(6, 2)
    coupling = corner_coupling.reshape(24, WIDE)
    ids = coarse_ids.reshape(1, 8)
    square = (WIDE, WIDE)
    wide = (CASES, WIDE)
    long = CASES + 32

    messages = call(
        prep_kernel, [((CASES + 8, FD), F32)] * 3, [rhs, partner.reshape(3, FD)]
    )
    messages = [passed_along(m, a, 1) for m, a in zip(messages, AXES)]
    blocks = [b.reshape(6, FD, FD) for b in (dirichlet_diag, dirichlet_couple, flex_diag, flex_couple)]
    sources = blocks + [coarse_inverse, coupling]
    *dense, target = call(
        setup_kernel,
        [(square, BF16)] * 6 + [((WIDE, FD), BF16)] * 2 + [((FD, WIDE), BF16), ((8, FD), F32)],
        [pairs, ids] + sources,
        specs=[SMEM] * 2 + [pl.BlockSpec(memory_space=pl.ANY)] * 6,
        scratch=[pltpu.VMEM(source.shape, F32) for source in sources]
        + [pltpu.VMEM((FD, WIDE), F32), pltpu.VMEM(square, F32), pltpu.SemaphoreType.DMA((6,))],
    )
    dirichlet, flex, inverse, weights = dense[0:2], dense[2:4], dense[4:6], dense[6:9]
    residual, shown, own, *pieces = call(
        start_kernel,
        [(wide, F32), (wide, F32), ((24, WIDE), F32)] + [((long, FD), F32)] * 6,
        [rhs, *messages, *dirichlet, coupling, target],
    )
    others = across_faces(pieces)
    joint = call(
        joint_kernel,
        [((QPAD, WIDE), BF16), ((QPAD, WIDE), BF16), ((3 * QPAD, QPAD), BF16)],
        [own, target, *others],
        scratch=[pltpu.VMEM((QPAD, WIDE), F32)],
    )
    joint, others = lax.optimization_barrier((joint, others))

    kept = []
    for iteration in range(ITERS):
        first, last = iteration == 0, iteration + 1 == ITERS
        z, flexed, out = call(
            functools.partial(load_kernel, first),
            [(wide, F32), (wide, F32), ((plane, 5, 4, FD), F32)],
            [*messages, shown, *others, residual, *flex, *weights, *kept[:2]],
        )
        slots = swapped(out, PLANE)
        (layers,) = call(layer_kernel, [((gz, 5, 4, FD), F32)], [slots, flexed])
        layers = swapped(layers, "gz")
        (total,) = call(spread_kernel, [((plane, 4, FD), F32)], [layers])
        total = swapped(total, PLANE)
        common = [total, slots, layers, flexed, z, residual, *inverse, *joint]
        kernel = functools.partial(step_kernel, first, last)
        if last:
            multipliers, left = call(kernel, [((3, CASES, FD), F32)] * 2, common + kept)
            break
        *kept, residual, shown, p0, p1, p2, p3, p4, p5 = call(
            kernel,
            [(wide, F32)] * 3 + [((CASES, FD), F32), ((3, CASES, FD), F32), (wide, F32), (wide, F32)]
            + [((CASES, FD), F32)] * 6,
            common + [*messages, *dirichlet] + kept,
        )
        others = across_faces((p0, p1, p2, p3, p4, p5))
    return multipliers.reshape(jump_rhs.shape), left.reshape(jump_rhs.shape)


def solution(mesh):
    placed = (
        P("gx", "gy", "gz", None, None, None),
        P("gx", "gy", "gz", None, None, None),
        P("gx", "gy", "gz", None, None, None),
        P("gx", "gy", "gz", None, None, None),
        P("gx", "gy", "gz", None, None, None),
        P("gx", "gy", "gz", None, None),
        P("gx", "gy", "gz", None, None),
        P("gx", "gy", "gz", None),
        P("gx", "gy", "gz", None, None),
        P(),
    )
    return jax.shard_map(
        body,
        mesh=mesh,
        in_specs=placed,
        out_specs=(P("gx", "gy", "gz", None, None, None), P("gx", "gy", "gz", None, None, None)),
        check_vma=False,
    )
```

```python
import functools

import jax
import jax.numpy as jnp
from jax import lax
from jax.experimental import pallas as pl
from jax.experimental.pallas import tpu as pltpu
from jax.sharding import PartitionSpec as P

ITERS = 3
CASES = 16
FD = 128
WIDE = 6 * FD
QPAD = 256
SUBS = 32
AXES = ("gx", "gy", "gz")
PLANE = ("gx", "gy")
F32 = jnp.float32
BF16 = jnp.bfloat16
VMEM = pl.BlockSpec(memory_space=pltpu.VMEM)
SMEM = pl.BlockSpec(memory_space=pltpu.SMEM)


def call(kernel, outs, args, specs=(), scratch=()):
    return pl.pallas_call(
        kernel,
        out_shape=[jax.ShapeDtypeStruct(shape, dtype) for shape, dtype in outs],
        in_specs=list(specs) + [VMEM] * (len(args) - len(specs)),
        out_specs=[VMEM] * len(outs),
        scratch_shapes=list(scratch),
        compiler_params=pltpu.CompilerParams(vmem_limit_bytes=40 * 1024 * 1024),
    )(*args)


def halves(x):
    high = x.astype(BF16)
    return high, (x - high.astype(F32)).astype(BF16)


def dot_exact(x, selector):
    rows = x.shape[0]
    high, low = halves(x)
    both = jnp.dot(jnp.concatenate([high, low], 0), selector, preferred_element_type=F32)
    return both[:rows] + both[rows:]


def dot_split(x, high_ref, low_ref):
    rows = x.shape[0]
    high, low = halves(x)
    both = jnp.dot(jnp.concatenate([high, low], 0), high_ref[...], preferred_element_type=F32)
    rest = jnp.dot(high, low_ref[...], preferred_element_type=F32)
    return both[:rows] + both[rows:] + rest


def face(x, f):
    return x[:, f * FD:(f + 1) * FD]


def take(x, row):
    index = jnp.broadcast_to(row.astype(jnp.int32), x.shape)
    return jnp.take_along_axis(x, index, axis=1, mode="promise_in_bounds")


def lower_changed(x, rows):
    parts = []
    for d in range(3):
        parts.append(-take(face(x, 2 * d), rows[d]))
        parts.append(face(x, 2 * d + 1))
    return jnp.concatenate(parts, axis=1)


def partner_rows(messages):
    return [m[CASES:CASES + 1, :] for m in messages]


def inverse_rows(messages):
    return [m[CASES + 1:CASES + 2, :] for m in messages]


def apply_dense(field, messages, high_ref, low_ref):
    loads = lower_changed(field, inverse_rows(messages))
    return loads, lower_changed(dot_split(loads, high_ref, low_ref), partner_rows(messages))


def position():
    gy = lax.axis_size("gy")
    places = [(lax.axis_index(a), lax.axis_size(a)) for a in ("gx", "gy", "gz")]
    there = []
    for place, size in places:
        there += [place > 0, place < size - 1]
    return places[0][0] * gy + places[1][0], places[2][0], there


def steps():
    gy = lax.axis_size("gy")
    return (-gy, gy, -1, 1)


def cube_groups(start):
    gx, gy, gz = (lax.axis_size(a) for a in AXES)
    return [
        [
            (i + a) % gx * gy * gz + (j + b) % gy * gz + (k + c) % gz
            for a in range(2) for b in range(2) for c in range(2)
        ]
        for i in range(start, gx + start, 2)
        for j in range(start, gy + start, 2)
        for k in range(start, gz + start, 2)
    ]


def cube_places():
    odd = [lax.rem(lax.axis_index(a), 2) for a in AXES]
    first = odd[0] * 4 + odd[1] * 2 + odd[2]
    found = []
    for d in range(3):
        bit = 4 >> d
        other = first + bit * (1 - 2 * odd[d])
        found.append((odd[d] == 0, other, 7 - other))
    return found


def put_cubes(first_ref, second_ref, piece):
    first_ref[...] = jnp.zeros_like(first_ref)
    second_ref[...] = jnp.zeros_like(second_ref)
    for d, (even, one, two) in enumerate(cube_places()):
        lower, upper = piece(2 * d), piece(2 * d + 1)
        first_ref[one] = jnp.where(even, upper, lower)
        second_ref[two] = jnp.where(even, lower, upper)


def take_cubes(first_ref, second_ref, rows):
    got = []
    for even, one, two in cube_places():
        a, b = first_ref[one, rows, :], second_ref[two, rows, :]
        got += [jnp.where(even, b, a), jnp.where(even, a, b)]
    return got


def mask_row(there):
    return jnp.concatenate([jnp.full((1, FD), t.astype(F32)) for t in there], axis=1)


def put_rows(slots_ref, spot, rows):
    for q in range(4):
        slots_ref[spot, q] = rows[4 * q:4 * q + 4, :]


def take_rows(slots_ref, spot):
    return jnp.concatenate([slots_ref[spot, q] for q in range(4)], axis=0)


def prep_kernel(rhs_ref, partner_ref, *message_refs):
    _, _, there = position()
    for d in range(3):
        message_ref = message_refs[d]
        row = partner_ref[0, 0, 0, d:d + 1, :]
        message_ref[0:CASES, :] = rhs_ref[d] * there[2 * d + 1].astype(F32)
        wanted = lax.broadcasted_iota(jnp.int32, (FD, FD), 0)
        hits = (wanted == jnp.broadcast_to(row, (FD, FD))).astype(F32).astype(BF16)
        count = lax.broadcasted_iota(jnp.int32, (16, FD), 1).astype(F32).astype(BF16)
        inverse = lax.dot_general(
            count, hits, (((1,), (1,)), ((), ())), preferred_element_type=F32
        )
        message_ref[CASES:CASES + 1, :] = row.astype(F32)
        message_ref[CASES + 1:CASES + 2, :] = inverse[0:1, :]
        message_ref[CASES + 2:CASES + 8, :] = jnp.zeros((6, FD), F32)


def put_dense(pairs, diag_ref, couple_ref, high_ref, low_ref):
    high_ref[...] = jnp.zeros_like(high_ref)
    low_ref[...] = jnp.zeros_like(low_ref)

    def put(rows, cols, block):
        high, low = halves(block)
        high_ref[pl.ds(rows, FD), pl.ds(cols, FD)] = high
        low_ref[pl.ds(rows, FD), pl.ds(cols, FD)] = low

    for f in range(6):
        put(f * FD, f * FD, diag_ref[f])
    for k in range(6):
        first = pl.multiple_of(pairs[0, 0, 0, k, 0] * FD, FD)
        second = pl.multiple_of(pairs[0, 0, 0, k, 1] * FD, FD)
        block = couple_ref[k]
        put(second, first, block)
        put(first, second, block.T)


def setup_kernel(pairs, ids, *rest):
    sources, rest = rest[:6], rest[6:]
    (dh_ref, dl_ref, fh_ref, fl_ref, kh_ref, kl_ref, wh_ref, wl_ref, expand_ref, target_ref) = rest[:10]
    held, (pad, square, sems) = rest[10:16], rest[16:]
    copies = [
        pltpu.make_async_copy(source, target, sems.at[i])
        for i, (source, target) in enumerate(zip(sources, held))
    ]
    for copy in copies:
        copy.start()
    lanes = lax.broadcasted_iota(jnp.int32, (8, FD), 1) % SUBS
    target = jnp.full((8, FD), -1, jnp.int32)
    for r in range(24):
        target = jnp.where(lanes == r, (r % 3) * QPAD + ids[0, 0, 0, r // 3], target)
    target_ref[...] = target.astype(F32)
    pad[...] = jnp.zeros_like(pad)
    lanes = lax.broadcasted_iota(jnp.int32, (1, 3 * QPAD), 1)
    for r in range(24):
        spot = (r % 3) * QPAD + ids[0, 0, 0, r // 3]
        pad[r:r + 1, :] = (lanes == spot).astype(F32)
    expand_ref[...] = pad[...].astype(BF16)
    copies[0].wait()
    copies[1].wait()
    put_dense(pairs, held[0], held[1], dh_ref, dl_ref)
    copies[2].wait()
    copies[3].wait()
    put_dense(pairs, held[2], held[3], fh_ref, fl_ref)
    square[...] = jnp.zeros_like(square)
    copies[4].wait()
    for p in range(3):
        for q in range(3):
            square[p * QPAD:p * QPAD + 192, q * QPAD:q * QPAD + 192] = held[4][
                p * 192:(p + 1) * 192, q * 192:(q + 1) * 192
            ]
    high, low = halves(square[...])
    kh_ref[...] = high
    kl_ref[...] = low
    pad[...] = jnp.zeros_like(pad)
    copies[5].wait()
    pad[0:24, :] = held[5][...]
    for f in range(6):
        high, low = halves(pad[:, f * FD:(f + 1) * FD].T)
        wh_ref[f * FD:(f + 1) * FD, :] = high
        wl_ref[f * FD:(f + 1) * FD, :] = low


def start_kernel(rhs_ref, mx_ref, my_ref, mz_ref, dh_ref, dl_ref, coupling_ref, target_ref,
                 field_ref, shown_ref, own_ref, first_ref, second_ref):
    _, _, there = position()
    messages = (mx_ref, my_ref, mz_ref)
    parts = []
    for d in range(3):
        parts.append(messages[d][0:CASES, :])
        parts.append(rhs_ref[d] * there[2 * d + 1].astype(F32))
    field = jnp.concatenate(parts, axis=1)
    field_ref[...] = field
    _, shown = apply_dense(field, messages, dh_ref, dl_ref)
    shown_ref[...] = shown
    own = lower_changed(coupling_ref[...], partner_rows(messages))
    own_ref[...] = own
    target = target_ref[...]
    put_cubes(
        first_ref, second_ref,
        lambda f: jnp.concatenate([face(shown, f), face(own, f), target], axis=0),
    )


def joint_kernel(own_ref, target_ref, first_ref, second_ref, gh_ref, gl_ref, pick_ref, whole):
    _, _, there = position()
    others = take_cubes(first_ref, second_ref, slice(CASES, CASES + 32))
    whole[...] = jnp.zeros_like(whole)
    whole[0:24, :] = own_ref[...]
    lanes = lax.broadcasted_iota(jnp.int32, (8, FD), 1)
    targets = [target_ref[...]]
    for f in range(6):
        exists = there[f].astype(F32)
        whole[SUBS * (f + 1):SUBS * (f + 1) + 24, f * FD:(f + 1) * FD] = (
            others[f][0:24, :] * exists
        )
        targets.append(others[f][24:32, :] * exists)
    high, low = halves(whole[...])
    gh_ref[...] = high
    gl_ref[...] = low
    rows = lax.broadcasted_iota(jnp.int32, (3 * QPAD, FD), 0)
    for half in range(2):
        wanted = jnp.full((8, FD), -1.0, F32)
        for n in range(4 * half, min(4 * half + 4, 7)):
            wanted = jnp.where(lanes // SUBS == n % 4, targets[n], wanted)
        wanted = jnp.broadcast_to(wanted[0:1, :].astype(jnp.int32), (3 * QPAD, FD))
        pick_ref[:, half * FD:(half + 1) * FD] = (rows == wanted).astype(F32).astype(BF16)


def load_kernel(first, mx_ref, my_ref, mz_ref, shown_ref, one_ref, two_ref, residual_ref, fh_ref,
                fl_ref, wh_ref, wl_ref, expand_ref, *rest):
    if first:
        z_ref, flexed_ref, out_ref = rest
    else:
        search_ref, applied_ref, z_ref, flexed_ref, out_ref = rest
    messages = (mx_ref, my_ref, mz_ref)
    here, _, there = position()
    across = jnp.concatenate(take_cubes(one_ref, two_ref, slice(0, CASES)), axis=1)
    z = 0.25 * (shown_ref[...] + across) * mask_row(there)
    z_ref[...] = z
    loads, flexed = apply_dense(z, messages, fh_ref, fl_ref)
    flexed_ref[...] = flexed
    corner = dot_split(loads, wh_ref, wl_ref)
    gathered = dot_exact(corner, expand_ref[...])

    def upper_sum(a):
        return jnp.sum(face(a, 1) + face(a, 3) + face(a, 5), axis=1, keepdims=True)

    sums = [upper_sum(z * residual_ref[...]), jnp.sum(z * flexed, axis=1, keepdims=True)]
    if not first:
        sums.append(
            upper_sum(z * applied_ref[...])
            + jnp.sum(search_ref[...] * flexed, axis=1, keepdims=True)
        )
    lanes = lax.broadcasted_iota(jnp.int32, (CASES, FD), 1)
    out_ref[...] = jnp.zeros_like(out_ref)
    for b in range(6):
        block = face(gathered, b)
        if b == 1:
            for t, value in enumerate(sums):
                block = jnp.where(lanes == 64 + t, value, block)
        for q in range(4):
            out_ref[4 * b + q, 4] = block[4 * q:4 * q + 4, :]
    for f, by in enumerate(steps()):
        @pl.when(there[f])
        def _():
            put_rows(out_ref, here + by, face(flexed, f))


def layer_kernel(slots_ref, flexed_ref, out_ref):
    _, layer, there = position()
    total = jnp.sum(slots_ref[:, 4], axis=0)
    out_ref[...] = jnp.zeros_like(out_ref)
    for i in range(out_ref.shape[0]):
        out_ref[i, 4] = total
    for f, by in ((4, -1), (5, 1)):
        @pl.when(there[f])
        def _():
            put_rows(out_ref, layer + by, flexed_ref[:, f * FD:(f + 1) * FD])


def spread_kernel(slots_ref, out_ref):
    total = jnp.sum(slots_ref[:, 4], axis=0)
    for i in range(out_ref.shape[0]):
        out_ref[i] = total


def step_kernel(first, last, total_ref, slots_ref, layers_ref, flexed_ref,
                z_ref, residual_ref, kh_ref, kl_ref, gh_ref, gl_ref, pick_ref, *rest):
    rest = list(rest)
    if not last:
        mx_ref, my_ref, mz_ref, dh_ref, dl_ref = rest[:5]
        rest = rest[5:]
    if not first:
        search_ref, applied_ref, load_ref, scale_ref, iterate_ref = rest[:5]
        rest = rest[5:]
    here, layer, there = position()
    across = []
    for f, by in enumerate(steps()):
        across.append(take_rows(slots_ref, jnp.where(there[f], here + by, here)))
    for f, by in ((4, -1), (5, 1)):
        across.append(take_rows(layers_ref, jnp.where(there[f], layer + by, layer)))
    mask = mask_row(there)
    applied = (flexed_ref[...] + jnp.concatenate(across, axis=1)) * mask
    search = z_ref[...]
    blocks = []
    for b in range(6):
        blocks.append(jnp.concatenate([total_ref[4 * b + q] for q in range(4)], axis=0))
    norm = blocks[1][:, 64:65]
    energy = blocks[1][:, 65:66]
    load = jnp.concatenate(blocks, axis=1)
    lanes = lax.broadcasted_iota(jnp.int32, load.shape, 1) % QPAD
    load = jnp.where(lanes < 192, load, 0.0)
    if not first:
        beta = norm / scale_ref[:, 0:1]
        cross = blocks[1][:, 66:67]
        energy = energy + beta * cross + beta * beta * scale_ref[:, 1:2]
        applied = applied + beta * applied_ref[...]
        search = search + beta * search_ref[...]
        load = load + beta * load_ref[...]
    coarse = dot_split(load, kh_ref, kl_ref)
    step = norm / (energy + jnp.sum(load * coarse, axis=1, keepdims=True))
    corner = dot_exact(coarse, pick_ref[...])
    correction = dot_split(corner, gh_ref, gl_ref) * mask
    residual = residual_ref[...] - step * (applied + correction)
    moved = step * search
    if last:
        multipliers_ref, left_ref = rest
        for d in range(3):
            multipliers_ref[d] = iterate_ref[d] + face(moved, 2 * d + 1)
            left_ref[d] = face(residual, 2 * d + 1)
        return
    search_out, applied_out, load_out, scale_out, iterate_out, residual_out, shown_ref = rest[:7]
    first_ref, second_ref = rest[7:]
    search_out[...] = search
    applied_out[...] = applied
    load_out[...] = load
    residual_out[...] = residual
    lanes = lax.broadcasted_iota(jnp.int32, (CASES, FD), 1)
    scale_out[...] = jnp.where(lanes == 0, norm, energy)
    for d in range(3):
        moved_face = face(moved, 2 * d + 1)
        iterate_out[d] = moved_face if first else iterate_ref[d] + moved_face
    _, shown = apply_dense(residual, (mx_ref, my_ref, mz_ref), dh_ref, dl_ref)
    shown_ref[...] = shown
    put_cubes(first_ref, second_ref, lambda f: face(shown, f))


def passed_along(shard, axis, by):
    peers = lax.axis_size(axis)
    pairs = [(i, i + by) for i in range(peers) if 0 <= i + by < peers]
    return lax.ppermute(shard, axis, pairs)


def swapped(slots, axes):
    return lax.all_to_all(slots, axes, 0, 0)


def across_faces(one, two):
    one = lax.all_to_all(one, AXES, 0, 0, axis_index_groups=cube_groups(0))
    one, two = lax.optimization_barrier((one, two))
    return [one, lax.all_to_all(two, AXES, 0, 0, axis_index_groups=cube_groups(1))]


def body(
    jump_rhs,
    flex_diag,
    flex_couple,
    dirichlet_diag,
    dirichlet_couple,
    face_pairs,
    corner_coupling,
    coarse_ids,
    partner,
    coarse_inverse,
):
    gx, gy, gz = (lax.axis_size(a) for a in AXES)
    plane = gx * gy
    rhs = jump_rhs.reshape(3, CASES, FD)
    coupling = corner_coupling.reshape(24, WIDE)
    square = (WIDE, WIDE)
    wide = (CASES, WIDE)
    long = CASES + 32

    messages = call(
        prep_kernel, [((CASES + 8, FD), F32)] * 3, [rhs, partner]
    )
    messages = [passed_along(m, a, 1) for m, a in zip(messages, AXES)]
    blocks = [b.reshape(6, FD, FD) for b in (dirichlet_diag, dirichlet_couple, flex_diag, flex_couple)]
    sources = blocks + [coarse_inverse, coupling]
    *dense, target = call(
        setup_kernel,
        [(square, BF16)] * 6 + [((WIDE, FD), BF16)] * 2 + [((FD, WIDE), BF16), ((8, FD), F32)],
        [face_pairs, coarse_ids] + sources,
        specs=[SMEM] * 2 + [pl.BlockSpec(memory_space=pltpu.HBM)] * 6,
        scratch=[pltpu.VMEM(source.shape, F32) for source in sources]
        + [pltpu.VMEM((FD, WIDE), F32), pltpu.VMEM(square, F32), pltpu.SemaphoreType.DMA((6,))],
    )
    dirichlet, flex, inverse, weights = dense[0:2], dense[2:4], dense[4:6], dense[6:9]
    residual, shown, own, one, two = call(
        start_kernel,
        [(wide, F32), (wide, F32), ((24, WIDE), F32)] + [((8, long, FD), F32)] * 2,
        [rhs, *messages, *dirichlet, coupling, target],
    )
    others = across_faces(one, two)
    joint = call(
        joint_kernel,
        [((QPAD, WIDE), BF16), ((QPAD, WIDE), BF16), ((3 * QPAD, QPAD), BF16)],
        [own, target, *others],
        scratch=[pltpu.VMEM((QPAD, WIDE), F32)],
    )
    joint, others = lax.optimization_barrier((joint, others))

    kept = []
    for iteration in range(ITERS):
        first, last = iteration == 0, iteration + 1 == ITERS
        z, flexed, out = call(
            functools.partial(load_kernel, first),
            [(wide, F32), (wide, F32), ((plane, 5, 4, FD), F32)],
            [*messages, shown, *others, residual, *flex, *weights, *kept[:2]],
        )
        slots = swapped(out, PLANE)
        (layers,) = call(layer_kernel, [((gz, 5, 4, FD), F32)], [slots, flexed])
        layers = swapped(layers, "gz")
        (total,) = call(spread_kernel, [((plane, 4, FD), F32)], [layers])
        total = swapped(total, PLANE)
        common = [total, slots, layers, flexed, z, residual, *inverse, *joint]
        kernel = functools.partial(step_kernel, first, last)
        if last:
            multipliers, left = call(kernel, [((3, CASES, FD), F32)] * 2, common + kept)
            break
        *kept, residual, shown, one, two = call(
            kernel,
            [(wide, F32)] * 3 + [((CASES, FD), F32), ((3, CASES, FD), F32), (wide, F32), (wide, F32)]
            + [((8, CASES, FD), F32)] * 2,
            common + [*messages, *dirichlet] + kept,
        )
        others = across_faces(one, two)
    return multipliers.reshape(jump_rhs.shape), left.reshape(jump_rhs.shape)


def solution(mesh):
    placed = (
        P("gx", "gy", "gz", None, None, None),
        P("gx", "gy", "gz", None, None, None),
        P("gx", "gy", "gz", None, None, None),
        P("gx", "gy", "gz", None, None, None),
        P("gx", "gy", "gz", None, None, None),
        P("gx", "gy", "gz", None, None),
        P("gx", "gy", "gz", None, None),
        P("gx", "gy", "gz", None),
        P("gx", "gy", "gz", None, None),
        P(),
    )
    return jax.shard_map(
        body,
        mesh=mesh,
        in_specs=placed,
        out_specs=(P("gx", "gy", "gz", None, None, None), P("gx", "gy", "gz", None, None, None)),
        check_vma=False,
    )
```

```python
import functools

import jax
import jax.numpy as jnp
from jax import lax
from jax.experimental import pallas as pl
from jax.experimental.pallas import tpu as pltpu
from jax.sharding import PartitionSpec as P

ITERS = 3
CASES = 16
FD = 128
WIDE = 6 * FD
QPAD = 256
SUBS = 32
AXES = ("gx", "gy", "gz")
PLANE = ("gx", "gy")
F32 = jnp.float32
BF16 = jnp.bfloat16
VMEM = pl.BlockSpec(memory_space=pltpu.VMEM)
SMEM = pl.BlockSpec(memory_space=pltpu.SMEM)


def call(kernel, outs, args, specs=(), scratch=()):
    return pl.pallas_call(
        kernel,
        out_shape=[jax.ShapeDtypeStruct(shape, dtype) for shape, dtype in outs],
        in_specs=list(specs) + [VMEM] * (len(args) - len(specs)),
        out_specs=[VMEM] * len(outs),
        scratch_shapes=list(scratch),
        compiler_params=pltpu.CompilerParams(vmem_limit_bytes=40 * 1024 * 1024),
    )(*args)


def halves(x):
    high = x.astype(BF16)
    return high, (x - high.astype(F32)).astype(BF16)


def dot_exact(x, selector):
    rows = x.shape[0]
    high, low = halves(x)
    both = jnp.dot(jnp.concatenate([high, low], 0), selector, preferred_element_type=F32)
    return both[:rows] + both[rows:]


def dot_across(x, matrix):
    return lax.dot_general(x, matrix, (((1,), (1,)), ((), ())), preferred_element_type=F32)


def dot_split(x, high_ref, low_ref):
    rows = x.shape[0]
    high, low = halves(x)
    both = jnp.dot(jnp.concatenate([high, low], 0), high_ref[...], preferred_element_type=F32)
    rest = jnp.dot(high, low_ref[...], preferred_element_type=F32)
    return both[:rows] + both[rows:] + rest


def face(x, f):
    return x[:, f * FD:(f + 1) * FD]


def take(x, row):
    index = jnp.broadcast_to(row.astype(jnp.int32), x.shape)
    return jnp.take_along_axis(x, index, axis=1, mode="promise_in_bounds")


def lower_changed(x, rows):
    parts = []
    for d in range(3):
        parts.append(-take(face(x, 2 * d), rows[d]))
        parts.append(face(x, 2 * d + 1))
    return jnp.concatenate(parts, axis=1)


def partner_rows(messages):
    return [m[CASES:CASES + 1, :] for m in messages]


def inverse_rows(messages):
    return [m[CASES + 1:CASES + 2, :] for m in messages]


def apply_dense(field, messages, high_ref, low_ref):
    loads = lower_changed(field, inverse_rows(messages))
    return loads, lower_changed(dot_split(loads, high_ref, low_ref), partner_rows(messages))


def position():
    gy = lax.axis_size("gy")
    places = [(lax.axis_index(a), lax.axis_size(a)) for a in ("gx", "gy", "gz")]
    there = []
    for place, size in places:
        there += [place > 0, place < size - 1]
    return places[0][0] * gy + places[1][0], places[2][0], there


def steps():
    gy = lax.axis_size("gy")
    return (-gy, gy, -1, 1)


def cube_groups(start):
    gx, gy, gz = (lax.axis_size(a) for a in AXES)
    return [
        [
            (i + a) % gx * gy * gz + (j + b) % gy * gz + (k + c) % gz
            for a in range(2) for b in range(2) for c in range(2)
        ]
        for i in range(start, gx + start, 2)
        for j in range(start, gy + start, 2)
        for k in range(start, gz + start, 2)
    ]


def cube_places():
    odd = [lax.rem(lax.axis_index(a), 2) for a in AXES]
    first = odd[0] * 4 + odd[1] * 2 + odd[2]
    found = []
    for d in range(3):
        bit = 4 >> d
        other = first + bit * (1 - 2 * odd[d])
        found.append((odd[d] == 0, other, 7 - other))
    return found


def put_cubes(first_ref, second_ref, piece):
    first_ref[...] = jnp.zeros_like(first_ref)
    second_ref[...] = jnp.zeros_like(second_ref)
    for d, (even, one, two) in enumerate(cube_places()):
        lower, upper = piece(2 * d), piece(2 * d + 1)
        first_ref[one] = jnp.where(even, upper, lower)
        second_ref[two] = jnp.where(even, lower, upper)


def take_cubes(first_ref, second_ref, rows):
    got = []
    for even, one, two in cube_places():
        a, b = first_ref[one, rows, :], second_ref[two, rows, :]
        got += [jnp.where(even, b, a), jnp.where(even, a, b)]
    return got


def mask_row(there):
    return jnp.concatenate([jnp.full((1, FD), t.astype(F32)) for t in there], axis=1)


def put_rows(slots_ref, spot, rows):
    for q in range(4):
        slots_ref[spot, q] = rows[4 * q:4 * q + 4, :]


def take_rows(slots_ref, spot):
    return jnp.concatenate([slots_ref[spot, q] for q in range(4)], axis=0)


def prep_kernel(rhs_ref, partner_ref, *message_refs):
    _, _, there = position()
    for d in range(3):
        message_ref = message_refs[d]
        row = partner_ref[0, 0, 0, d:d + 1, :]
        message_ref[0:CASES, :] = rhs_ref[d] * there[2 * d + 1].astype(F32)
        wanted = lax.broadcasted_iota(jnp.int32, (FD, FD), 0)
        hits = (wanted == jnp.broadcast_to(row, (FD, FD))).astype(F32).astype(BF16)
        count = lax.broadcasted_iota(jnp.int32, (16, FD), 1).astype(F32).astype(BF16)
        inverse = lax.dot_general(
            count, hits, (((1,), (1,)), ((), ())), preferred_element_type=F32
        )
        message_ref[CASES:CASES + 1, :] = row.astype(F32)
        message_ref[CASES + 1:CASES + 2, :] = inverse[0:1, :]
        message_ref[CASES + 2:CASES + 8, :] = jnp.zeros((6, FD), F32)


def put_dense(pairs, diag_ref, couple_ref, high_ref, low_ref):
    high_ref[...] = jnp.zeros_like(high_ref)
    low_ref[...] = jnp.zeros_like(low_ref)

    def put(rows, cols, block):
        high, low = halves(block)
        high_ref[pl.ds(rows, FD), pl.ds(cols, FD)] = high
        low_ref[pl.ds(rows, FD), pl.ds(cols, FD)] = low

    for f in range(6):
        put(f * FD, f * FD, diag_ref[f])
    for k in range(6):
        first = pl.multiple_of(pairs[0, 0, 0, k, 0] * FD, FD)
        second = pl.multiple_of(pairs[0, 0, 0, k, 1] * FD, FD)
        block = couple_ref[k]
        put(second, first, block)
        put(first, second, block.T)


def target_rows(ids):
    lanes = lax.broadcasted_iota(jnp.int32, (8, FD), 1) % SUBS
    target = jnp.full((8, FD), -1, jnp.int32)
    for r in range(24):
        target = jnp.where(lanes == r, (r % 3) * QPAD + ids[0, 0, 0, r // 3], target)
    return target.astype(F32)


def dense_kernel(pairs, ids, diag_ref, couple_ref, high_ref, low_ref, target_ref):
    put_dense(pairs, diag_ref, couple_ref, high_ref, low_ref)
    target_ref[...] = target_rows(ids)


def start_kernel(rhs_ref, mx_ref, my_ref, mz_ref, dh_ref, dl_ref, coupling_ref, target_ref,
                 field_ref, shown_ref, own_ref, first_ref, second_ref):
    _, _, there = position()
    messages = (mx_ref, my_ref, mz_ref)
    parts = []
    for d in range(3):
        parts.append(messages[d][0:CASES, :])
        parts.append(rhs_ref[d] * there[2 * d + 1].astype(F32))
    field = jnp.concatenate(parts, axis=1)
    field_ref[...] = field
    _, shown = apply_dense(field, messages, dh_ref, dl_ref)
    shown_ref[...] = shown
    own = lower_changed(coupling_ref[...], partner_rows(messages))
    own_ref[...] = own
    target = target_ref[...]
    put_cubes(
        first_ref, second_ref,
        lambda f: jnp.concatenate([face(shown, f), face(own, f), target], axis=0),
    )


def setup_kernel(pairs, ids, diag_ref, couple_ref, inverse_ref, coupling_ref, own_ref, target_ref,
                 first_ref, second_ref, fh_ref, fl_ref, kh_ref, kl_ref, wh_ref, wl_ref, expand_ref,
                 gh_ref, gl_ref, pick_ref, pad, square):
    _, _, there = position()
    put_dense(pairs, diag_ref, couple_ref, fh_ref, fl_ref)
    square[...] = jnp.zeros_like(square)
    for p in range(3):
        for q in range(3):
            square[p * QPAD:p * QPAD + 192, q * QPAD:q * QPAD + 192] = inverse_ref[
                p * 192:(p + 1) * 192, q * 192:(q + 1) * 192
            ]
    high, low = halves(square[...])
    kh_ref[...] = high
    kl_ref[...] = low
    pad[...] = jnp.zeros_like(pad)
    pad[0:24, :] = coupling_ref[...]
    for f in range(6):
        high, low = halves(pad[0:FD, f * FD:(f + 1) * FD].T)
        wh_ref[f * FD:(f + 1) * FD, :] = high
        wl_ref[f * FD:(f + 1) * FD, :] = low
    lanes = lax.broadcasted_iota(jnp.int32, (1, 3 * QPAD), 1)
    for r in range(24):
        spot = (r % 3) * QPAD + ids[0, 0, 0, r // 3]
        pad[r:r + 1, :] = (lanes == spot).astype(F32)
    expand_ref[...] = pad[0:FD, :].astype(BF16)
    others = take_cubes(first_ref, second_ref, slice(CASES, CASES + 32))
    pad[0:24, :] = own_ref[...]
    lanes = lax.broadcasted_iota(jnp.int32, (8, FD), 1)
    targets = [target_ref[...]]
    for f in range(6):
        exists = there[f].astype(F32)
        pad[SUBS * (f + 1):SUBS * (f + 1) + 24, f * FD:(f + 1) * FD] = others[f][0:24, :] * exists
        targets.append(others[f][24:32, :] * exists)
    high, low = halves(pad[...])
    gh_ref[...] = high
    gl_ref[...] = low
    rows = lax.broadcasted_iota(jnp.int32, (3 * QPAD, FD), 0)
    for half in range(2):
        wanted = jnp.full((8, FD), -1.0, F32)
        for n in range(4 * half, min(4 * half + 4, 7)):
            wanted = jnp.where(lanes // SUBS == n % 4, targets[n], wanted)
        wanted = jnp.broadcast_to(wanted[0:1, :].astype(jnp.int32), (3 * QPAD, FD))
        pick_ref[:, half * FD:(half + 1) * FD] = (rows == wanted).astype(F32).astype(BF16)


def face_sum(x, faces=range(6)):
    total = None
    for f in faces:
        total = face(x, f) if total is None else total + face(x, f)
    return total


def put_payload(out_ref, gathered, extras):
    lanes = lax.broadcasted_iota(jnp.int32, (CASES, FD), 1)
    for b in range(6):
        block = face(gathered, b)
        if b == 1:
            for t, value in enumerate(extras):
                block = jnp.where(lanes == 64 + t, value, block)
        for c in range(CASES):
            out_ref[2 * c + b // 3, 4, b % 3:b % 3 + 1, :] = block[c:c + 1, :]


def load_kernel(mx_ref, my_ref, mz_ref, shown_ref, one_ref, two_ref, residual_ref, fh_ref,
                fl_ref, wh_ref, wl_ref, expand_ref, z_ref, flexed_ref, out_ref):
    here, _, there = position()
    across = jnp.concatenate(take_cubes(one_ref, two_ref, slice(0, CASES)), axis=1)
    z = 0.25 * (shown_ref[...] + across) * mask_row(there)
    z_ref[...] = z
    loads, flexed = apply_dense(z, (mx_ref, my_ref, mz_ref), fh_ref, fl_ref)
    flexed_ref[...] = flexed
    gathered = dot_exact(dot_split(loads, wh_ref, wl_ref), expand_ref[...])
    norm = jnp.sum(face_sum(z * residual_ref[...], (1, 3, 5)), axis=1, keepdims=True)
    energy = jnp.sum(face_sum(z * flexed), axis=1, keepdims=True)
    out_ref[...] = jnp.zeros_like(out_ref)
    put_payload(out_ref, gathered, [norm, energy])
    for f, by in enumerate(steps()):
        @pl.when(there[f])
        def _():
            put_rows(out_ref, here + by, face(flexed, f))


def put_layers(out_ref, total, flexed_ref, layer, there):
    out_ref[...] = jnp.zeros_like(out_ref)
    for i in range(out_ref.shape[0]):
        out_ref[i, 4] = total
    for f, by in ((4, -1), (5, 1)):
        @pl.when(there[f])
        def _():
            put_rows(out_ref, layer + by, flexed_ref[:, f * FD:(f + 1) * FD])


def layer_kernel(slots_ref, flexed_ref, out_ref):
    _, layer, there = position()
    put_layers(out_ref, jnp.sum(slots_ref[:, 4], axis=0), flexed_ref, layer, there)


def spread_kernel(slots_ref, out_ref):
    total = jnp.sum(slots_ref[:, 4], axis=0)
    for i in range(out_ref.shape[0]):
        out_ref[i] = total


def flex_kernel(mx_ref, my_ref, mz_ref, shown_ref, slots_ref, below_ref, above_ref, fh_ref, fl_ref,
                search_ref, applied_ref, z_ref, flexed_ref, out_ref, turn):
    here, layer, there = position()
    across = []
    for f, by in enumerate(steps()):
        across.append(take_rows(slots_ref, jnp.where(there[f], here + by, here)))
    across += [below_ref[...], above_ref[...]]
    z = 0.25 * (shown_ref[...] + jnp.concatenate(across, axis=1)) * mask_row(there)
    z_ref[...] = z
    _, flexed = apply_dense(z, (mx_ref, my_ref, mz_ref), fh_ref, fl_ref)
    flexed_ref[...] = flexed
    turn[...] = jnp.zeros_like(turn)
    turn[0:CASES, :] = face_sum(z * flexed)
    turn[CASES:2 * CASES, :] = (
        face_sum(z * applied_ref[...], (1, 3, 5)) + face_sum(search_ref[...] * flexed)
    )
    sums = jnp.sum(turn[...].T, axis=0, keepdims=True)
    total = jnp.sum(slots_ref[:, 4], axis=0)
    rows = lax.broadcasted_iota(jnp.int32, total.shape, 0)
    total = jnp.where(rows == 3, jnp.broadcast_to(sums, total.shape), total)
    put_layers(out_ref, total, flexed_ref, layer, there)


def share_kernel(layers_ref, flexed_ref, out_ref):
    here, _, there = position()
    total = jnp.sum(layers_ref[:, 4], axis=0)
    out_ref[...] = jnp.zeros_like(out_ref)
    for i in range(out_ref.shape[0]):
        out_ref[i, 4] = total
    for f, by in enumerate(steps()):
        @pl.when(there[f])
        def _():
            put_rows(out_ref, here + by, flexed_ref[:, f * FD:(f + 1) * FD])


def step_kernel(first, last, total_ref, slots_ref, layers_ref, flexed_ref,
                z_ref, residual_ref, kh_ref, kl_ref, gh_ref, gl_ref, pick_ref, *rest):
    rest, whole = list(rest[:-1]), rest[-1]
    if not last:
        mx_ref, my_ref, mz_ref, dh_ref, dl_ref = rest[:5]
        rest = rest[5:]
    if not first:
        search_ref, applied_ref, load_ref, scale_ref, iterate_ref = rest[:5]
        rest = rest[5:]
    here, layer, there = position()
    across = []
    for f, by in enumerate(steps()):
        across.append(take_rows(slots_ref, jnp.where(there[f], here + by, here)))
    for f, by in ((4, -1), (5, 1)):
        across.append(take_rows(layers_ref, jnp.where(there[f], layer + by, layer)))
    mask = mask_row(there)
    applied = (flexed_ref[...] + jnp.concatenate(across, axis=1)) * mask
    search = z_ref[...]
    for c in range(CASES):
        for b in range(6):
            slot, row = 2 * c + b // 3, slice(b % 3, b % 3 + 1)
            whole[c:c + 1, b * FD:(b + 1) * FD] = (
                total_ref[slot, row, :] if first else total_ref[slot, 4, row, :]
            )
    load = whole[...]
    norm = load[:, FD + 64:FD + 65]
    if first:
        energy = load[:, FD + 65:FD + 66]
    else:
        sums = jnp.sum(total_ref[:, 4], axis=0)[3:4, :]
        sums = jnp.broadcast_to(sums, (FD, FD)).T
        energy, cross = sums[0:CASES, 0:1], sums[CASES:2 * CASES, 0:1]
    lanes = lax.broadcasted_iota(jnp.int32, load.shape, 1) % QPAD
    load = jnp.where(lanes < 192, load, 0.0)
    if not first:
        beta = norm / scale_ref[:, 0:1]
        energy = energy + beta * cross + beta * beta * scale_ref[:, 1:2]
        applied = applied + beta * applied_ref[...]
        search = search + beta * search_ref[...]
        load = load + beta * load_ref[...]
    coarse = dot_split(load, kh_ref, kl_ref)
    step = norm / (energy + jnp.sum(load * coarse, axis=1, keepdims=True))
    corner = dot_exact(coarse, pick_ref[...])
    correction = dot_split(corner, gh_ref, gl_ref) * mask
    residual = residual_ref[...] - step * (applied + correction)
    moved = step * search
    if last:
        multipliers_ref, left_ref = rest
        for d in range(3):
            multipliers_ref[d] = iterate_ref[d] + face(moved, 2 * d + 1)
            left_ref[d] = face(residual, 2 * d + 1)
        return
    search_out, applied_out, load_out, scale_out, iterate_out, residual_out, shown_ref = rest[:7]
    out_ref, down_ref, up_ref = rest[7:]
    search_out[...] = search
    applied_out[...] = applied
    load_out[...] = load
    residual_out[...] = residual
    lanes = lax.broadcasted_iota(jnp.int32, (CASES, FD), 1)
    scale_out[...] = jnp.where(lanes == 0, norm, energy)
    for d in range(3):
        moved_face = face(moved, 2 * d + 1)
        iterate_out[d] = moved_face if first else iterate_ref[d] + moved_face
    _, shown = apply_dense(residual, (mx_ref, my_ref, mz_ref), dh_ref, dl_ref)
    shown_ref[...] = shown
    down_ref[...] = face(shown, 4)
    up_ref[...] = face(shown, 5)
    share = 0.25 * shown * mask
    high, low = halves(share)
    both = dot_across(jnp.concatenate([high, low], 0), gh_ref[...])
    corner = both[:CASES] + both[CASES:] + dot_across(high, gl_ref[...])
    high, low = halves(corner)
    both = dot_across(jnp.concatenate([high, low], 0), pick_ref[...])
    next_norm = jnp.sum(face_sum(share * residual), axis=1, keepdims=True)
    out_ref[...] = jnp.zeros_like(out_ref)
    put_payload(out_ref, both[:CASES] + both[CASES:], [next_norm])
    for f, by in enumerate(steps()):
        @pl.when(there[f])
        def _():
            put_rows(out_ref, here + by, face(shown, f))


def passed_along(shard, axis, by):
    peers = lax.axis_size(axis)
    pairs = [(i, i + by) for i in range(peers) if 0 <= i + by < peers]
    return lax.ppermute(shard, axis, pairs)


def swapped(slots, axes):
    return lax.all_to_all(slots, axes, 0, 0)


def across_faces(one, two):
    one = lax.all_to_all(one, AXES, 0, 0, axis_index_groups=cube_groups(0))
    one, two = lax.optimization_barrier((one, two))
    return [one, lax.all_to_all(two, AXES, 0, 0, axis_index_groups=cube_groups(1))]


def body(
    jump_rhs,
    flex_diag,
    flex_couple,
    dirichlet_diag,
    dirichlet_couple,
    face_pairs,
    corner_coupling,
    coarse_ids,
    partner,
    coarse_inverse,
):
    gx, gy, gz = (lax.axis_size(a) for a in AXES)
    plane = gx * gy
    rhs = jump_rhs.reshape(3, CASES, FD)
    coupling = corner_coupling.reshape(24, WIDE)
    square = (WIDE, WIDE)
    wide = (CASES, WIDE)
    long = CASES + 32

    messages = call(
        prep_kernel, [((CASES + 8, FD), F32)] * 3, [rhs, partner]
    )
    messages = [passed_along(m, a, 1) for m, a in zip(messages, AXES)]
    blocks = [b.reshape(6, FD, FD) for b in (dirichlet_diag, dirichlet_couple, flex_diag, flex_couple)]
    *dirichlet, target = call(
        dense_kernel, [(square, BF16)] * 2 + [((8, FD), F32)],
        [face_pairs, coarse_ids] + blocks[:2], specs=[SMEM] * 2,
    )
    residual, shown, own, one, two = call(
        start_kernel,
        [(wide, F32), (wide, F32), ((24, WIDE), F32)] + [((8, long, FD), F32)] * 2,
        [rhs, *messages, *dirichlet, coupling, target],
    )
    one, two = across_faces(one, two)
    dense = call(
        setup_kernel,
        [(square, BF16)] * 4 + [((WIDE, FD), BF16)] * 2
        + [((FD, WIDE), BF16), ((QPAD, WIDE), BF16), ((QPAD, WIDE), BF16), ((3 * QPAD, QPAD), BF16)],
        [face_pairs, coarse_ids] + blocks[2:] + [coarse_inverse, coupling, own, target, one, two],
        specs=[SMEM] * 2,
        scratch=[pltpu.VMEM((QPAD, WIDE), F32), pltpu.VMEM(square, F32)],
    )
    flex, inverse, weights, joint = dense[0:2], dense[2:4], dense[4:7], dense[7:10]
    stacked = (plane, 5, 4, FD)

    kept = []
    for iteration in range(ITERS):
        first, last = iteration == 0, iteration + 1 == ITERS
        if first:
            z, flexed, slots = call(
                load_kernel,
                [(wide, F32), (wide, F32), (stacked, F32)],
                [*messages, shown, one, two, residual, *flex, *weights],
            )
            slots = swapped(slots, PLANE)
            (layers,) = call(layer_kernel, [((gz, 5, 4, FD), F32)], [slots, flexed])
            layers = swapped(layers, "gz")
            (total,) = call(spread_kernel, [((plane, 4, FD), F32)], [layers])
            total = swapped(total, PLANE)
        else:
            z, flexed, layers = call(
                flex_kernel,
                [(wide, F32), (wide, F32), ((gz, 5, 4, FD), F32)],
                [*messages, shown, slots, below, above, *flex, *kept[:2]],
                scratch=[pltpu.VMEM((FD, FD), F32)],
            )
            layers = swapped(layers, "gz")
            (total,) = call(share_kernel, [(stacked, F32)], [layers, flexed])
            slots = total = swapped(total, PLANE)
        common = [total, slots, layers, flexed, z, residual, *inverse, *joint]
        kernel = functools.partial(step_kernel, first, last)
        scratch = [pltpu.VMEM(wide, F32)]
        if last:
            multipliers, left = call(
                kernel, [((3, CASES, FD), F32)] * 2, common + kept, scratch=scratch
            )
            break
        *kept, residual, shown, slots, down, up = call(
            kernel,
            [(wide, F32)] * 3 + [((CASES, FD), F32), ((3, CASES, FD), F32), (wide, F32), (wide, F32)]
            + [(stacked, F32)] + [((CASES, FD), F32)] * 2,
            common + [*messages, *dirichlet] + kept, scratch=scratch,
        )
        below = passed_along(up, "gz", 1)
        above = passed_along(down, "gz", -1)
        slots, below, above = lax.optimization_barrier((slots, below, above))
        slots = swapped(slots, PLANE)
    return multipliers.reshape(jump_rhs.shape), left.reshape(jump_rhs.shape)


def solution(mesh):
    placed = (
        P("gx", "gy", "gz", None, None, None),
        P("gx", "gy", "gz", None, None, None),
        P("gx", "gy", "gz", None, None, None),
        P("gx", "gy", "gz", None, None, None),
        P("gx", "gy", "gz", None, None, None),
        P("gx", "gy", "gz", None, None),
        P("gx", "gy", "gz", None, None),
        P("gx", "gy", "gz", None),
        P("gx", "gy", "gz", None, None),
        P(),
    )
    return jax.shard_map(
        body,
        mesh=mesh,
        in_specs=placed,
        out_specs=(P("gx", "gy", "gz", None, None, None), P("gx", "gy", "gz", None, None, None)),
        check_vma=False,
    )
```

```python
import functools

import jax
import jax.numpy as jnp
from jax import lax
from jax.experimental import pallas as pl
from jax.experimental.pallas import tpu as pltpu
from jax.sharding import PartitionSpec as P

ITERS = 3
CASES = 16
FD = 128
WIDE = 6 * FD
QPAD = 256
SUBS = 32
AXES = ("gx", "gy", "gz")
PLANE = ("gx", "gy")
F32 = jnp.float32
BF16 = jnp.bfloat16
VMEM = pl.BlockSpec(memory_space=pltpu.VMEM)
SMEM = pl.BlockSpec(memory_space=pltpu.SMEM)


def call(kernel, outs, args, specs=(), scratch=()):
    return pl.pallas_call(
        kernel,
        out_shape=[jax.ShapeDtypeStruct(shape, dtype) for shape, dtype in outs],
        in_specs=list(specs) + [VMEM] * (len(args) - len(specs)),
        out_specs=[VMEM] * len(outs),
        scratch_shapes=list(scratch),
        compiler_params=pltpu.CompilerParams(vmem_limit_bytes=40 * 1024 * 1024),
    )(*args)


def halves(x):
    high = x.astype(BF16)
    return high, (x - high.astype(F32)).astype(BF16)


def dot_exact(x, selector):
    rows = x.shape[0]
    high, low = halves(x)
    both = jnp.dot(jnp.concatenate([high, low], 0), selector, preferred_element_type=F32)
    return both[:rows] + both[rows:]


def dot_across(x, matrix):
    return lax.dot_general(x, matrix, (((1,), (1,)), ((), ())), preferred_element_type=F32)


def dot_split(x, high_ref, low_ref):
    rows = x.shape[0]
    high, low = halves(x)
    both = jnp.dot(jnp.concatenate([high, low], 0), high_ref[...], preferred_element_type=F32)
    rest = jnp.dot(high, low_ref[...], preferred_element_type=F32)
    return both[:rows] + both[rows:] + rest


def face(x, f):
    return x[:, f * FD:(f + 1) * FD]


def take(x, row):
    index = jnp.broadcast_to(row.astype(jnp.int32), x.shape)
    return jnp.take_along_axis(x, index, axis=1, mode="promise_in_bounds")


def lower_changed(x, rows):
    parts = []
    for d in range(3):
        parts.append(-take(face(x, 2 * d), rows[d]))
        parts.append(face(x, 2 * d + 1))
    return jnp.concatenate(parts, axis=1)


def partner_rows(messages):
    return [m[CASES:CASES + 1, :] for m in messages]


def inverse_rows(messages):
    return [m[CASES + 1:CASES + 2, :] for m in messages]


def apply_dense(field, messages, high_ref, low_ref):
    loads = lower_changed(field, inverse_rows(messages))
    return loads, lower_changed(dot_split(loads, high_ref, low_ref), partner_rows(messages))


def position():
    gy = lax.axis_size("gy")
    places = [(lax.axis_index(a), lax.axis_size(a)) for a in ("gx", "gy", "gz")]
    there = []
    for place, size in places:
        there += [place > 0, place < size - 1]
    return places[0][0] * gy + places[1][0], places[2][0], there


def steps():
    gy = lax.axis_size("gy")
    return (-gy, gy, -1, 1)


def mask_row(there):
    return jnp.concatenate([jnp.full((1, FD), t.astype(F32)) for t in there], axis=1)


def put_rows(slots_ref, spot, rows):
    for q in range(4):
        slots_ref[spot, q] = rows[4 * q:4 * q + 4, :]


def take_rows(slots_ref, spot):
    return jnp.concatenate([slots_ref[spot, q] for q in range(4)], axis=0)


def target_rows(ids):
    lanes = lax.broadcasted_iota(jnp.int32, (8, FD), 1) % SUBS
    target = jnp.full((8, FD), -1, jnp.int32)
    for r in range(24):
        target = jnp.where(lanes == r, (r % 3) * QPAD + ids[0, 0, 0, r // 3], target)
    return target.astype(F32)


def prep_kernel(ids, rhs_ref, partner_ref, coupling_ref, *message_refs):
    _, _, there = position()
    target = target_rows(ids)
    for d in range(3):
        up_ref, down_ref = message_refs[d], message_refs[3 + d]
        row = partner_ref[0, 0, 0, d:d + 1, :]
        up_ref[0:CASES, :] = rhs_ref[d] * there[2 * d + 1].astype(F32)
        wanted = lax.broadcasted_iota(jnp.int32, (FD, FD), 0)
        hits = (wanted == jnp.broadcast_to(row, (FD, FD))).astype(F32).astype(BF16)
        count = lax.broadcasted_iota(jnp.int32, (16, FD), 1).astype(F32).astype(BF16)
        up_ref[CASES:CASES + 8, :] = jnp.zeros((8, FD), F32)
        up_ref[CASES:CASES + 1, :] = row.astype(F32)
        up_ref[CASES + 1:CASES + 2, :] = dot_across(count, hits)[0:1, :]
        up_ref[24:48, :] = coupling_ref[:, (2 * d + 1) * FD:(2 * d + 2) * FD]
        up_ref[48:56, :] = target
        down_ref[0:24, :] = coupling_ref[:, 2 * d * FD:(2 * d + 1) * FD]
        down_ref[24:32, :] = target


def put_dense(pairs, diag_ref, couple_ref, high_ref, low_ref):
    high_ref[...] = jnp.zeros_like(high_ref)
    low_ref[...] = jnp.zeros_like(low_ref)

    def put(rows, cols, block):
        high, low = halves(block)
        high_ref[pl.ds(rows, FD), pl.ds(cols, FD)] = high
        low_ref[pl.ds(rows, FD), pl.ds(cols, FD)] = low

    for f in range(6):
        put(f * FD, f * FD, diag_ref[f])
    for k in range(6):
        first = pl.multiple_of(pairs[0, 0, 0, k, 0] * FD, FD)
        second = pl.multiple_of(pairs[0, 0, 0, k, 1] * FD, FD)
        block = couple_ref[k]
        put(second, first, block)
        put(first, second, block.T)


def dense_kernel(pairs, diag_ref, couple_ref, high_ref, low_ref):
    put_dense(pairs, diag_ref, couple_ref, high_ref, low_ref)


def start_kernel(ux_ref, uy_ref, uz_ref, mx_ref, my_ref, mz_ref, nx_ref, ny_ref, nz_ref, dh_ref,
                 dl_ref, coupling_ref, field_ref, shown_ref, gh_ref, gl_ref, pick_ref, down_ref,
                 up_ref, pad):
    _, _, there = position()
    own, messages, above = (ux_ref, uy_ref, uz_ref), (mx_ref, my_ref, mz_ref), (nx_ref, ny_ref, nz_ref)
    parts = []
    for d in range(3):
        parts += [messages[d][0:CASES, :], own[d][0:CASES, :]]
    field = jnp.concatenate(parts, axis=1)
    field_ref[...] = field
    _, shown = apply_dense(field, messages, dh_ref, dl_ref)
    shown_ref[...] = shown
    down_ref[...] = face(shown, 4)
    up_ref[...] = face(shown, 5)
    pad[...] = jnp.zeros_like(pad)
    pad[0:24, :] = lower_changed(coupling_ref[...], partner_rows(messages))
    targets = [own[0][48:56, :]]
    for d in range(3):
        row = own[d][CASES:CASES + 1, :]
        sides = (
            (messages[d][24:48, :], messages[d][48:56, :]),
            (-take(above[d][0:24, :], row), above[d][24:32, :]),
        )
        for f, (rows, target) in zip((2 * d, 2 * d + 1), sides):
            exists = there[f].astype(F32)
            pad[SUBS * (f + 1):SUBS * (f + 1) + 24, f * FD:(f + 1) * FD] = rows * exists
            targets.append(target * exists)
    high, low = halves(pad[...])
    gh_ref[...] = high
    gl_ref[...] = low
    lanes = lax.broadcasted_iota(jnp.int32, (8, FD), 1)
    rows = lax.broadcasted_iota(jnp.int32, (3 * QPAD, FD), 0)
    for half in range(2):
        wanted = jnp.full((8, FD), -1.0, F32)
        for n in range(4 * half, min(4 * half + 4, 7)):
            wanted = jnp.where(lanes // SUBS == n % 4, targets[n], wanted)
        wanted = jnp.broadcast_to(wanted[0:1, :].astype(jnp.int32), (3 * QPAD, FD))
        pick_ref[:, half * FD:(half + 1) * FD] = (rows == wanted).astype(F32).astype(BF16)


def late_kernel(pairs, diag_ref, couple_ref, inverse_ref, _, fh_ref, fl_ref, kh_ref, kl_ref, square):
    put_dense(pairs, diag_ref, couple_ref, fh_ref, fl_ref)
    square[...] = jnp.zeros_like(square)
    for p in range(3):
        for q in range(3):
            square[p * QPAD:p * QPAD + 192, q * QPAD:q * QPAD + 192] = inverse_ref[
                p * 192:(p + 1) * 192, q * 192:(q + 1) * 192
            ]
    high, low = halves(square[...])
    kh_ref[...] = high
    kl_ref[...] = low


def face_sum(x, faces=range(6)):
    total = None
    for f in faces:
        total = face(x, f) if total is None else total + face(x, f)
    return total


def put_payload(out_ref, gathered, extras):
    lanes = lax.broadcasted_iota(jnp.int32, (CASES, FD), 1)
    for b in range(6):
        block = face(gathered, b)
        if b == 1:
            for t, value in enumerate(extras):
                block = jnp.where(lanes == 64 + t, value, block)
        for c in range(CASES):
            out_ref[2 * c + b // 3, 4, b % 3:b % 3 + 1, :] = block[c:c + 1, :]


def sum_kernel(shown_ref, residual_ref, gh_ref, gl_ref, pick_ref, out_ref):
    here, _, there = position()
    shown = shown_ref[...]
    share = 0.25 * shown * mask_row(there)
    high, low = halves(share)
    both = dot_across(jnp.concatenate([high, low], 0), gh_ref[...])
    corner = both[:CASES] + both[CASES:] + dot_across(high, gl_ref[...])
    high, low = halves(corner)
    both = dot_across(jnp.concatenate([high, low], 0), pick_ref[...])
    norm = jnp.sum(face_sum(share * residual_ref[...]), axis=1, keepdims=True)
    out_ref[...] = jnp.zeros_like(out_ref)
    put_payload(out_ref, both[:CASES] + both[CASES:], [norm])
    for f, by in enumerate(steps()):
        @pl.when(there[f])
        def _():
            put_rows(out_ref, here + by, face(shown, f))


def put_layers(out_ref, total, flexed_ref, layer, there):
    out_ref[...] = jnp.zeros_like(out_ref)
    for i in range(out_ref.shape[0]):
        out_ref[i, 4] = total
    for f, by in ((4, -1), (5, 1)):
        @pl.when(there[f])
        def _():
            put_rows(out_ref, layer + by, flexed_ref[:, f * FD:(f + 1) * FD])


def flex_kernel(first, mx_ref, my_ref, mz_ref, shown_ref, slots_ref, below_ref, above_ref, fh_ref,
                fl_ref, *rest):
    rest = list(rest)
    if not first:
        search_ref, applied_ref = rest[:2]
        rest = rest[2:]
    z_ref, flexed_ref, out_ref, turn = rest
    here, layer, there = position()
    across = []
    for f, by in enumerate(steps()):
        across.append(take_rows(slots_ref, jnp.where(there[f], here + by, here)))
    across += [below_ref[...], above_ref[...]]
    z = 0.25 * (shown_ref[...] + jnp.concatenate(across, axis=1)) * mask_row(there)
    z_ref[...] = z
    _, flexed = apply_dense(z, (mx_ref, my_ref, mz_ref), fh_ref, fl_ref)
    flexed_ref[...] = flexed
    turn[...] = jnp.zeros_like(turn)
    turn[0:CASES, :] = face_sum(z * flexed)
    if not first:
        turn[CASES:2 * CASES, :] = (
            face_sum(z * applied_ref[...], (1, 3, 5)) + face_sum(search_ref[...] * flexed)
        )
    sums = jnp.sum(turn[...].T, axis=0, keepdims=True)
    total = jnp.sum(slots_ref[:, 4], axis=0)
    rows = lax.broadcasted_iota(jnp.int32, total.shape, 0)
    total = jnp.where(rows == 3, jnp.broadcast_to(sums, total.shape), total)
    put_layers(out_ref, total, flexed_ref, layer, there)


def share_kernel(layers_ref, flexed_ref, out_ref):
    here, _, there = position()
    total = jnp.sum(layers_ref[:, 4], axis=0)
    out_ref[...] = jnp.zeros_like(out_ref)
    for i in range(out_ref.shape[0]):
        out_ref[i, 4] = total
    for f, by in enumerate(steps()):
        @pl.when(there[f])
        def _():
            put_rows(out_ref, here + by, flexed_ref[:, f * FD:(f + 1) * FD])


def step_kernel(first, last, slots_ref, layers_ref, flexed_ref, z_ref,
                residual_ref, kh_ref, kl_ref, gh_ref, gl_ref, pick_ref, *rest):
    rest, whole = list(rest[:-1]), rest[-1]
    if not last:
        mx_ref, my_ref, mz_ref, dh_ref, dl_ref = rest[:5]
        rest = rest[5:]
    if not first:
        search_ref, applied_ref, load_ref, scale_ref, iterate_ref = rest[:5]
        rest = rest[5:]
    here, layer, there = position()
    across = []
    for f, by in enumerate(steps()):
        across.append(take_rows(slots_ref, jnp.where(there[f], here + by, here)))
    for f, by in ((4, -1), (5, 1)):
        across.append(take_rows(layers_ref, jnp.where(there[f], layer + by, layer)))
    mask = mask_row(there)
    applied = (flexed_ref[...] + jnp.concatenate(across, axis=1)) * mask
    search = z_ref[...]
    for c in range(CASES):
        for b in range(6):
            row = slice(b % 3, b % 3 + 1)
            whole[c:c + 1, b * FD:(b + 1) * FD] = slots_ref[2 * c + b // 3, 4, row, :]
    load = whole[...]
    norm = load[:, FD + 64:FD + 65]
    sums = jnp.sum(slots_ref[:, 4], axis=0)[3:4, :]
    sums = jnp.broadcast_to(sums, (FD, FD)).T
    energy, cross = sums[0:CASES, 0:1], sums[CASES:2 * CASES, 0:1]
    lanes = lax.broadcasted_iota(jnp.int32, load.shape, 1) % QPAD
    load = jnp.where(lanes < 192, load, 0.0)
    if not first:
        beta = norm / scale_ref[:, 0:1]
        energy = energy + beta * cross + beta * beta * scale_ref[:, 1:2]
        applied = applied + beta * applied_ref[...]
        search = search + beta * search_ref[...]
        load = load + beta * load_ref[...]
    coarse = dot_split(load, kh_ref, kl_ref)
    step = norm / (energy + jnp.sum(load * coarse, axis=1, keepdims=True))
    corner = dot_exact(coarse, pick_ref[...])
    correction = dot_split(corner, gh_ref, gl_ref) * mask
    residual = residual_ref[...] - step * (applied + correction)
    moved = step * search
    if last:
        multipliers_ref, left_ref = rest
        for d in range(3):
            multipliers_ref[d] = iterate_ref[d] + face(moved, 2 * d + 1)
            left_ref[d] = face(residual, 2 * d + 1)
        return
    search_out, applied_out, load_out, scale_out, iterate_out, residual_out, shown_ref = rest[:7]
    down_ref, up_ref = rest[7:]
    search_out[...] = search
    applied_out[...] = applied
    load_out[...] = load
    residual_out[...] = residual
    lanes = lax.broadcasted_iota(jnp.int32, (CASES, FD), 1)
    scale_out[...] = jnp.where(lanes == 0, norm, energy)
    for d in range(3):
        moved_face = face(moved, 2 * d + 1)
        iterate_out[d] = moved_face if first else iterate_ref[d] + moved_face
    _, shown = apply_dense(residual, (mx_ref, my_ref, mz_ref), dh_ref, dl_ref)
    shown_ref[...] = shown
    down_ref[...] = face(shown, 4)
    up_ref[...] = face(shown, 5)


def passed_along(shard, axis, by):
    peers = lax.axis_size(axis)
    pairs = [(i, i + by) for i in range(peers) if 0 <= i + by < peers]
    return lax.ppermute(shard, axis, pairs)


def swapped(slots, axes):
    return lax.all_to_all(slots, axes, 0, 0)


def body(
    jump_rhs,
    flex_diag,
    flex_couple,
    dirichlet_diag,
    dirichlet_couple,
    face_pairs,
    corner_coupling,
    coarse_ids,
    partner,
    coarse_inverse,
):
    gx, gy, gz = (lax.axis_size(a) for a in AXES)
    plane = gx * gy
    rhs = jump_rhs.reshape(3, CASES, FD)
    coupling = corner_coupling.reshape(24, WIDE)
    square = (WIDE, WIDE)
    wide = (CASES, WIDE)

    *ups, dx, dy, dz = call(
        prep_kernel, [((56, FD), F32)] * 3 + [((32, FD), F32)] * 3,
        [coarse_ids, rhs, partner, coupling], specs=[SMEM],
    )
    messages = [passed_along(m, a, 1) for m, a in zip(ups, AXES)]
    above = [passed_along(m, a, -1) for m, a in zip((dx, dy, dz), AXES)]
    blocks = [b.reshape(6, FD, FD) for b in (dirichlet_diag, dirichlet_couple, flex_diag, flex_couple)]
    dirichlet = call(
        dense_kernel, [(square, BF16)] * 2, [face_pairs] + blocks[:2], specs=[SMEM]
    )
    residual, shown, *joint, down, up = call(
        start_kernel,
        [(wide, F32)] * 2 + [((QPAD, WIDE), BF16)] * 2 + [((3 * QPAD, QPAD), BF16)]
        + [((CASES, FD), F32)] * 2,
        [*ups, *messages, *above, *dirichlet, coupling],
        scratch=[pltpu.VMEM((QPAD, WIDE), F32)],
    )
    stacked = (plane, 5, 4, FD)

    kept = []
    for iteration in range(ITERS):
        first, last = iteration == 0, iteration + 1 == ITERS
        below = passed_along(up, "gz", 1)
        over = passed_along(down, "gz", -1)
        (slots,) = call(sum_kernel, [(stacked, F32)], [shown, residual, *joint])
        slots, below, over = lax.optimization_barrier((slots, below, over))
        slots = swapped(slots, PLANE)
        if first:
            late = call(
                late_kernel, [(square, BF16)] * 4,
                [face_pairs] + blocks[2:] + [coarse_inverse, slots],
                specs=[SMEM] + [VMEM] * 3 + [pl.BlockSpec(memory_space=pl.ANY)],
                scratch=[pltpu.VMEM(square, F32)],
            )
            flex, inverse = late[:2], late[2:]
        z, flexed, layers = call(
            functools.partial(flex_kernel, first),
            [(wide, F32), (wide, F32), ((gz, 5, 4, FD), F32)],
            [*messages, shown, slots, below, over, *flex, *kept[:2]],
            scratch=[pltpu.VMEM((FD, FD), F32)],
        )
        layers = swapped(layers, "gz")
        (slots,) = call(share_kernel, [(stacked, F32)], [layers, flexed])
        slots = swapped(slots, PLANE)
        common = [slots, layers, flexed, z, residual, *inverse, *joint]
        kernel = functools.partial(step_kernel, first, last)
        scratch = [pltpu.VMEM(wide, F32)]
        if last:
            multipliers, left = call(
                kernel, [((3, CASES, FD), F32)] * 2, common + kept, scratch=scratch
            )
            break
        *kept, residual, shown, down, up = call(
            kernel,
            [(wide, F32)] * 3 + [((CASES, FD), F32), ((3, CASES, FD), F32), (wide, F32), (wide, F32)]
            + [((CASES, FD), F32)] * 2,
            common + [*messages, *dirichlet] + kept, scratch=scratch,
        )
    return multipliers.reshape(jump_rhs.shape), left.reshape(jump_rhs.shape)


def solution(mesh):
    placed = (
        P("gx", "gy", "gz", None, None, None),
        P("gx", "gy", "gz", None, None, None),
        P("gx", "gy", "gz", None, None, None),
        P("gx", "gy", "gz", None, None, None),
        P("gx", "gy", "gz", None, None, None),
        P("gx", "gy", "gz", None, None),
        P("gx", "gy", "gz", None, None),
        P("gx", "gy", "gz", None),
        P("gx", "gy", "gz", None, None),
        P(),
    )
    return jax.shard_map(
        body,
        mesh=mesh,
        in_specs=placed,
        out_specs=(P("gx", "gy", "gz", None, None, None), P("gx", "gy", "gz", None, None, None)),
        check_vma=False,
    )
```

```python
import functools

import jax
import jax.numpy as jnp
from jax import lax
from jax.experimental import pallas as pl
from jax.experimental.pallas import tpu as pltpu
from jax.sharding import PartitionSpec as P

ITERS = 3
CASES = 16
FD = 128
WIDE = 6 * FD
QPAD = 256
SUBS = 32
AXES = ("gx", "gy", "gz")
PLANE = ("gx", "gy")
F32 = jnp.float32
BF16 = jnp.bfloat16
VMEM = pl.BlockSpec(memory_space=pltpu.VMEM)
SMEM = pl.BlockSpec(memory_space=pltpu.SMEM)


def call(kernel, outs, args, specs=(), scratch=()):
    return pl.pallas_call(
        kernel,
        out_shape=[jax.ShapeDtypeStruct(shape, dtype) for shape, dtype in outs],
        in_specs=list(specs) + [VMEM] * (len(args) - len(specs)),
        out_specs=[VMEM] * len(outs),
        scratch_shapes=list(scratch),
        compiler_params=pltpu.CompilerParams(vmem_limit_bytes=40 * 1024 * 1024),
    )(*args)


def halves(x):
    high = x.astype(BF16)
    return high, (x - high.astype(F32)).astype(BF16)


def dot_exact(x, selector):
    rows = x.shape[0]
    high, low = halves(x)
    both = jnp.dot(jnp.concatenate([high, low], 0), selector, preferred_element_type=F32)
    return both[:rows] + both[rows:]


def dot_across(x, matrix):
    return lax.dot_general(x, matrix, (((1,), (1,)), ((), ())), preferred_element_type=F32)


def dot_split(x, high_ref, low_ref):
    rows = x.shape[0]
    high, low = halves(x)
    both = jnp.dot(jnp.concatenate([high, low], 0), high_ref[...], preferred_element_type=F32)
    rest = jnp.dot(high, low_ref[...], preferred_element_type=F32)
    return both[:rows] + both[rows:] + rest


def face(x, f):
    return x[:, f * FD:(f + 1) * FD]


def take(x, row):
    index = jnp.broadcast_to(row.astype(jnp.int32), x.shape)
    return jnp.take_along_axis(x, index, axis=1, mode="promise_in_bounds")


def lower_changed(x, rows):
    parts = []
    for d in range(3):
        parts.append(-take(face(x, 2 * d), rows[d]))
        parts.append(face(x, 2 * d + 1))
    return jnp.concatenate(parts, axis=1)


def partner_rows(messages):
    return [m[CASES:CASES + 1, :] for m in messages]


def inverse_rows(messages):
    return [m[CASES + 1:CASES + 2, :] for m in messages]


def apply_dense(field, messages, high_ref, low_ref):
    loads = lower_changed(field, inverse_rows(messages))
    return loads, lower_changed(dot_split(loads, high_ref, low_ref), partner_rows(messages))


def position():
    gy = lax.axis_size("gy")
    places = [(lax.axis_index(a), lax.axis_size(a)) for a in ("gx", "gy", "gz")]
    there = []
    for place, size in places:
        there += [place > 0, place < size - 1]
    return places[0][0] * gy + places[1][0], places[2][0], there


def steps():
    gy = lax.axis_size("gy")
    return (-gy, gy, -1, 1)


def mask_row(there):
    return jnp.concatenate([jnp.full((1, FD), t.astype(F32)) for t in there], axis=1)


def put_rows(slots_ref, spot, rows):
    for q in range(4):
        slots_ref[spot, q] = rows[4 * q:4 * q + 4, :]


def take_rows(slots_ref, spot):
    return jnp.concatenate([slots_ref[spot, q] for q in range(4)], axis=0)


def target_rows(ids):
    lanes = lax.broadcasted_iota(jnp.int32, (8, FD), 1) % SUBS
    target = jnp.full((8, FD), -1, jnp.int32)
    for r in range(24):
        target = jnp.where(lanes == r, (r % 3) * QPAD + ids[0, 0, 0, r // 3], target)
    return target.astype(F32)


def prep_kernel(ids, rhs_ref, partner_ref, coupling_ref, *message_refs):
    _, _, there = position()
    target = target_rows(ids)
    for d in range(3):
        up_ref, down_ref = message_refs[d], message_refs[3 + d]
        row = partner_ref[0, 0, d, :, :]
        up_ref[0:CASES, :] = rhs_ref[d] * there[2 * d + 1].astype(F32)
        wanted = lax.broadcasted_iota(jnp.int32, (FD, FD), 0)
        hits = (wanted == jnp.broadcast_to(row, (FD, FD))).astype(F32).astype(BF16)
        count = lax.broadcasted_iota(jnp.int32, (16, FD), 1).astype(F32).astype(BF16)
        up_ref[CASES:CASES + 8, :] = jnp.zeros((8, FD), F32)
        up_ref[CASES:CASES + 1, :] = row.astype(F32)
        up_ref[CASES + 1:CASES + 2, :] = dot_across(count, hits)[0:1, :]
        up_ref[24:48, :] = coupling_ref[:, (2 * d + 1) * FD:(2 * d + 2) * FD]
        up_ref[48:56, :] = target
        down_ref[0:24, :] = coupling_ref[:, 2 * d * FD:(2 * d + 1) * FD]
        down_ref[24:32, :] = target


def put_dense(pairs, diag_ref, couple_ref, high_ref, low_ref):
    high_ref[...] = jnp.zeros_like(high_ref)
    low_ref[...] = jnp.zeros_like(low_ref)

    def put(rows, cols, block):
        high, low = halves(block)
        high_ref[pl.ds(rows, FD), pl.ds(cols, FD)] = high
        low_ref[pl.ds(rows, FD), pl.ds(cols, FD)] = low

    for f in range(6):
        put(f * FD, f * FD, diag_ref[f])
    for k in range(6):
        first = pl.multiple_of(pairs[0, 0, 0, 0, k] * FD, FD)
        second = pl.multiple_of(pairs[0, 0, 0, 1, k] * FD, FD)
        block = couple_ref[k]
        put(second, first, block)
        put(first, second, block.T)


def dense_kernel(pairs, diag_ref, couple_ref, high_ref, low_ref):
    put_dense(pairs, diag_ref, couple_ref, high_ref, low_ref)


def start_kernel(ux_ref, uy_ref, uz_ref, mx_ref, my_ref, mz_ref, dz_ref, dh_ref, dl_ref, field_ref,
                 shown_ref, down_ref, up_ref):
    own, messages = (ux_ref, uy_ref, uz_ref), (mx_ref, my_ref, mz_ref)
    parts = []
    for d in range(3):
        parts += [messages[d][0:CASES, :], own[d][0:CASES, :]]
    field = jnp.concatenate(parts, axis=1)
    field_ref[...] = field
    _, shown = apply_dense(field, messages, dh_ref, dl_ref)
    shown_ref[...] = shown
    down_ref[0:CASES, :] = face(shown, 4)
    down_ref[CASES:CASES + 32, :] = dz_ref[...]
    up_ref[...] = face(shown, 5)


def joint_kernel(ux_ref, uy_ref, uz_ref, mx_ref, my_ref, mz_ref, dx_ref, dy_ref, dz_ref, nx_ref, ny_ref,
                 over_ref, shown_ref, residual_ref, gh_ref, gl_ref, pick_ref, out_ref, pad):
    _, _, there = position()
    own, messages, lower = (ux_ref, uy_ref, uz_ref), (mx_ref, my_ref, mz_ref), (dx_ref, dy_ref, dz_ref)
    above = (nx_ref[...], ny_ref[...], over_ref[CASES:CASES + 32, :])
    pad[...] = jnp.zeros_like(pad)
    targets = [own[0][48:56, :]]
    for d in range(3):
        row = own[d][CASES:CASES + 1, :]
        low, high = slice(2 * d * FD, (2 * d + 1) * FD), slice((2 * d + 1) * FD, (2 * d + 2) * FD)
        pad[0:24, low] = -take(lower[d][0:24, :], messages[d][CASES:CASES + 1, :])
        pad[0:24, high] = own[d][24:48, :]
        sides = (
            (low, messages[d][24:48, :], messages[d][48:56, :]),
            (high, -take(above[d][0:24, :], row), above[d][24:32, :]),
        )
        for f, (lanes, rows, target) in zip((2 * d, 2 * d + 1), sides):
            exists = there[f].astype(F32)
            pad[SUBS * (f + 1):SUBS * (f + 1) + 24, lanes] = rows * exists
            targets.append(target * exists)
    high, low = halves(pad[...])
    gh_ref[...] = high
    gl_ref[...] = low
    lanes = lax.broadcasted_iota(jnp.int32, (8, FD), 1)
    rows = lax.broadcasted_iota(jnp.int32, (3 * QPAD, FD), 0)
    for half in range(2):
        wanted = jnp.full((8, FD), -1.0, F32)
        for n in range(4 * half, min(4 * half + 4, 7)):
            wanted = jnp.where(lanes // SUBS == n % 4, targets[n], wanted)
        wanted = jnp.broadcast_to(wanted[0:1, :].astype(jnp.int32), (3 * QPAD, FD))
        pick_ref[:, half * FD:(half + 1) * FD] = (rows == wanted).astype(F32).astype(BF16)
    sum_kernel(shown_ref, residual_ref, gh_ref, gl_ref, pick_ref, out_ref)


def late_kernel(pairs, diag_ref, couple_ref, inverse_ref, _, fh_ref, fl_ref, kh_ref, kl_ref, square):
    put_dense(pairs, diag_ref, couple_ref, fh_ref, fl_ref)
    square[...] = jnp.zeros_like(square)
    for p in range(3):
        for q in range(3):
            square[p * QPAD:p * QPAD + 192, q * QPAD:q * QPAD + 192] = inverse_ref[
                p * 192:(p + 1) * 192, q * 192:(q + 1) * 192
            ]
    high, low = halves(square[...])
    kh_ref[...] = high
    kl_ref[...] = low


def face_sum(x, faces=range(6)):
    total = None
    for f in faces:
        total = face(x, f) if total is None else total + face(x, f)
    return total


def put_payload(out_ref, gathered, extras):
    lanes = lax.broadcasted_iota(jnp.int32, (CASES, FD), 1)
    for b in range(6):
        block = face(gathered, b)
        if b == 1:
            for t, value in enumerate(extras):
                block = jnp.where(lanes == 64 + t, value, block)
        for c in range(CASES):
            out_ref[2 * c + b // 3, 4, b % 3:b % 3 + 1, :] = block[c:c + 1, :]


def sum_kernel(shown_ref, residual_ref, gh_ref, gl_ref, pick_ref, out_ref):
    here, _, there = position()
    shown = shown_ref[...]
    share = 0.25 * shown * mask_row(there)
    high, low = halves(share)
    both = dot_across(jnp.concatenate([high, low], 0), gh_ref[...])
    corner = both[:CASES] + both[CASES:] + dot_across(high, gl_ref[...])
    high, low = halves(corner)
    both = dot_across(jnp.concatenate([high, low], 0), pick_ref[...])
    norm = jnp.sum(face_sum(share * residual_ref[...]), axis=1, keepdims=True)
    out_ref[...] = jnp.zeros_like(out_ref)
    put_payload(out_ref, both[:CASES] + both[CASES:], [norm])
    for f, by in enumerate(steps()):
        @pl.when(there[f])
        def _():
            put_rows(out_ref, here + by, face(shown, f))


def put_layers(out_ref, total, flexed_ref, layer, there):
    out_ref[...] = jnp.zeros_like(out_ref)
    for i in range(out_ref.shape[0]):
        out_ref[i, 4] = total
    for f, by in ((4, -1), (5, 1)):
        @pl.when(there[f])
        def _():
            put_rows(out_ref, layer + by, flexed_ref[:, f * FD:(f + 1) * FD])


def flex_kernel(first, mx_ref, my_ref, mz_ref, shown_ref, slots_ref, below_ref, above_ref, fh_ref,
                fl_ref, *rest):
    rest = list(rest)
    if not first:
        search_ref, applied_ref = rest[:2]
        rest = rest[2:]
    z_ref, flexed_ref, out_ref, turn = rest
    here, layer, there = position()
    across = []
    for f, by in enumerate(steps()):
        across.append(take_rows(slots_ref, jnp.where(there[f], here + by, here)))
    across += [below_ref[...], above_ref[0:CASES, :]]
    z = 0.25 * (shown_ref[...] + jnp.concatenate(across, axis=1)) * mask_row(there)
    z_ref[...] = z
    _, flexed = apply_dense(z, (mx_ref, my_ref, mz_ref), fh_ref, fl_ref)
    flexed_ref[...] = flexed
    turn[...] = jnp.zeros_like(turn)
    turn[0:CASES, :] = face_sum(z * flexed)
    if not first:
        turn[CASES:2 * CASES, :] = (
            face_sum(z * applied_ref[...], (1, 3, 5)) + face_sum(search_ref[...] * flexed)
        )
    sums = jnp.sum(turn[...].T, axis=0, keepdims=True)
    total = jnp.sum(slots_ref[:, 4], axis=0)
    rows = lax.broadcasted_iota(jnp.int32, total.shape, 0)
    total = jnp.where(rows == 3, jnp.broadcast_to(sums, total.shape), total)
    put_layers(out_ref, total, flexed_ref, layer, there)


def share_kernel(layers_ref, flexed_ref, out_ref):
    here, _, there = position()
    total = jnp.sum(layers_ref[:, 4], axis=0)
    out_ref[...] = jnp.zeros_like(out_ref)
    for i in range(out_ref.shape[0]):
        out_ref[i, 4] = total
    for f, by in enumerate(steps()):
        @pl.when(there[f])
        def _():
            put_rows(out_ref, here + by, flexed_ref[:, f * FD:(f + 1) * FD])


def step_kernel(first, last, slots_ref, layers_ref, flexed_ref, z_ref,
                residual_ref, kh_ref, kl_ref, gh_ref, gl_ref, pick_ref, *rest):
    rest, whole = list(rest[:-1]), rest[-1]
    if not last:
        mx_ref, my_ref, mz_ref, dh_ref, dl_ref = rest[:5]
        rest = rest[5:]
    if not first:
        search_ref, applied_ref, load_ref, scale_ref, iterate_ref = rest[:5]
        rest = rest[5:]
    here, layer, there = position()
    across = []
    for f, by in enumerate(steps()):
        across.append(take_rows(slots_ref, jnp.where(there[f], here + by, here)))
    for f, by in ((4, -1), (5, 1)):
        across.append(take_rows(layers_ref, jnp.where(there[f], layer + by, layer)))
    mask = mask_row(there)
    applied = (flexed_ref[...] + jnp.concatenate(across, axis=1)) * mask
    search = z_ref[...]
    for c in range(CASES):
        for b in range(6):
            row = slice(b % 3, b % 3 + 1)
            whole[c:c + 1, b * FD:(b + 1) * FD] = slots_ref[2 * c + b // 3, 4, row, :]
    load = whole[...]
    norm = load[:, FD + 64:FD + 65]
    sums = jnp.sum(slots_ref[:, 4], axis=0)[3:4, :]
    sums = jnp.broadcast_to(sums, (FD, FD)).T
    energy, cross = sums[0:CASES, 0:1], sums[CASES:2 * CASES, 0:1]
    lanes = lax.broadcasted_iota(jnp.int32, load.shape, 1) % QPAD
    load = jnp.where(lanes < 192, load, 0.0)
    if not first:
        beta = norm / scale_ref[:, 0:1]
        energy = energy + beta * cross + beta * beta * scale_ref[:, 1:2]
        applied = applied + beta * applied_ref[...]
        search = search + beta * search_ref[...]
        load = load + beta * load_ref[...]
    coarse = dot_split(load, kh_ref, kl_ref)
    step = norm / (energy + jnp.sum(load * coarse, axis=1, keepdims=True))
    corner = dot_exact(coarse, pick_ref[...])
    correction = dot_split(corner, gh_ref, gl_ref) * mask
    residual = residual_ref[...] - step * (applied + correction)
    moved = step * search
    if last:
        multipliers_ref, left_ref = rest
        for d in range(3):
            multipliers_ref[d] = iterate_ref[d] + face(moved, 2 * d + 1)
            left_ref[d] = face(residual, 2 * d + 1)
        return
    search_out, applied_out, load_out, scale_out, iterate_out, residual_out, shown_ref = rest[:7]
    down_ref, up_ref = rest[7:]
    search_out[...] = search
    applied_out[...] = applied
    load_out[...] = load
    residual_out[...] = residual
    lanes = lax.broadcasted_iota(jnp.int32, (CASES, FD), 1)
    scale_out[...] = jnp.where(lanes == 0, norm, energy)
    for d in range(3):
        moved_face = face(moved, 2 * d + 1)
        iterate_out[d] = moved_face if first else iterate_ref[d] + moved_face
    _, shown = apply_dense(residual, (mx_ref, my_ref, mz_ref), dh_ref, dl_ref)
    shown_ref[...] = shown
    down_ref[...] = face(shown, 4)
    up_ref[...] = face(shown, 5)


def passed_along(shard, axis, by):
    peers = lax.axis_size(axis)
    pairs = [(i, i + by) for i in range(peers) if 0 <= i + by < peers]
    return lax.ppermute(shard, axis, pairs)


def swapped(slots, axes):
    return lax.all_to_all(slots, axes, 0, 0)


def body(
    jump_rhs,
    flex_diag,
    flex_couple,
    dirichlet_diag,
    dirichlet_couple,
    face_pairs,
    corner_coupling,
    coarse_ids,
    partner,
    coarse_inverse,
):
    gx, gy, gz = (lax.axis_size(a) for a in AXES)
    plane = gx * gy
    rhs = jump_rhs.reshape(3, CASES, FD)
    coupling = corner_coupling.reshape(24, WIDE)
    square = (WIDE, WIDE)
    wide = (CASES, WIDE)

    *ups, dx, dy, dz = call(
        prep_kernel, [((56, FD), F32)] * 3 + [((32, FD), F32)] * 3,
        [coarse_ids, rhs, jnp.swapaxes(partner, 2, 3), coupling], specs=[SMEM],
    )
    messages = [passed_along(m, a, 1) for m, a in zip(ups, AXES)]
    above = [passed_along(m, a, -1) for m, a in zip((dx, dy), AXES)]
    pairs = jnp.swapaxes(face_pairs, 3, 4)
    blocks = [b.reshape(6, FD, FD) for b in (dirichlet_diag, dirichlet_couple, flex_diag, flex_couple)]
    dirichlet = call(
        dense_kernel, [(square, BF16)] * 2, [pairs] + blocks[:2], specs=[SMEM]
    )
    residual, shown, down, up = call(
        start_kernel,
        [(wide, F32)] * 2 + [((CASES + 32, FD), F32), ((CASES, FD), F32)],
        [*ups, *messages, dz, *dirichlet],
    )
    stacked = (plane, 5, 4, FD)

    kept = []
    for iteration in range(ITERS):
        first, last = iteration == 0, iteration + 1 == ITERS
        below = passed_along(up, "gz", 1)
        over = passed_along(down, "gz", -1)
        if first:
            *joint, slots = call(
                joint_kernel,
                [((QPAD, WIDE), BF16)] * 2 + [((3 * QPAD, QPAD), BF16), (stacked, F32)],
                [*ups, *messages, dx, dy, dz, *above, over, shown, residual],
                scratch=[pltpu.VMEM((QPAD, WIDE), F32)],
            )
        else:
            (slots,) = call(sum_kernel, [(stacked, F32)], [shown, residual, *joint])
        slots, below, over = lax.optimization_barrier((slots, below, over))
        slots = swapped(slots, PLANE)
        if first:
            late = call(
                late_kernel, [(square, BF16)] * 4,
                [pairs] + blocks[2:] + [coarse_inverse, slots],
                specs=[SMEM] + [VMEM] * 3 + [pl.BlockSpec(memory_space=pl.ANY)],
                scratch=[pltpu.VMEM(square, F32)],
            )
            flex, inverse = late[:2], late[2:]
        z, flexed, layers = call(
            functools.partial(flex_kernel, first),
            [(wide, F32), (wide, F32), ((gz, 5, 4, FD), F32)],
            [*messages, shown, slots, below, over, *flex, *kept[:2]],
            scratch=[pltpu.VMEM((FD, FD), F32)],
        )
        layers = swapped(layers, "gz")
        (slots,) = call(share_kernel, [(stacked, F32)], [layers, flexed])
        slots = swapped(slots, PLANE)
        common = [slots, layers, flexed, z, residual, *inverse, *joint]
        kernel = functools.partial(step_kernel, first, last)
        scratch = [pltpu.VMEM(wide, F32)]
        if last:
            multipliers, left = call(
                kernel, [((3, CASES, FD), F32)] * 2, common + kept, scratch=scratch
            )
            break
        *kept, residual, shown, down, up = call(
            kernel,
            [(wide, F32)] * 3 + [((CASES, FD), F32), ((3, CASES, FD), F32), (wide, F32), (wide, F32)]
            + [((CASES, FD), F32)] * 2,
            common + [*messages, *dirichlet] + kept, scratch=scratch,
        )
    return multipliers.reshape(jump_rhs.shape), left.reshape(jump_rhs.shape)


def solution(mesh):
    placed = (
        P("gx", "gy", "gz", None, None, None),
        P("gx", "gy", "gz", None, None, None),
        P("gx", "gy", "gz", None, None, None),
        P("gx", "gy", "gz", None, None, None),
        P("gx", "gy", "gz", None, None, None),
        P("gx", "gy", "gz", None, None),
        P("gx", "gy", "gz", None, None),
        P("gx", "gy", "gz", None),
        P("gx", "gy", "gz", None, None),
        P(),
    )
    return jax.shard_map(
        body,
        mesh=mesh,
        in_specs=placed,
        out_specs=(P("gx", "gy", "gz", None, None, None), P("gx", "gy", "gz", None, None, None)),
        check_vma=False,
    )
```

```python
import functools

import jax
import jax.numpy as jnp
from jax import lax
from jax.experimental import pallas as pl
from jax.experimental.pallas import tpu as pltpu
from jax.sharding import PartitionSpec as P

ITERS = 3
CASES = 16
FD = 128
WIDE = 6 * FD
QPAD = 256
SUBS = 32
AXES = ("gx", "gy", "gz")
PLANE = ("gx", "gy")
F32 = jnp.float32
BF16 = jnp.bfloat16
VMEM = pl.BlockSpec(memory_space=pltpu.VMEM)
SMEM = pl.BlockSpec(memory_space=pltpu.SMEM)


def call(kernel, outs, args, specs=(), scratch=()):
    return pl.pallas_call(
        kernel,
        out_shape=[jax.ShapeDtypeStruct(shape, dtype) for shape, dtype in outs],
        in_specs=list(specs) + [VMEM] * (len(args) - len(specs)),
        out_specs=[VMEM] * len(outs),
        scratch_shapes=list(scratch),
        compiler_params=pltpu.CompilerParams(vmem_limit_bytes=40 * 1024 * 1024),
    )(*args)


def halves(x):
    high = x.astype(BF16)
    return high, (x - high.astype(F32)).astype(BF16)


def dot_exact(x, selector):
    rows = x.shape[0]
    high, low = halves(x)
    both = jnp.dot(jnp.concatenate([high, low], 0), selector, preferred_element_type=F32)
    return both[:rows] + both[rows:]


def dot_across(x, matrix):
    return lax.dot_general(x, matrix, (((1,), (1,)), ((), ())), preferred_element_type=F32)


def dot_split(x, high_ref, low_ref):
    rows = x.shape[0]
    high, low = halves(x)
    both = jnp.dot(jnp.concatenate([high, low], 0), high_ref[...], preferred_element_type=F32)
    rest = jnp.dot(high, low_ref[...], preferred_element_type=F32)
    return both[:rows] + both[rows:] + rest


def face(x, f):
    return x[:, f * FD:(f + 1) * FD]


def take(x, row):
    index = jnp.broadcast_to(row.astype(jnp.int32), x.shape)
    return jnp.take_along_axis(x, index, axis=1, mode="promise_in_bounds")


def lower_changed(x, rows):
    parts = []
    for d in range(3):
        parts.append(-take(face(x, 2 * d), rows[d]))
        parts.append(face(x, 2 * d + 1))
    return jnp.concatenate(parts, axis=1)


RESIDUAL, SHOWN, SEARCH, APPLIED, LOAD, REST = (slice(CASES * i, CASES * (i + 1)) for i in range(6))
ORDERS = 6 * CASES
STATE = (ORDERS + 8, WIDE)


def apply_dense(field, state_ref, high_ref, low_ref):
    orders = state_ref[ORDERS:ORDERS + 8, :]
    partner = [face(orders[0:1, :], d) for d in range(3)]
    inverse = [face(orders[1:2, :], d) for d in range(3)]
    loads = lower_changed(field, inverse)
    return lower_changed(dot_split(loads, high_ref, low_ref), partner)


def position():
    gy = lax.axis_size("gy")
    places = [(lax.axis_index(a), lax.axis_size(a)) for a in ("gx", "gy", "gz")]
    there = []
    for place, size in places:
        there += [place > 0, place < size - 1]
    return places[0][0] * gy + places[1][0], places[2][0], there


def steps():
    gy = lax.axis_size("gy")
    return (-gy, gy, -1, 1)


def mask_row(there):
    return jnp.concatenate([jnp.full((1, FD), t.astype(F32)) for t in there], axis=1)


def put_rows(slots_ref, spot, rows):
    for q in range(4):
        slots_ref[spot, q] = rows[4 * q:4 * q + 4, :]


def take_rows(slots_ref, spot):
    return jnp.concatenate([slots_ref[spot, q] for q in range(4)], axis=0)


def target_rows(ids_row):
    row = lax.broadcasted_iota(jnp.int32, (8, FD), 1) % SUBS
    ids = take(jnp.broadcast_to(ids_row.astype(F32), (8, FD)), jnp.minimum(row // 3, 7))
    return jnp.where(row < 24, ids + (row % 3 * QPAD).astype(F32), -1.0)


def prep_kernel(table_ref, rhs_ref, coupling_ref, *message_refs):
    _, _, there = position()
    target = target_rows(table_ref[0, 0, 3])
    for d in range(3):
        up_ref, down_ref = message_refs[d], message_refs[3 + d]
        row = table_ref[0, 0, d]
        up_ref[0:CASES, :] = rhs_ref[d] * there[2 * d + 1].astype(F32)
        wanted = lax.broadcasted_iota(jnp.int32, (FD, FD), 0)
        hits = (wanted == jnp.broadcast_to(row, (FD, FD))).astype(F32).astype(BF16)
        count = lax.broadcasted_iota(jnp.int32, (16, FD), 1).astype(F32).astype(BF16)
        up_ref[CASES:CASES + 8, :] = jnp.zeros((8, FD), F32)
        up_ref[CASES:CASES + 1, :] = row.astype(F32)
        up_ref[CASES + 1:CASES + 2, :] = dot_across(count, hits)[0:1, :]
        up_ref[24:48, :] = coupling_ref[:, (2 * d + 1) * FD:(2 * d + 2) * FD]
        up_ref[48:56, :] = target
        down_ref[0:24, :] = coupling_ref[:, 2 * d * FD:(2 * d + 1) * FD]
        down_ref[24:32, :] = target


def put_dense(table, diag_ref, couple_ref, high_ref, low_ref):
    high_ref[...] = jnp.zeros_like(high_ref)
    low_ref[...] = jnp.zeros_like(low_ref)

    def put(rows, cols, block):
        high, low = halves(block)
        high_ref[pl.ds(rows, FD), pl.ds(cols, FD)] = high
        low_ref[pl.ds(rows, FD), pl.ds(cols, FD)] = low

    for f in range(6):
        put(f * FD, f * FD, diag_ref[f])
    for k in range(6):
        first = pl.multiple_of(table[0, 0, 4, 0, k] * FD, FD)
        second = pl.multiple_of(table[0, 0, 5, 0, k] * FD, FD)
        block = couple_ref[k]
        put(second, first, block)
        put(first, second, block.T)


def dense_kernel(table, diag_ref, couple_ref, high_ref, low_ref):
    put_dense(table, diag_ref, couple_ref, high_ref, low_ref)


def start_kernel(ux_ref, uy_ref, uz_ref, mx_ref, my_ref, mz_ref, dz_ref, dh_ref, dl_ref, state_ref,
                 down_ref, up_ref):
    own, messages = (ux_ref, uy_ref, uz_ref), (mx_ref, my_ref, mz_ref)
    state_ref[...] = jnp.zeros_like(state_ref)
    parts = []
    for d in range(3):
        parts += [messages[d][0:CASES, :], own[d][0:CASES, :]]
        state_ref[ORDERS:ORDERS + 8, d * FD:(d + 1) * FD] = messages[d][CASES:CASES + 8, :]
    field = jnp.concatenate(parts, axis=1)
    state_ref[RESIDUAL, :] = field
    shown = apply_dense(field, state_ref, dh_ref, dl_ref)
    state_ref[SHOWN, :] = shown
    down_ref[0:CASES, :] = face(shown, 4)
    down_ref[CASES:CASES + 32, :] = dz_ref[...]
    up_ref[...] = face(shown, 5)


def joint_kernel(ux_ref, uy_ref, uz_ref, mx_ref, my_ref, mz_ref, dx_ref, dy_ref, dz_ref, nx_ref, ny_ref,
                 over_ref, state_ref, gh_ref, gl_ref, pick_ref, out_ref, pad):
    _, _, there = position()
    own, messages, lower = (ux_ref, uy_ref, uz_ref), (mx_ref, my_ref, mz_ref), (dx_ref, dy_ref, dz_ref)
    above = (nx_ref[...], ny_ref[...], over_ref[CASES:CASES + 32, :])
    pad[...] = jnp.zeros_like(pad)
    targets = [own[0][48:56, :]]
    for d in range(3):
        row = own[d][CASES:CASES + 1, :]
        low, high = slice(2 * d * FD, (2 * d + 1) * FD), slice((2 * d + 1) * FD, (2 * d + 2) * FD)
        pad[0:24, low] = -take(lower[d][0:24, :], messages[d][CASES:CASES + 1, :])
        pad[0:24, high] = own[d][24:48, :]
        sides = (
            (low, messages[d][24:48, :], messages[d][48:56, :]),
            (high, -take(above[d][0:24, :], row), above[d][24:32, :]),
        )
        for f, (lanes, rows, target) in zip((2 * d, 2 * d + 1), sides):
            exists = there[f].astype(F32)
            pad[SUBS * (f + 1):SUBS * (f + 1) + 24, lanes] = rows * exists
            targets.append(target * exists)
    high, low = halves(pad[...])
    gh_ref[...] = high
    gl_ref[...] = low
    lanes = lax.broadcasted_iota(jnp.int32, (8, FD), 1)
    rows = lax.broadcasted_iota(jnp.int32, (3 * QPAD, FD), 0)
    for half in range(2):
        wanted = jnp.full((8, FD), -1.0, F32)
        for n in range(4 * half, min(4 * half + 4, 7)):
            wanted = jnp.where(lanes // SUBS == n % 4, targets[n], wanted)
        wanted = jnp.broadcast_to(wanted[0:1, :].astype(jnp.int32), (3 * QPAD, FD))
        pick_ref[:, half * FD:(half + 1) * FD] = (rows == wanted).astype(F32).astype(BF16)
    sum_kernel(state_ref, gh_ref, gl_ref, pick_ref, out_ref)


def late_kernel(table, diag_ref, couple_ref, inverse_ref, _, fh_ref, fl_ref, kh_ref, kl_ref, square):
    put_dense(table, diag_ref, couple_ref, fh_ref, fl_ref)
    square[...] = jnp.zeros_like(square)
    for p in range(3):
        for q in range(3):
            square[p * QPAD:p * QPAD + 192, q * QPAD:q * QPAD + 192] = inverse_ref[
                p * 192:(p + 1) * 192, q * 192:(q + 1) * 192
            ]
    high, low = halves(square[...])
    kh_ref[...] = high
    kl_ref[...] = low


def face_sum(x, faces=range(6)):
    total = None
    for f in faces:
        total = face(x, f) if total is None else total + face(x, f)
    return total


def put_payload(out_ref, gathered, extras):
    lanes = lax.broadcasted_iota(jnp.int32, (CASES, FD), 1)
    for b in range(6):
        block = face(gathered, b)
        if b == 1:
            for t, value in enumerate(extras):
                block = jnp.where(lanes == 64 + t, value, block)
        for c in range(CASES):
            out_ref[2 * c + b // 3, 4, b % 3:b % 3 + 1, :] = block[c:c + 1, :]


def sum_kernel(state_ref, gh_ref, gl_ref, pick_ref, out_ref):
    here, _, there = position()
    shown = state_ref[SHOWN, :]
    share = 0.25 * shown * mask_row(there)
    high, low = halves(share)
    both = dot_across(jnp.concatenate([high, low], 0), gh_ref[...])
    corner = both[:CASES] + both[CASES:] + dot_across(high, gl_ref[...])
    high, low = halves(corner)
    both = dot_across(jnp.concatenate([high, low], 0), pick_ref[...])
    norm = jnp.sum(face_sum(share * state_ref[RESIDUAL, :]), axis=1, keepdims=True)
    out_ref[...] = jnp.zeros_like(out_ref)
    put_payload(out_ref, both[:CASES] + both[CASES:], [norm])
    for f, by in enumerate(steps()):
        @pl.when(there[f])
        def _():
            put_rows(out_ref, here + by, face(shown, f))


def put_layers(out_ref, total, flexed_ref, layer, there):
    out_ref[...] = jnp.zeros_like(out_ref)
    for i in range(out_ref.shape[0]):
        out_ref[i, 4] = total
    for f, by in ((4, -1), (5, 1)):
        @pl.when(there[f])
        def _():
            put_rows(out_ref, layer + by, flexed_ref[:, f * FD:(f + 1) * FD])


def flex_kernel(first, state_ref, slots_ref, below_ref, above_ref, fh_ref, fl_ref, z_ref, flexed_ref,
                out_ref, turn):
    here, layer, there = position()
    across = []
    for f, by in enumerate(steps()):
        across.append(take_rows(slots_ref, jnp.where(there[f], here + by, here)))
    across += [below_ref[...], above_ref[0:CASES, :]]
    z = 0.25 * (state_ref[SHOWN, :] + jnp.concatenate(across, axis=1)) * mask_row(there)
    z_ref[...] = z
    flexed = apply_dense(z, state_ref, fh_ref, fl_ref)
    flexed_ref[...] = flexed
    turn[...] = jnp.zeros_like(turn)
    turn[0:CASES, :] = face_sum(z * flexed)
    if not first:
        turn[CASES:2 * CASES, :] = (
            face_sum(z * state_ref[APPLIED, :], (1, 3, 5))
            + face_sum(state_ref[SEARCH, :] * flexed)
        )
    sums = jnp.sum(turn[...].T, axis=0, keepdims=True)
    total = jnp.sum(slots_ref[:, 4], axis=0)
    rows = lax.broadcasted_iota(jnp.int32, total.shape, 0)
    total = jnp.where(rows == 3, jnp.broadcast_to(sums, total.shape), total)
    put_layers(out_ref, total, flexed_ref, layer, there)


def share_kernel(layers_ref, flexed_ref, out_ref):
    here, _, there = position()
    total = jnp.sum(layers_ref[:, 4], axis=0)
    out_ref[...] = jnp.zeros_like(out_ref)
    for i in range(out_ref.shape[0]):
        out_ref[i, 4] = total
    for f, by in enumerate(steps()):
        @pl.when(there[f])
        def _():
            put_rows(out_ref, here + by, flexed_ref[:, f * FD:(f + 1) * FD])


def step_kernel(first, last, slots_ref, layers_ref, flexed_ref, z_ref, state_ref, kh_ref, kl_ref,
                gh_ref, gl_ref, pick_ref, *rest):
    rest, whole = rest[:-1], rest[-1]
    here, layer, there = position()
    across = []
    for f, by in enumerate(steps()):
        across.append(take_rows(slots_ref, jnp.where(there[f], here + by, here)))
    for f, by in ((4, -1), (5, 1)):
        across.append(take_rows(layers_ref, jnp.where(there[f], layer + by, layer)))
    mask = mask_row(there)
    applied = (flexed_ref[...] + jnp.concatenate(across, axis=1)) * mask
    search = z_ref[...]
    for c in range(CASES):
        for b in range(6):
            row = slice(b % 3, b % 3 + 1)
            whole[c:c + 1, b * FD:(b + 1) * FD] = slots_ref[2 * c + b // 3, 4, row, :]
    load = whole[...]
    norm = load[:, FD + 64:FD + 65]
    sums = jnp.sum(slots_ref[:, 4], axis=0)[3:4, :]
    sums = jnp.broadcast_to(sums, (FD, FD)).T
    energy, cross = sums[0:CASES, 0:1], sums[CASES:2 * CASES, 0:1]
    lanes = lax.broadcasted_iota(jnp.int32, load.shape, 1) % QPAD
    load = jnp.where(lanes < 192, load, 0.0)
    if not first:
        scale = state_ref[REST, 0:FD]
        beta = norm / scale[:, 0:1]
        energy = energy + beta * cross + beta * beta * scale[:, 1:2]
        applied = applied + beta * state_ref[APPLIED, :]
        search = search + beta * state_ref[SEARCH, :]
        load = load + beta * state_ref[LOAD, :]
    coarse = dot_split(load, kh_ref, kl_ref)
    step = norm / (energy + jnp.sum(load * coarse, axis=1, keepdims=True))
    corner = dot_exact(coarse, pick_ref[...])
    correction = dot_split(corner, gh_ref, gl_ref) * mask
    residual = state_ref[RESIDUAL, :] - step * (applied + correction)
    moved = step * search
    if last:
        multipliers_ref, left_ref = rest
        for d in range(3):
            before = state_ref[REST, (d + 1) * FD:(d + 2) * FD]
            multipliers_ref[d] = before + face(moved, 2 * d + 1)
            left_ref[d] = face(residual, 2 * d + 1)
        return
    dh_ref, dl_ref, new_ref, down_ref, up_ref = rest
    new_ref[RESIDUAL, :] = residual
    shown = apply_dense(residual, state_ref, dh_ref, dl_ref)
    new_ref[SHOWN, :] = shown
    down_ref[...] = face(shown, 4)
    up_ref[...] = face(shown, 5)
    new_ref[SEARCH, :] = search
    new_ref[APPLIED, :] = applied
    new_ref[LOAD, :] = load
    lanes = lax.broadcasted_iota(jnp.int32, (CASES, FD), 1)
    scale = jnp.where(lanes == 0, norm, energy)
    parts = [scale]
    for d in range(3):
        parts.append(state_ref[REST, (d + 1) * FD:(d + 2) * FD] + face(moved, 2 * d + 1))
    new_ref[REST, :] = jnp.concatenate(parts + [scale, scale], axis=1)
    new_ref[ORDERS:ORDERS + 8, :] = state_ref[ORDERS:ORDERS + 8, :]


def passed_along(shard, axis, by):
    peers = lax.axis_size(axis)
    pairs = [(i, i + by) for i in range(peers) if 0 <= i + by < peers]
    return lax.ppermute(shard, axis, pairs)


def swapped(slots, axes):
    return lax.all_to_all(slots, axes, 0, 0)


def body(
    jump_rhs,
    flex_diag,
    flex_couple,
    dirichlet_diag,
    dirichlet_couple,
    face_pairs,
    corner_coupling,
    coarse_ids,
    partner,
    coarse_inverse,
):
    gx, gy, gz = (lax.axis_size(a) for a in AXES)
    plane = gx * gy
    rhs = jump_rhs.reshape(3, CASES, FD)
    coupling = corner_coupling.reshape(24, WIDE)
    square = (WIDE, WIDE)
    wide = (CASES, WIDE)

    width = ((0, 0),) * 4
    table = jnp.concatenate(
        [
            jnp.swapaxes(partner, 2, 3),
            jnp.pad(coarse_ids[:, :, :, None, :], width + ((0, FD - 8),)),
            jnp.pad(jnp.transpose(face_pairs, (0, 1, 4, 2, 3)), width + ((0, FD - 6),)),
        ],
        axis=2,
    )
    *ups, dx, dy, dz = call(
        prep_kernel, [((56, FD), F32)] * 3 + [((32, FD), F32)] * 3,
        [table, rhs, coupling],
    )
    messages = [passed_along(m, a, 1) for m, a in zip(ups, AXES)]
    above = [passed_along(m, a, -1) for m, a in zip((dx, dy), AXES)]
    blocks = [b.reshape(6, FD, FD) for b in (dirichlet_diag, dirichlet_couple, flex_diag, flex_couple)]
    dirichlet = call(
        dense_kernel, [(square, BF16)] * 2, [table] + blocks[:2], specs=[SMEM]
    )
    state, down, up = call(
        start_kernel,
        [(STATE, F32), ((CASES + 32, FD), F32), ((CASES, FD), F32)],
        [*ups, *messages, dz, *dirichlet],
    )
    stacked = (plane, 5, 4, FD)

    for iteration in range(ITERS):
        first, last = iteration == 0, iteration + 1 == ITERS
        below = passed_along(up, "gz", 1)
        over = passed_along(down, "gz", -1)
        if first:
            *joint, slots = call(
                joint_kernel,
                [((QPAD, WIDE), BF16)] * 2 + [((3 * QPAD, QPAD), BF16), (stacked, F32)],
                [*ups, *messages, dx, dy, dz, *above, over, state],
                scratch=[pltpu.VMEM((QPAD, WIDE), F32)],
            )
        else:
            (slots,) = call(sum_kernel, [(stacked, F32)], [state, *joint])
        slots, below, over = lax.optimization_barrier((slots, below, over))
        slots = swapped(slots, PLANE)
        if first:
            late = call(
                late_kernel, [(square, BF16)] * 4,
                [table] + blocks[2:] + [coarse_inverse, slots],
                specs=[SMEM] + [VMEM] * 3 + [pl.BlockSpec(memory_space=pl.ANY)],
                scratch=[pltpu.VMEM(square, F32)],
            )
            flex, inverse = late[:2], late[2:]
        z, flexed, layers = call(
            functools.partial(flex_kernel, first),
            [(wide, F32), (wide, F32), ((gz, 5, 4, FD), F32)],
            [state, slots, below, over, *flex],
            scratch=[pltpu.VMEM((FD, FD), F32)],
        )
        layers = swapped(layers, "gz")
        (slots,) = call(share_kernel, [(stacked, F32)], [layers, flexed])
        slots = swapped(slots, PLANE)
        common = [slots, layers, flexed, z, state, *inverse, *joint]
        kernel = functools.partial(step_kernel, first, last)
        scratch = [pltpu.VMEM(wide, F32)]
        if last:
            multipliers, left = call(kernel, [((3, CASES, FD), F32)] * 2, common, scratch=scratch)
            break
        state, down, up = call(
            kernel, [(STATE, F32)] + [((CASES, FD), F32)] * 2, common + [*dirichlet], scratch=scratch
        )
    return multipliers.reshape(jump_rhs.shape), left.reshape(jump_rhs.shape)


def solution(mesh):
    placed = (
        P("gx", "gy", "gz", None, None, None),
        P("gx", "gy", "gz", None, None, None),
        P("gx", "gy", "gz", None, None, None),
        P("gx", "gy", "gz", None, None, None),
        P("gx", "gy", "gz", None, None, None),
        P("gx", "gy", "gz", None, None),
        P("gx", "gy", "gz", None, None),
        P("gx", "gy", "gz", None),
        P("gx", "gy", "gz", None, None),
        P(),
    )
    return jax.shard_map(
        body,
        mesh=mesh,
        in_specs=placed,
        out_specs=(P("gx", "gy", "gz", None, None, None), P("gx", "gy", "gz", None, None, None)),
        check_vma=False,
    )
```

```python
import functools

import jax
import jax.numpy as jnp
from jax import lax
from jax.experimental import pallas as pl
from jax.experimental.pallas import tpu as pltpu
from jax.sharding import PartitionSpec as P

ITERS = 3
CASES = 16
FD = 128
WIDE = 6 * FD
AGGREGATES = 192
COARSE = 640
SUBS = 32
CORNERS = 256
AXES = ("gx", "gy", "gz")
PLANE = ("gx", "gy")
F32 = jnp.float32
BF16 = jnp.bfloat16
VMEM = pl.BlockSpec(memory_space=pltpu.VMEM)
SMEM = pl.BlockSpec(memory_space=pltpu.SMEM)


def call(kernel, outs, args, specs=(), scratch=()):
    return pl.pallas_call(
        kernel,
        out_shape=[jax.ShapeDtypeStruct(shape, dtype) for shape, dtype in outs],
        in_specs=list(specs) + [VMEM] * (len(args) - len(specs)),
        out_specs=[VMEM] * len(outs),
        scratch_shapes=list(scratch),
        compiler_params=pltpu.CompilerParams(vmem_limit_bytes=40 * 1024 * 1024),
    )(*args)


def halves(x):
    high = x.astype(BF16)
    return high, (x - high.astype(F32)).astype(BF16)


def dot_exact(x, selector):
    rows = x.shape[0]
    high, low = halves(x)
    both = jnp.dot(jnp.concatenate([high, low], 0), selector, preferred_element_type=F32)
    return both[:rows] + both[rows:]


def dot_across(x, matrix):
    return lax.dot_general(x, matrix, (((1,), (1,)), ((), ())), preferred_element_type=F32)


def dot_split(x, high_ref, low_ref):
    rows = x.shape[0]
    high, low = halves(x)
    both = jnp.dot(jnp.concatenate([high, low], 0), high_ref[...], preferred_element_type=F32)
    rest = jnp.dot(high, low_ref[...], preferred_element_type=F32)
    return both[:rows] + both[rows:] + rest


def face(x, f):
    return x[:, f * FD:(f + 1) * FD]


def take(x, row):
    index = jnp.broadcast_to(row.astype(jnp.int32), x.shape)
    return jnp.take_along_axis(x, index, axis=1, mode="promise_in_bounds")


def lower_changed(x, rows):
    parts = []
    for d in range(3):
        parts.append(-take(face(x, 2 * d), rows[d]))
        parts.append(face(x, 2 * d + 1))
    return jnp.concatenate(parts, axis=1)


RESIDUAL, SHOWN, SEARCH, APPLIED, LOAD, REST = (slice(CASES * i, CASES * (i + 1)) for i in range(6))
ORDERS = 6 * CASES
STATE = (ORDERS + 8, WIDE)


def apply_dense(field, state_ref, high_ref, low_ref):
    orders = state_ref[ORDERS:ORDERS + 8, :]
    partner = [face(orders[0:1, :], d) for d in range(3)]
    inverse = [face(orders[1:2, :], d) for d in range(3)]
    loads = lower_changed(field, inverse)
    return lower_changed(dot_split(loads, high_ref, low_ref), partner)


def position():
    gy = lax.axis_size("gy")
    places = [(lax.axis_index(a), lax.axis_size(a)) for a in ("gx", "gy", "gz")]
    there = []
    for place, size in places:
        there += [place > 0, place < size - 1]
    return places[0][0] * gy + places[1][0], places[2][0], there


def steps():
    gy = lax.axis_size("gy")
    return (-gy, gy, -1, 1)


def mask_row(there):
    return jnp.concatenate([jnp.full((1, FD), t.astype(F32)) for t in there], axis=1)


def put_rows(slots_ref, spot, rows):
    for q in range(4):
        slots_ref[spot, q] = rows[4 * q:4 * q + 4, :]


def take_rows(slots_ref, spot):
    return jnp.concatenate([slots_ref[spot, q] for q in range(4)], axis=0)


def target_rows(ids_row):
    row = lax.broadcasted_iota(jnp.int32, (8, FD), 1) % SUBS
    ids = take(jnp.broadcast_to(ids_row.astype(F32), (8, FD)), jnp.minimum(row // 3, 7))
    return jnp.where(row < 24, ids + (row % 3 * AGGREGATES).astype(F32), -1.0)


def prep_kernel(table_ref, rhs_ref, coupling_ref, *message_refs):
    _, _, there = position()
    target = target_rows(table_ref[0, 0, 3])
    for d in range(3):
        up_ref, down_ref = message_refs[d], message_refs[3 + d]
        row = table_ref[0, 0, d]
        up_ref[0:CASES, :] = rhs_ref[d] * there[2 * d + 1].astype(F32)
        wanted = lax.broadcasted_iota(jnp.int32, (FD, FD), 0)
        hits = (wanted == jnp.broadcast_to(row, (FD, FD))).astype(F32).astype(BF16)
        count = lax.broadcasted_iota(jnp.int32, (16, FD), 1).astype(F32).astype(BF16)
        up_ref[CASES:CASES + 8, :] = jnp.zeros((8, FD), F32)
        up_ref[CASES:CASES + 1, :] = row.astype(F32)
        up_ref[CASES + 1:CASES + 2, :] = dot_across(count, hits)[0:1, :]
        up_ref[24:48, :] = coupling_ref[:, (2 * d + 1) * FD:(2 * d + 2) * FD]
        up_ref[48:56, :] = target
        down_ref[0:24, :] = coupling_ref[:, 2 * d * FD:(2 * d + 1) * FD]
        down_ref[24:32, :] = target


def put_dense(table, diag_ref, couple_ref, high_ref, low_ref):
    high_ref[...] = jnp.zeros_like(high_ref)
    low_ref[...] = jnp.zeros_like(low_ref)

    def put(rows, cols, block):
        high, low = halves(block)
        high_ref[pl.ds(rows, FD), pl.ds(cols, FD)] = high
        low_ref[pl.ds(rows, FD), pl.ds(cols, FD)] = low

    for f in range(6):
        put(f * FD, f * FD, diag_ref[f])
    for k in range(6):
        first = pl.multiple_of(table[0, 0, 4, 0, k] * FD, FD)
        second = pl.multiple_of(table[0, 0, 5, 0, k] * FD, FD)
        block = couple_ref[k]
        put(second, first, block)
        put(first, second, block.T)


def dense_kernel(table, diag_ref, couple_ref, high_ref, low_ref):
    put_dense(table, diag_ref, couple_ref, high_ref, low_ref)


def start_kernel(ux_ref, uy_ref, uz_ref, mx_ref, my_ref, mz_ref, dz_ref, dh_ref, dl_ref, state_ref,
                 down_ref, up_ref):
    own, messages = (ux_ref, uy_ref, uz_ref), (mx_ref, my_ref, mz_ref)
    state_ref[...] = jnp.zeros_like(state_ref)
    parts = []
    for d in range(3):
        parts += [messages[d][0:CASES, :], own[d][0:CASES, :]]
        state_ref[ORDERS:ORDERS + 8, d * FD:(d + 1) * FD] = messages[d][CASES:CASES + 8, :]
    field = jnp.concatenate(parts, axis=1)
    state_ref[RESIDUAL, :] = field
    shown = apply_dense(field, state_ref, dh_ref, dl_ref)
    state_ref[SHOWN, :] = shown
    down_ref[0:CASES, :] = face(shown, 4)
    down_ref[CASES:CASES + 32, :] = dz_ref[...]
    up_ref[...] = face(shown, 5)


def joint_kernel(ux_ref, uy_ref, uz_ref, mx_ref, my_ref, mz_ref, dx_ref, dy_ref, dz_ref, nx_ref, ny_ref,
                 over_ref, state_ref, gh_ref, gl_ref, pick_ref, out_ref, pad):
    _, _, there = position()
    own, messages, lower = (ux_ref, uy_ref, uz_ref), (mx_ref, my_ref, mz_ref), (dx_ref, dy_ref, dz_ref)
    above = (nx_ref[...], ny_ref[...], over_ref[CASES:CASES + 32, :])
    pad[...] = jnp.zeros_like(pad)
    targets = [own[0][48:56, :]]
    for d in range(3):
        row = own[d][CASES:CASES + 1, :]
        low, high = slice(2 * d * FD, (2 * d + 1) * FD), slice((2 * d + 1) * FD, (2 * d + 2) * FD)
        pad[0:24, low] = -take(lower[d][0:24, :], messages[d][CASES:CASES + 1, :])
        pad[0:24, high] = own[d][24:48, :]
        sides = (
            (low, messages[d][24:48, :], messages[d][48:56, :]),
            (high, -take(above[d][0:24, :], row), above[d][24:32, :]),
        )
        for f, (lanes, rows, target) in zip((2 * d, 2 * d + 1), sides):
            exists = there[f].astype(F32)
            pad[SUBS * (f + 1):SUBS * (f + 1) + 24, lanes] = rows * exists
            targets.append(target * exists)
    high, low = halves(pad[...])
    gh_ref[...] = high
    gl_ref[...] = low
    lanes = lax.broadcasted_iota(jnp.int32, (8, FD), 1)
    rows = lax.broadcasted_iota(jnp.int32, (COARSE, FD), 0)
    for half in range(2):
        wanted = jnp.full((8, FD), -1.0, F32)
        for n in range(4 * half, min(4 * half + 4, 7)):
            wanted = jnp.where(lanes // SUBS == n % 4, targets[n], wanted)
        wanted = jnp.broadcast_to(wanted[0:1, :].astype(jnp.int32), (COARSE, FD))
        pick_ref[:, half * FD:(half + 1) * FD] = (rows == wanted).astype(F32).astype(BF16)
    sum_kernel(state_ref, gh_ref, gl_ref, pick_ref, out_ref)


def late_kernel(table, diag_ref, couple_ref, inverse_ref, _, fh_ref, fl_ref, kh_ref, kl_ref):
    put_dense(table, diag_ref, couple_ref, fh_ref, fl_ref)
    count = inverse_ref.shape[0]
    high, low = halves(inverse_ref[...])
    for ref, piece in ((kh_ref, high), (kl_ref, low)):
        ref[...] = jnp.zeros_like(ref)
        ref[0:count, 0:count] = piece


def face_sum(x, faces=range(6)):
    total = None
    for f in faces:
        total = face(x, f) if total is None else total + face(x, f)
    return total


def payload_places():
    for c in range(CASES):
        for b in range(COARSE // FD):
            spot, row = divmod(c * (COARSE // FD) + b, 3)
            yield c, b, spot, slice(row, row + 1)


def put_payload(out_ref, gathered, norm):
    lanes = lax.broadcasted_iota(jnp.int32, (CASES, FD), 1)
    blocks = [face(gathered, b) for b in range(COARSE // FD)]
    blocks[-1] = jnp.where(lanes == 64, norm, blocks[-1])
    for c, b, spot, row in payload_places():
        out_ref[spot, 4, row, :] = blocks[b][c:c + 1, :]


def sum_kernel(state_ref, gh_ref, gl_ref, pick_ref, out_ref):
    here, _, there = position()
    shown = state_ref[SHOWN, :]
    share = 0.25 * shown * mask_row(there)
    high, low = halves(share)
    both = dot_across(jnp.concatenate([high, low], 0), gh_ref[...])
    corner = both[:CASES] + both[CASES:] + dot_across(high, gl_ref[...])
    high, low = halves(corner)
    both = dot_across(jnp.concatenate([high, low], 0), pick_ref[...])
    norm = jnp.sum(face_sum(share * state_ref[RESIDUAL, :]), axis=1, keepdims=True)
    out_ref[...] = jnp.zeros_like(out_ref)
    put_payload(out_ref, both[:CASES] + both[CASES:], norm)
    for f, by in enumerate(steps()):
        @pl.when(there[f])
        def _():
            put_rows(out_ref, here + by, face(shown, f))


def put_layers(out_ref, total, flexed_ref, layer, there):
    out_ref[...] = jnp.zeros_like(out_ref)
    for i in range(out_ref.shape[0]):
        out_ref[i, 4] = total
    for f, by in ((4, -1), (5, 1)):
        @pl.when(there[f])
        def _():
            put_rows(out_ref, layer + by, flexed_ref[:, f * FD:(f + 1) * FD])


def flex_kernel(first, state_ref, slots_ref, below_ref, above_ref, fh_ref, fl_ref, z_ref, flexed_ref,
                out_ref, turn):
    here, layer, there = position()
    across = []
    for f, by in enumerate(steps()):
        across.append(take_rows(slots_ref, jnp.where(there[f], here + by, here)))
    across += [below_ref[...], above_ref[0:CASES, :]]
    z = 0.25 * (state_ref[SHOWN, :] + jnp.concatenate(across, axis=1)) * mask_row(there)
    z_ref[...] = z
    flexed = apply_dense(z, state_ref, fh_ref, fl_ref)
    flexed_ref[...] = flexed
    turn[...] = jnp.zeros_like(turn)
    turn[0:CASES, :] = face_sum(z * flexed)
    if not first:
        turn[CASES:2 * CASES, :] = (
            face_sum(z * state_ref[APPLIED, :], (1, 3, 5))
            + face_sum(state_ref[SEARCH, :] * flexed)
        )
    sums = jnp.sum(turn[...].T, axis=0, keepdims=True)
    total = jnp.sum(slots_ref[:, 4], axis=0)
    rows = lax.broadcasted_iota(jnp.int32, total.shape, 0)
    total = jnp.where(rows == 3, jnp.broadcast_to(sums, total.shape), total)
    put_layers(out_ref, total, flexed_ref, layer, there)


def share_kernel(layers_ref, flexed_ref, out_ref):
    here, _, there = position()
    total = jnp.sum(layers_ref[:, 4], axis=0)
    out_ref[...] = jnp.zeros_like(out_ref)
    for i in range(out_ref.shape[0]):
        out_ref[i, 4] = total
    for f, by in enumerate(steps()):
        @pl.when(there[f])
        def _():
            put_rows(out_ref, here + by, flexed_ref[:, f * FD:(f + 1) * FD])


def step_kernel(first, last, slots_ref, layers_ref, flexed_ref, z_ref, state_ref, kh_ref, kl_ref,
                gh_ref, gl_ref, pick_ref, *rest):
    rest, whole = rest[:-1], rest[-1]
    here, layer, there = position()
    across = []
    for f, by in enumerate(steps()):
        across.append(take_rows(slots_ref, jnp.where(there[f], here + by, here)))
    for f, by in ((4, -1), (5, 1)):
        across.append(take_rows(layers_ref, jnp.where(there[f], layer + by, layer)))
    mask = mask_row(there)
    applied = (flexed_ref[...] + jnp.concatenate(across, axis=1)) * mask
    search = z_ref[...]
    for c, b, spot, row in payload_places():
        whole[c:c + 1, b * FD:(b + 1) * FD] = slots_ref[spot, 4, row, :]
    load = whole[...]
    norm = load[:, COARSE - 64:COARSE - 63]
    sums = jnp.sum(slots_ref[:, 4], axis=0)[3:4, :]
    sums = jnp.broadcast_to(sums, (FD, FD)).T
    energy, cross = sums[0:CASES, 0:1], sums[CASES:2 * CASES, 0:1]
    lanes = lax.broadcasted_iota(jnp.int32, load.shape, 1)
    load = jnp.where(lanes < 3 * AGGREGATES, load, 0.0)
    if not first:
        scale = state_ref[REST, 0:FD]
        beta = norm / scale[:, 0:1]
        energy = energy + beta * cross + beta * beta * scale[:, 1:2]
        applied = applied + beta * state_ref[APPLIED, :]
        search = search + beta * state_ref[SEARCH, :]
        load = load + beta * state_ref[LOAD, 0:COARSE]
    coarse = dot_split(load, kh_ref, kl_ref)
    step = norm / (energy + jnp.sum(load * coarse, axis=1, keepdims=True))
    corner = dot_exact(coarse, pick_ref[...])
    correction = dot_split(corner, gh_ref, gl_ref) * mask
    residual = state_ref[RESIDUAL, :] - step * (applied + correction)
    moved = step * search
    if last:
        multipliers_ref, left_ref = rest
        for d in range(3):
            before = state_ref[REST, (d + 1) * FD:(d + 2) * FD]
            multipliers_ref[d] = before + face(moved, 2 * d + 1)
            left_ref[d] = face(residual, 2 * d + 1)
        return
    dh_ref, dl_ref, new_ref, down_ref, up_ref = rest
    new_ref[RESIDUAL, :] = residual
    shown = apply_dense(residual, state_ref, dh_ref, dl_ref)
    new_ref[SHOWN, :] = shown
    down_ref[...] = face(shown, 4)
    up_ref[...] = face(shown, 5)
    new_ref[SEARCH, :] = search
    new_ref[APPLIED, :] = applied
    new_ref[LOAD, 0:COARSE] = load
    new_ref[LOAD, COARSE:] = jnp.zeros((CASES, WIDE - COARSE), F32)
    lanes = lax.broadcasted_iota(jnp.int32, (CASES, FD), 1)
    scale = jnp.where(lanes == 0, norm, energy)
    parts = [scale]
    for d in range(3):
        parts.append(state_ref[REST, (d + 1) * FD:(d + 2) * FD] + face(moved, 2 * d + 1))
    new_ref[REST, :] = jnp.concatenate(parts + [scale, scale], axis=1)
    new_ref[ORDERS:ORDERS + 8, :] = state_ref[ORDERS:ORDERS + 8, :]


def passed_along(shard, axis, by):
    peers = lax.axis_size(axis)
    pairs = [(i, i + by) for i in range(peers) if 0 <= i + by < peers]
    return lax.ppermute(shard, axis, pairs)


def swapped(slots, axes):
    return lax.all_to_all(slots, axes, 0, 0)


def body(
    jump_rhs,
    flex_diag,
    flex_couple,
    dirichlet_diag,
    dirichlet_couple,
    face_pairs,
    corner_coupling,
    coarse_ids,
    partner,
    coarse_inverse,
):
    gx, gy, gz = (lax.axis_size(a) for a in AXES)
    plane = gx * gy
    rhs = jump_rhs.reshape(3, CASES, FD)
    coupling = corner_coupling.reshape(24, WIDE)
    square = (WIDE, WIDE)
    wide = (CASES, WIDE)

    width = ((0, 0),) * 4
    table = jnp.concatenate(
        [
            jnp.swapaxes(partner, 2, 3),
            jnp.pad(coarse_ids[:, :, :, None, :], width + ((0, FD - 8),)),
            jnp.pad(jnp.transpose(face_pairs, (0, 1, 4, 2, 3)), width + ((0, FD - 6),)),
        ],
        axis=2,
    )
    *ups, dx, dy, dz = call(
        prep_kernel, [((56, FD), F32)] * 3 + [((32, FD), F32)] * 3,
        [table, rhs, coupling],
    )
    messages = [passed_along(m, a, 1) for m, a in zip(ups, AXES)]
    above = [passed_along(m, a, -1) for m, a in zip((dx, dy), AXES)]
    blocks = [b.reshape(6, FD, FD) for b in (dirichlet_diag, dirichlet_couple, flex_diag, flex_couple)]
    dirichlet = call(
        dense_kernel, [(square, BF16)] * 2, [table] + blocks[:2], specs=[SMEM]
    )
    state, down, up = call(
        start_kernel,
        [(STATE, F32), ((CASES + 32, FD), F32), ((CASES, FD), F32)],
        [*ups, *messages, dz, *dirichlet],
    )
    stacked = (plane, 5, 4, FD)

    for iteration in range(ITERS):
        first, last = iteration == 0, iteration + 1 == ITERS
        below = passed_along(up, "gz", 1)
        over = passed_along(down, "gz", -1)
        if first:
            *joint, slots = call(
                joint_kernel,
                [((CORNERS, WIDE), BF16)] * 2 + [((COARSE, CORNERS), BF16), (stacked, F32)],
                [*ups, *messages, dx, dy, dz, *above, over, state],
                scratch=[pltpu.VMEM((CORNERS, WIDE), F32)],
            )
        else:
            (slots,) = call(sum_kernel, [(stacked, F32)], [state, *joint])
        slots, below, over = lax.optimization_barrier((slots, below, over))
        slots = swapped(slots, PLANE)
        if first:
            late = call(
                late_kernel, [(square, BF16)] * 2 + [((COARSE, COARSE), BF16)] * 2,
                [table] + blocks[2:] + [coarse_inverse, slots],
                specs=[SMEM] + [VMEM] * 3 + [pl.BlockSpec(memory_space=pl.ANY)],
            )
            flex, inverse = late[:2], late[2:]
        z, flexed, layers = call(
            functools.partial(flex_kernel, first),
            [(wide, F32), (wide, F32), ((gz, 5, 4, FD), F32)],
            [state, slots, below, over, *flex],
            scratch=[pltpu.VMEM((FD, FD), F32)],
        )
        layers = swapped(layers, "gz")
        (slots,) = call(share_kernel, [(stacked, F32)], [layers, flexed])
        slots = swapped(slots, PLANE)
        common = [slots, layers, flexed, z, state, *inverse, *joint]
        kernel = functools.partial(step_kernel, first, last)
        scratch = [pltpu.VMEM((CASES, COARSE), F32)]
        if last:
            multipliers, left = call(kernel, [((3, CASES, FD), F32)] * 2, common, scratch=scratch)
            break
        state, down, up = call(
            kernel, [(STATE, F32)] + [((CASES, FD), F32)] * 2, common + [*dirichlet], scratch=scratch
        )
    return multipliers.reshape(jump_rhs.shape), left.reshape(jump_rhs.shape)


def solution(mesh):
    placed = (
        P("gx", "gy", "gz", None, None, None),
        P("gx", "gy", "gz", None, None, None),
        P("gx", "gy", "gz", None, None, None),
        P("gx", "gy", "gz", None, None, None),
        P("gx", "gy", "gz", None, None, None),
        P("gx", "gy", "gz", None, None),
        P("gx", "gy", "gz", None, None),
        P("gx", "gy", "gz", None),
        P("gx", "gy", "gz", None, None),
        P(),
    )
    return jax.shard_map(
        body,
        mesh=mesh,
        in_specs=placed,
        out_specs=(P("gx", "gy", "gz", None, None, None), P("gx", "gy", "gz", None, None, None)),
        check_vma=False,
    )
```

```python
import functools

import jax
import jax.numpy as jnp
from jax import lax
from jax.experimental import pallas as pl
from jax.experimental.pallas import tpu as pltpu
from jax.sharding import PartitionSpec as P

ITERS = 3
CASES = 16
FD = 128
WIDE = 6 * FD
AGGREGATES = 192
COARSE = 640
SUBS = 32
CORNERS = 256
AXES = ("gx", "gy", "gz")
PLANE = ("gx", "gy")
F32 = jnp.float32
BF16 = jnp.bfloat16
VMEM = pl.BlockSpec(memory_space=pltpu.VMEM)
SMEM = pl.BlockSpec(memory_space=pltpu.SMEM)


def call(kernel, outs, args, specs=(), scratch=()):
    return pl.pallas_call(
        kernel,
        out_shape=[jax.ShapeDtypeStruct(shape, dtype) for shape, dtype in outs],
        in_specs=list(specs) + [VMEM] * (len(args) - len(specs)),
        out_specs=[VMEM] * len(outs),
        scratch_shapes=list(scratch),
        compiler_params=pltpu.CompilerParams(vmem_limit_bytes=40 * 1024 * 1024),
    )(*args)


def halves(x):
    high = x.astype(BF16)
    return high, (x - high.astype(F32)).astype(BF16)


def dot_exact(x, selector):
    rows = x.shape[0]
    high, low = halves(x)
    both = jnp.dot(jnp.concatenate([high, low], 0), selector, preferred_element_type=F32)
    return both[:rows] + both[rows:]


def dot_across(x, matrix):
    return lax.dot_general(x, matrix, (((1,), (1,)), ((), ())), preferred_element_type=F32)


def dot_split(x, high_ref, low_ref):
    rows = x.shape[0]
    high, low = halves(x)
    both = jnp.dot(jnp.concatenate([high, low], 0), high_ref[...], preferred_element_type=F32)
    rest = jnp.dot(high, low_ref[...], preferred_element_type=F32)
    return both[:rows] + both[rows:] + rest


def face(x, f):
    return x[:, f * FD:(f + 1) * FD]


def take(x, row):
    index = jnp.broadcast_to(row.astype(jnp.int32), x.shape)
    return jnp.take_along_axis(x, index, axis=1, mode="promise_in_bounds")


def lower_changed(x, rows):
    parts = []
    for d in range(3):
        parts.append(-take(face(x, 2 * d), rows[d]))
        parts.append(face(x, 2 * d + 1))
    return jnp.concatenate(parts, axis=1)


RESIDUAL, SHOWN, SEARCH, APPLIED, LOAD, REST = (slice(CASES * i, CASES * (i + 1)) for i in range(6))
ORDERS = 6 * CASES
STATE = (ORDERS + 8, WIDE)


def apply_dense(field, state_ref, high_ref, low_ref):
    orders = state_ref[ORDERS:ORDERS + 8, :]
    partner = [face(orders[0:1, :], d) for d in range(3)]
    inverse = [face(orders[1:2, :], d) for d in range(3)]
    loads = lower_changed(field, inverse)
    return lower_changed(dot_split(loads, high_ref, low_ref), partner)


def position():
    gy = lax.axis_size("gy")
    places = [(lax.axis_index(a), lax.axis_size(a)) for a in ("gx", "gy", "gz")]
    there = []
    for place, size in places:
        there += [place > 0, place < size - 1]
    return places[0][0] * gy + places[1][0], places[2][0], there


def steps():
    gy = lax.axis_size("gy")
    return (-gy, gy, -1, 1)


def mask_row(there):
    return jnp.concatenate([jnp.full((1, FD), t.astype(F32)) for t in there], axis=1)


def put_rows(slots_ref, spot, rows):
    for q in range(4):
        slots_ref[spot, q] = rows[4 * q:4 * q + 4, :]


def take_rows(slots_ref, spot):
    return jnp.concatenate([slots_ref[spot, q] for q in range(4)], axis=0)


def target_rows(ids_row):
    row = lax.broadcasted_iota(jnp.int32, (8, FD), 1) % SUBS
    ids = take(jnp.broadcast_to(ids_row.astype(F32), (8, FD)), jnp.minimum(row // 3, 7))
    return jnp.where(row < 24, ids + (row % 3 * AGGREGATES).astype(F32), -1.0)


def prep_kernel(table_ref, rhs_ref, coupling_ref, *message_refs):
    _, _, there = position()
    target = target_rows(table_ref[0, 0, 3])
    for d in range(3):
        up_ref, down_ref = message_refs[d], message_refs[3 + d]
        row = table_ref[0, 0, d]
        up_ref[0:CASES, :] = rhs_ref[d] * there[2 * d + 1].astype(F32)
        wanted = lax.broadcasted_iota(jnp.int32, (FD, FD), 0)
        hits = (wanted == jnp.broadcast_to(row, (FD, FD))).astype(F32).astype(BF16)
        count = lax.broadcasted_iota(jnp.int32, (16, FD), 1).astype(F32).astype(BF16)
        up_ref[CASES:CASES + 8, :] = jnp.zeros((8, FD), F32)
        up_ref[CASES:CASES + 1, :] = row.astype(F32)
        up_ref[CASES + 1:CASES + 2, :] = dot_across(count, hits)[0:1, :]
        up_ref[24:48, :] = coupling_ref[:, (2 * d + 1) * FD:(2 * d + 2) * FD]
        up_ref[48:56, :] = target
        down_ref[0:24, :] = coupling_ref[:, 2 * d * FD:(2 * d + 1) * FD]
        down_ref[24:32, :] = target


def put_dense(table, diag_ref, couple_ref, high_ref, low_ref):
    high_ref[...] = jnp.zeros_like(high_ref)
    low_ref[...] = jnp.zeros_like(low_ref)

    def put(rows, cols, block):
        high, low = halves(block)
        high_ref[pl.ds(rows, FD), pl.ds(cols, FD)] = high
        low_ref[pl.ds(rows, FD), pl.ds(cols, FD)] = low

    for f in range(6):
        put(f * FD, f * FD, diag_ref[f])
    for k in range(6):
        first = pl.multiple_of(table[0, 0, 4, 0, k] * FD, FD)
        second = pl.multiple_of(table[0, 0, 5, 0, k] * FD, FD)
        block = couple_ref[k]
        put(second, first, block)
        put(first, second, block.T)


def dense_kernel(table, diag_ref, couple_ref, high_ref, low_ref):
    put_dense(table, diag_ref, couple_ref, high_ref, low_ref)


def start_kernel(ux_ref, uy_ref, uz_ref, mx_ref, my_ref, mz_ref, dz_ref, dh_ref, dl_ref, state_ref,
                 down_ref, up_ref):
    own, messages = (ux_ref, uy_ref, uz_ref), (mx_ref, my_ref, mz_ref)
    state_ref[...] = jnp.zeros_like(state_ref)
    parts = []
    for d in range(3):
        parts += [messages[d][0:CASES, :], own[d][0:CASES, :]]
        state_ref[ORDERS:ORDERS + 8, d * FD:(d + 1) * FD] = messages[d][CASES:CASES + 8, :]
    field = jnp.concatenate(parts, axis=1)
    state_ref[RESIDUAL, :] = field
    shown = apply_dense(field, state_ref, dh_ref, dl_ref)
    state_ref[SHOWN, :] = shown
    down_ref[0:CASES, :] = face(shown, 4)
    down_ref[CASES:CASES + 32, :] = dz_ref[...]
    up_ref[...] = face(shown, 5)


def joint_kernel(ux_ref, uy_ref, uz_ref, mx_ref, my_ref, mz_ref, dx_ref, dy_ref, dz_ref, nx_ref, ny_ref,
                 over_ref, state_ref, gh_ref, gl_ref, pick_ref, out_ref, pad):
    _, _, there = position()
    own, messages, lower = (ux_ref, uy_ref, uz_ref), (mx_ref, my_ref, mz_ref), (dx_ref, dy_ref, dz_ref)
    above = (nx_ref[...], ny_ref[...], over_ref[CASES:CASES + 32, :])
    pad[...] = jnp.zeros_like(pad)
    targets = [own[0][48:56, :]]
    for d in range(3):
        row = own[d][CASES:CASES + 1, :]
        low, high = slice(2 * d * FD, (2 * d + 1) * FD), slice((2 * d + 1) * FD, (2 * d + 2) * FD)
        pad[0:24, low] = -take(lower[d][0:24, :], messages[d][CASES:CASES + 1, :])
        pad[0:24, high] = own[d][24:48, :]
        sides = (
            (low, messages[d][24:48, :], messages[d][48:56, :]),
            (high, -take(above[d][0:24, :], row), above[d][24:32, :]),
        )
        for f, (lanes, rows, target) in zip((2 * d, 2 * d + 1), sides):
            exists = there[f].astype(F32)
            pad[SUBS * (f + 1):SUBS * (f + 1) + 24, lanes] = rows * exists
            targets.append(target * exists)
    high, low = halves(pad[...])
    gh_ref[...] = high
    gl_ref[...] = low
    lanes = lax.broadcasted_iota(jnp.int32, (8, FD), 1)
    rows = lax.broadcasted_iota(jnp.int32, (COARSE, FD), 0)
    for half in range(2):
        wanted = jnp.full((8, FD), -1.0, F32)
        for n in range(4 * half, min(4 * half + 4, 7)):
            wanted = jnp.where(lanes // SUBS == n % 4, targets[n], wanted)
        wanted = jnp.broadcast_to(wanted[0:1, :].astype(jnp.int32), (COARSE, FD))
        pick_ref[:, half * FD:(half + 1) * FD] = (rows == wanted).astype(F32).astype(BF16)
    sum_kernel(state_ref, gh_ref, gl_ref, pick_ref, out_ref)


def late_kernel(table, diag_ref, couple_ref, inverse_ref, _, fh_ref, fl_ref, kh_ref, kl_ref):
    put_dense(table, diag_ref, couple_ref, fh_ref, fl_ref)
    count = inverse_ref.shape[0]
    high, low = halves(inverse_ref[...])
    for ref, piece in ((kh_ref, high), (kl_ref, low)):
        ref[...] = jnp.zeros_like(ref)
        ref[0:count, 0:count] = piece


def face_sum(x, faces=range(6)):
    total = None
    for f in faces:
        total = face(x, f) if total is None else total + face(x, f)
    return total


def payload_places():
    for c in range(CASES):
        for b in range(COARSE // FD):
            spot, row = divmod(c * (COARSE // FD) + b, 3)
            yield c, b, spot, slice(row, row + 1)


def put_payload(out_ref, gathered, norm):
    lanes = lax.broadcasted_iota(jnp.int32, (CASES, FD), 1)
    blocks = [face(gathered, b) for b in range(COARSE // FD)]
    blocks[-1] = jnp.where(lanes == 64, norm, blocks[-1])
    for c, b, spot, row in payload_places():
        out_ref[spot, 4, row, :] = blocks[b][c:c + 1, :]


def sum_kernel(state_ref, gh_ref, gl_ref, pick_ref, out_ref):
    here, _, there = position()
    shown = state_ref[SHOWN, :]
    share = 0.25 * shown * mask_row(there)
    high, low = halves(share)
    both = dot_across(jnp.concatenate([high, low], 0), gh_ref[...])
    corner = both[:CASES] + both[CASES:] + dot_across(high, gl_ref[...])
    high, low = halves(corner)
    both = dot_across(jnp.concatenate([high, low], 0), pick_ref[...])
    norm = jnp.sum(face_sum(share * state_ref[RESIDUAL, :]), axis=1, keepdims=True)
    out_ref[...] = jnp.zeros_like(out_ref)
    put_payload(out_ref, both[:CASES] + both[CASES:], norm)
    for f, by in enumerate(steps()):
        @pl.when(there[f])
        def _():
            put_rows(out_ref, here + by, face(shown, f))


def put_layers(out_ref, total, flexed_ref, layer, there):
    out_ref[...] = jnp.zeros_like(out_ref)
    for i in range(out_ref.shape[0]):
        out_ref[i, 4] = total
    for f, by in ((4, -1), (5, 1)):
        @pl.when(there[f])
        def _():
            put_rows(out_ref, layer + by, flexed_ref[:, f * FD:(f + 1) * FD])


def flex_kernel(first, state_ref, slots_ref, below_ref, above_ref, fh_ref, fl_ref, z_ref, flexed_ref,
                out_ref, turn):
    here, layer, there = position()
    across = []
    for f, by in enumerate(steps()):
        across.append(take_rows(slots_ref, jnp.where(there[f], here + by, here)))
    across += [below_ref[...], above_ref[0:CASES, :]]
    z = 0.25 * (state_ref[SHOWN, :] + jnp.concatenate(across, axis=1)) * mask_row(there)
    z_ref[...] = z
    flexed = apply_dense(z, state_ref, fh_ref, fl_ref)
    flexed_ref[...] = flexed
    turn[...] = jnp.zeros_like(turn)
    turn[0:CASES, :] = face_sum(z * flexed)
    if not first:
        turn[CASES:2 * CASES, :] = (
            face_sum(z * state_ref[APPLIED, :], (1, 3, 5))
            + face_sum(state_ref[SEARCH, :] * flexed)
        )
    sums = jnp.sum(turn[...].T, axis=0, keepdims=True)
    total = jnp.sum(slots_ref[:, 4], axis=0)
    rows = lax.broadcasted_iota(jnp.int32, total.shape, 0)
    total = jnp.where(rows == 3, jnp.broadcast_to(sums, total.shape), total)
    put_layers(out_ref, total, flexed_ref, layer, there)


def share_kernel(layers_ref, flexed_ref, out_ref):
    here, _, there = position()
    total = jnp.sum(layers_ref[:, 4], axis=0)
    out_ref[...] = jnp.zeros_like(out_ref)
    for i in range(out_ref.shape[0]):
        out_ref[i, 4] = total
    for f, by in enumerate(steps()):
        @pl.when(there[f])
        def _():
            put_rows(out_ref, here + by, flexed_ref[:, f * FD:(f + 1) * FD])


def step_kernel(first, last, slots_ref, layers_ref, flexed_ref, z_ref, state_ref, kh_ref, kl_ref,
                gh_ref, gl_ref, pick_ref, *rest):
    rest, whole = rest[:-1], rest[-1]
    here, layer, there = position()
    across = []
    for f, by in enumerate(steps()):
        across.append(take_rows(slots_ref, jnp.where(there[f], here + by, here)))
    for f, by in ((4, -1), (5, 1)):
        across.append(take_rows(layers_ref, jnp.where(there[f], layer + by, layer)))
    mask = mask_row(there)
    applied = (flexed_ref[...] + jnp.concatenate(across, axis=1)) * mask
    search = z_ref[...]
    for c, b, spot, row in payload_places():
        whole[c:c + 1, b * FD:(b + 1) * FD] = slots_ref[spot, 4, row, :]
    load = whole[...]
    norm = load[:, COARSE - 64:COARSE - 63]
    sums = jnp.sum(slots_ref[:, 4], axis=0)[3:4, :]
    sums = jnp.broadcast_to(sums, (FD, FD)).T
    energy, cross = sums[0:CASES, 0:1], sums[CASES:2 * CASES, 0:1]
    lanes = lax.broadcasted_iota(jnp.int32, load.shape, 1)
    load = jnp.where(lanes < 3 * AGGREGATES, load, 0.0)
    if not first:
        scale = state_ref[REST, 0:FD]
        beta = norm / scale[:, 0:1]
        energy = energy + beta * cross + beta * beta * scale[:, 1:2]
        applied = applied + beta * state_ref[APPLIED, :]
        search = search + beta * state_ref[SEARCH, :]
        load = load + beta * state_ref[LOAD, 0:COARSE]
    coarse = dot_split(load, kh_ref, kl_ref)
    step = norm / (energy + jnp.sum(load * coarse, axis=1, keepdims=True))
    corner = dot_exact(coarse, pick_ref[...])
    correction = dot_split(corner, gh_ref, gl_ref) * mask
    residual = state_ref[RESIDUAL, :] - step * (applied + correction)
    moved = step * search
    if last:
        multipliers_ref, left_ref = rest
        for d in range(3):
            before = state_ref[REST, (d + 1) * FD:(d + 2) * FD]
            multipliers_ref[d] = before + face(moved, 2 * d + 1)
            left_ref[d] = face(residual, 2 * d + 1)
        return
    dh_ref, dl_ref, new_ref, down_ref, up_ref = rest
    new_ref[RESIDUAL, :] = residual
    shown = apply_dense(residual, state_ref, dh_ref, dl_ref)
    new_ref[SHOWN, :] = shown
    down_ref[...] = face(shown, 4)
    up_ref[...] = face(shown, 5)
    new_ref[SEARCH, :] = search
    new_ref[APPLIED, :] = applied
    new_ref[LOAD, 0:COARSE] = load
    new_ref[LOAD, COARSE:] = jnp.zeros((CASES, WIDE - COARSE), F32)
    lanes = lax.broadcasted_iota(jnp.int32, (CASES, FD), 1)
    scale = jnp.where(lanes == 0, norm, energy)
    parts = [scale]
    for d in range(3):
        parts.append(state_ref[REST, (d + 1) * FD:(d + 2) * FD] + face(moved, 2 * d + 1))
    new_ref[REST, :] = jnp.concatenate(parts + [scale, scale], axis=1)
    new_ref[ORDERS:ORDERS + 8, :] = state_ref[ORDERS:ORDERS + 8, :]


def passed_along(shard, axis, by):
    peers = lax.axis_size(axis)
    pairs = [(i, i + by) for i in range(peers) if 0 <= i + by < peers]
    return lax.ppermute(shard, axis, pairs)


def swapped(slots, axes):
    return lax.all_to_all(slots, axes, 0, 0)


def body(
    jump_rhs,
    flex_diag,
    flex_couple,
    dirichlet_diag,
    dirichlet_couple,
    face_pairs,
    corner_coupling,
    coarse_ids,
    partner,
    coarse_inverse,
):
    gx, gy, gz = (lax.axis_size(a) for a in AXES)
    plane = gx * gy
    rhs = jump_rhs.reshape(3, CASES, FD)
    coupling = corner_coupling.reshape(24, WIDE)
    square = (WIDE, WIDE)
    wide = (CASES, WIDE)

    width = ((0, 0),) * 4
    table = jnp.concatenate(
        [
            jnp.swapaxes(partner, 2, 3),
            jnp.pad(coarse_ids[:, :, :, None, :], width + ((0, FD - 8),)),
            jnp.pad(jnp.transpose(face_pairs, (0, 1, 4, 2, 3)), width + ((0, FD - 6),)),
        ],
        axis=2,
    )
    *ups, dx, dy, dz = call(
        prep_kernel, [((56, FD), F32)] * 3 + [((32, FD), F32)] * 3,
        [table, rhs, coupling],
    )
    messages = [passed_along(m, a, 1) for m, a in zip(ups, AXES)]
    above = [passed_along(m, a, -1) for m, a in zip((dx, dy), AXES)]
    blocks = [b.reshape(6, FD, FD) for b in (dirichlet_diag, dirichlet_couple, flex_diag, flex_couple)]
    dirichlet = call(
        dense_kernel, [(square, BF16)] * 2, [table] + blocks[:2], specs=[SMEM]
    )
    state, down, up = call(
        start_kernel,
        [(STATE, F32), ((CASES + 32, FD), F32), ((CASES, FD), F32)],
        [*ups, *messages, dz, *dirichlet],
    )
    stacked = (plane, 5, 4, FD)

    for iteration in range(ITERS):
        first, last = iteration == 0, iteration + 1 == ITERS
        below = passed_along(up, "gz", 1)
        over = passed_along(down, "gz", -1)
        if first:
            *joint, slots = call(
                joint_kernel,
                [((CORNERS, WIDE), BF16)] * 2 + [((COARSE, CORNERS), BF16), (stacked, F32)],
                [*ups, *messages, dx, dy, dz, *above, over, state],
                scratch=[pltpu.VMEM((CORNERS, WIDE), F32)],
            )
        else:
            (slots,) = call(sum_kernel, [(stacked, F32)], [state, *joint])
        if not last:
            slots, below, over = lax.optimization_barrier((slots, below, over))
        slots = swapped(slots, PLANE)
        if first:
            late = call(
                late_kernel, [(square, BF16)] * 2 + [((COARSE, COARSE), BF16)] * 2,
                [table] + blocks[2:] + [coarse_inverse, slots],
                specs=[SMEM] + [VMEM] * 3 + [pl.BlockSpec(memory_space=pl.ANY)],
            )
            flex, inverse = late[:2], late[2:]
        z, flexed, layers = call(
            functools.partial(flex_kernel, first),
            [(wide, F32), (wide, F32), ((gz, 5, 4, FD), F32)],
            [state, slots, below, over, *flex],
            scratch=[pltpu.VMEM((FD, FD), F32)],
        )
        layers = swapped(layers, "gz")
        (slots,) = call(share_kernel, [(stacked, F32)], [layers, flexed])
        slots = swapped(slots, PLANE)
        common = [slots, layers, flexed, z, state, *inverse, *joint]
        kernel = functools.partial(step_kernel, first, last)
        scratch = [pltpu.VMEM((CASES, COARSE), F32)]
        if last:
            multipliers, left = call(kernel, [((3, CASES, FD), F32)] * 2, common, scratch=scratch)
            break
        state, down, up = call(
            kernel, [(STATE, F32)] + [((CASES, FD), F32)] * 2, common + [*dirichlet], scratch=scratch
        )
    return multipliers.reshape(jump_rhs.shape), left.reshape(jump_rhs.shape)


def solution(mesh):
    placed = (
        P("gx", "gy", "gz", None, None, None),
        P("gx", "gy", "gz", None, None, None),
        P("gx", "gy", "gz", None, None, None),
        P("gx", "gy", "gz", None, None, None),
        P("gx", "gy", "gz", None, None, None),
        P("gx", "gy", "gz", None, None),
        P("gx", "gy", "gz", None, None),
        P("gx", "gy", "gz", None),
        P("gx", "gy", "gz", None, None),
        P(),
    )
    return jax.shard_map(
        body,
        mesh=mesh,
        in_specs=placed,
        out_specs=(P("gx", "gy", "gz", None, None, None), P("gx", "gy", "gz", None, None, None)),
        check_vma=False,
    )
```

```python
import functools

import jax
import jax.numpy as jnp
from jax import lax
from jax.experimental import pallas as pl
from jax.experimental.pallas import tpu as pltpu
from jax.sharding import PartitionSpec as P

ITERS = 3
CASES = 16
FD = 128
WIDE = 6 * FD
AGGREGATES = 192
COARSE = 640
SUBS = 32
CORNERS = 256
AXES = ("gx", "gy", "gz")
PLANE = ("gx", "gy")
F32 = jnp.float32
BF16 = jnp.bfloat16
VMEM = pl.BlockSpec(memory_space=pltpu.VMEM)
SMEM = pl.BlockSpec(memory_space=pltpu.SMEM)


def call(kernel, outs, args, specs=(), scratch=()):
    return pl.pallas_call(
        kernel,
        out_shape=[jax.ShapeDtypeStruct(shape, dtype) for shape, dtype in outs],
        in_specs=list(specs) + [VMEM] * (len(args) - len(specs)),
        out_specs=[VMEM] * len(outs),
        scratch_shapes=list(scratch),
        compiler_params=pltpu.CompilerParams(vmem_limit_bytes=40 * 1024 * 1024),
    )(*args)


def halves(x):
    high = x.astype(BF16)
    return high, (x - high.astype(F32)).astype(BF16)


def dot_exact(x, selector):
    rows = x.shape[0]
    high, low = halves(x)
    both = jnp.dot(jnp.concatenate([high, low], 0), selector, preferred_element_type=F32)
    return both[:rows] + both[rows:]


def dot_across(x, matrix):
    return lax.dot_general(x, matrix, (((1,), (1,)), ((), ())), preferred_element_type=F32)


def dot_split(x, high_ref, low_ref):
    rows = x.shape[0]
    high, low = halves(x)
    both = jnp.dot(jnp.concatenate([high, low], 0), high_ref[...], preferred_element_type=F32)
    rest = jnp.dot(high, low_ref[...], preferred_element_type=F32)
    return both[:rows] + both[rows:] + rest


def face(x, f):
    return x[:, f * FD:(f + 1) * FD]


def take(x, row):
    index = jnp.broadcast_to(row.astype(jnp.int32), x.shape)
    return jnp.take_along_axis(x, index, axis=1, mode="promise_in_bounds")


def lower_changed(x, rows):
    parts = []
    for d in range(3):
        parts.append(-take(face(x, 2 * d), rows[d]))
        parts.append(face(x, 2 * d + 1))
    return jnp.concatenate(parts, axis=1)


RESIDUAL, SHOWN, SEARCH, APPLIED, LOAD, REST = (slice(CASES * i, CASES * (i + 1)) for i in range(6))
ORDERS = 6 * CASES
STATE = (ORDERS + 8, WIDE)


def apply_dense(field, state_ref, high_ref, low_ref):
    orders = state_ref[ORDERS:ORDERS + 8, :]
    partner = [face(orders[0:1, :], d) for d in range(3)]
    inverse = [face(orders[1:2, :], d) for d in range(3)]
    loads = lower_changed(field, inverse)
    return lower_changed(dot_split(loads, high_ref, low_ref), partner)


def position():
    gy = lax.axis_size("gy")
    places = [(lax.axis_index(a), lax.axis_size(a)) for a in ("gx", "gy", "gz")]
    there = []
    for place, size in places:
        there += [place > 0, place < size - 1]
    return places[0][0] * gy + places[1][0], places[2][0], there


def steps():
    gy = lax.axis_size("gy")
    return (-gy, gy, -1, 1)


def mask_row(there):
    return jnp.concatenate([jnp.full((1, FD), t.astype(F32)) for t in there], axis=1)


def put_rows(slots_ref, spot, rows):
    for q in range(4):
        slots_ref[spot, q] = rows[4 * q:4 * q + 4, :]


def take_rows(slots_ref, spot):
    return jnp.concatenate([slots_ref[spot, q] for q in range(4)], axis=0)


def target_rows(ids_row):
    row = lax.broadcasted_iota(jnp.int32, (8, FD), 1) % SUBS
    ids = take(jnp.broadcast_to(ids_row.astype(F32), (8, FD)), jnp.minimum(row // 3, 7))
    return jnp.where(row < 24, ids + (row % 3 * AGGREGATES).astype(F32), -1.0)


def prep_kernel(table_ref, rhs_ref, coupling_ref, *message_refs):
    _, _, there = position()
    target = target_rows(table_ref[0, 0, 3])
    for d in range(3):
        up_ref, down_ref = message_refs[d], message_refs[3 + d]
        row = table_ref[0, 0, d]
        up_ref[0:CASES, :] = rhs_ref[d] * there[2 * d + 1].astype(F32)
        wanted = lax.broadcasted_iota(jnp.int32, (FD, FD), 0)
        hits = (wanted == jnp.broadcast_to(row, (FD, FD))).astype(F32).astype(BF16)
        count = lax.broadcasted_iota(jnp.int32, (16, FD), 1).astype(F32).astype(BF16)
        up_ref[CASES:CASES + 8, :] = jnp.zeros((8, FD), F32)
        up_ref[CASES:CASES + 1, :] = row.astype(F32)
        up_ref[CASES + 1:CASES + 2, :] = dot_across(count, hits)[0:1, :]
        up_ref[24:48, :] = coupling_ref[:, (2 * d + 1) * FD:(2 * d + 2) * FD]
        up_ref[48:56, :] = target
        down_ref[0:24, :] = coupling_ref[:, 2 * d * FD:(2 * d + 1) * FD]
        down_ref[24:32, :] = target


def put_dense(table, diag_ref, couple_ref, high_ref, low_ref):
    high_ref[...] = jnp.zeros_like(high_ref)
    low_ref[...] = jnp.zeros_like(low_ref)

    def put(rows, cols, block):
        high, low = halves(block)
        high_ref[pl.ds(rows, FD), pl.ds(cols, FD)] = high
        low_ref[pl.ds(rows, FD), pl.ds(cols, FD)] = low

    for f in range(6):
        put(f * FD, f * FD, diag_ref[f])
    for k in range(6):
        first = pl.multiple_of(table[0, 0, 4, 0, k] * FD, FD)
        second = pl.multiple_of(table[0, 0, 5, 0, k] * FD, FD)
        block = couple_ref[k]
        put(second, first, block)
        put(first, second, block.T)


def dense_kernel(table, diag_ref, couple_ref, high_ref, low_ref):
    put_dense(table, diag_ref, couple_ref, high_ref, low_ref)


def start_kernel(ux_ref, uy_ref, uz_ref, mx_ref, my_ref, mz_ref, dz_ref, dh_ref, dl_ref, state_ref,
                 down_ref, up_ref):
    own, messages = (ux_ref, uy_ref, uz_ref), (mx_ref, my_ref, mz_ref)
    state_ref[...] = jnp.zeros_like(state_ref)
    parts = []
    for d in range(3):
        parts += [messages[d][0:CASES, :], own[d][0:CASES, :]]
        state_ref[ORDERS:ORDERS + 8, d * FD:(d + 1) * FD] = messages[d][CASES:CASES + 8, :]
    field = jnp.concatenate(parts, axis=1)
    state_ref[RESIDUAL, :] = field
    shown = apply_dense(field, state_ref, dh_ref, dl_ref)
    state_ref[SHOWN, :] = shown
    down_ref[0:CASES, :] = face(shown, 4)
    down_ref[CASES:CASES + 32, :] = dz_ref[...]
    up_ref[...] = face(shown, 5)


def joint_kernel(ux_ref, uy_ref, uz_ref, mx_ref, my_ref, mz_ref, dx_ref, dy_ref, dz_ref, nx_ref, ny_ref,
                 over_ref, state_ref, gh_ref, gl_ref, pick_ref, out_ref, pad):
    _, _, there = position()
    own, messages, lower = (ux_ref, uy_ref, uz_ref), (mx_ref, my_ref, mz_ref), (dx_ref, dy_ref, dz_ref)
    above = (nx_ref[...], ny_ref[...], over_ref[CASES:CASES + 32, :])
    pad[...] = jnp.zeros_like(pad)
    targets = [own[0][48:56, :]]
    for d in range(3):
        row = own[d][CASES:CASES + 1, :]
        low, high = slice(2 * d * FD, (2 * d + 1) * FD), slice((2 * d + 1) * FD, (2 * d + 2) * FD)
        pad[0:24, low] = -take(lower[d][0:24, :], messages[d][CASES:CASES + 1, :])
        pad[0:24, high] = own[d][24:48, :]
        sides = (
            (low, messages[d][24:48, :], messages[d][48:56, :]),
            (high, -take(above[d][0:24, :], row), above[d][24:32, :]),
        )
        for f, (lanes, rows, target) in zip((2 * d, 2 * d + 1), sides):
            exists = there[f].astype(F32)
            pad[SUBS * (f + 1):SUBS * (f + 1) + 24, lanes] = rows * exists
            targets.append(target * exists)
    high, low = halves(pad[...])
    gh_ref[...] = high
    gl_ref[...] = low
    lanes = lax.broadcasted_iota(jnp.int32, (8, FD), 1)
    rows = lax.broadcasted_iota(jnp.int32, (COARSE, FD), 0)
    for half in range(2):
        wanted = jnp.full((8, FD), -1.0, F32)
        for n in range(4 * half, min(4 * half + 4, 7)):
            wanted = jnp.where(lanes // SUBS == n % 4, targets[n], wanted)
        wanted = jnp.broadcast_to(wanted[0:1, :].astype(jnp.int32), (COARSE, FD))
        pick_ref[:, half * FD:(half + 1) * FD] = (rows == wanted).astype(F32).astype(BF16)
    sum_kernel(state_ref, gh_ref, gl_ref, pick_ref, out_ref)


def late_kernel(table, diag_ref, couple_ref, inverse_ref, gh_ref, gl_ref, pick_ref, _, fh_ref, fl_ref, kh_ref,
                kl_ref, gh2_ref, gl2_ref, pick2_ref):
    for ref, again_ref in ((gh_ref, gh2_ref), (gl_ref, gl2_ref), (pick_ref, pick2_ref)):
        again_ref[...] = ref[...]
    put_dense(table, diag_ref, couple_ref, fh_ref, fl_ref)
    count = inverse_ref.shape[0]
    high, low = halves(inverse_ref[...])
    for ref, piece in ((kh_ref, high), (kl_ref, low)):
        ref[...] = jnp.zeros_like(ref)
        ref[0:count, 0:count] = piece


def face_sum(x, faces=range(6)):
    total = None
    for f in faces:
        total = face(x, f) if total is None else total + face(x, f)
    return total


def payload_places():
    for c in range(CASES):
        for b in range(COARSE // FD):
            spot, row = divmod(c * (COARSE // FD) + b, 3)
            yield c, b, spot, slice(row, row + 1)


def put_payload(out_ref, gathered, norm):
    lanes = lax.broadcasted_iota(jnp.int32, (CASES, FD), 1)
    blocks = [face(gathered, b) for b in range(COARSE // FD)]
    blocks[-1] = jnp.where(lanes == 64, norm, blocks[-1])
    for c, b, spot, row in payload_places():
        out_ref[spot, 4, row, :] = blocks[b][c:c + 1, :]


def sum_kernel(state_ref, gh_ref, gl_ref, pick_ref, out_ref):
    here, _, there = position()
    shown = state_ref[SHOWN, :]
    share = 0.25 * shown * mask_row(there)
    high, low = halves(share)
    both = dot_across(jnp.concatenate([high, low], 0), gh_ref[...])
    corner = both[:CASES] + both[CASES:] + dot_across(high, gl_ref[...])
    high, low = halves(corner)
    both = dot_across(jnp.concatenate([high, low], 0), pick_ref[...])
    norm = jnp.sum(face_sum(share * state_ref[RESIDUAL, :]), axis=1, keepdims=True)
    out_ref[...] = jnp.zeros_like(out_ref)
    put_payload(out_ref, both[:CASES] + both[CASES:], norm)
    for f, by in enumerate(steps()):
        @pl.when(there[f])
        def _():
            put_rows(out_ref, here + by, face(shown, f))


def put_layers(out_ref, total, flexed_ref, layer, there):
    out_ref[...] = jnp.zeros_like(out_ref)
    for i in range(out_ref.shape[0]):
        out_ref[i, 4] = total
    for f, by in ((4, -1), (5, 1)):
        @pl.when(there[f])
        def _():
            put_rows(out_ref, layer + by, flexed_ref[:, f * FD:(f + 1) * FD])


def flex_kernel(first, state_ref, slots_ref, below_ref, above_ref, fh_ref, fl_ref, z_ref, flexed_ref,
                out_ref, turn):
    here, layer, there = position()
    across = []
    for f, by in enumerate(steps()):
        across.append(take_rows(slots_ref, jnp.where(there[f], here + by, here)))
    across += [below_ref[...], above_ref[0:CASES, :]]
    z = 0.25 * (state_ref[SHOWN, :] + jnp.concatenate(across, axis=1)) * mask_row(there)
    z_ref[...] = z
    flexed = apply_dense(z, state_ref, fh_ref, fl_ref)
    flexed_ref[...] = flexed
    turn[...] = jnp.zeros_like(turn)
    turn[0:CASES, :] = face_sum(z * flexed)
    if not first:
        turn[CASES:2 * CASES, :] = (
            face_sum(z * state_ref[APPLIED, :], (1, 3, 5))
            + face_sum(state_ref[SEARCH, :] * flexed)
        )
    sums = jnp.sum(turn[...].T, axis=0, keepdims=True)
    total = jnp.sum(slots_ref[:, 4], axis=0)
    rows = lax.broadcasted_iota(jnp.int32, total.shape, 0)
    total = jnp.where(rows == 3, jnp.broadcast_to(sums, total.shape), total)
    put_layers(out_ref, total, flexed_ref, layer, there)


def share_kernel(layers_ref, flexed_ref, out_ref):
    here, _, there = position()
    total = jnp.sum(layers_ref[:, 4], axis=0)
    out_ref[...] = jnp.zeros_like(out_ref)
    for i in range(out_ref.shape[0]):
        out_ref[i, 4] = total
    for f, by in enumerate(steps()):
        @pl.when(there[f])
        def _():
            put_rows(out_ref, here + by, flexed_ref[:, f * FD:(f + 1) * FD])


def step_kernel(first, last, slots_ref, layers_ref, flexed_ref, z_ref, state_ref, kh_ref, kl_ref,
                gh_ref, gl_ref, pick_ref, *rest):
    rest, whole = rest[:-1], rest[-1]
    here, layer, there = position()
    across = []
    for f, by in enumerate(steps()):
        across.append(take_rows(slots_ref, jnp.where(there[f], here + by, here)))
    for f, by in ((4, -1), (5, 1)):
        across.append(take_rows(layers_ref, jnp.where(there[f], layer + by, layer)))
    mask = mask_row(there)
    applied = (flexed_ref[...] + jnp.concatenate(across, axis=1)) * mask
    search = z_ref[...]
    for c, b, spot, row in payload_places():
        whole[c:c + 1, b * FD:(b + 1) * FD] = slots_ref[spot, 4, row, :]
    load = whole[...]
    norm = load[:, COARSE - 64:COARSE - 63]
    sums = jnp.sum(slots_ref[:, 4], axis=0)[3:4, :]
    sums = jnp.broadcast_to(sums, (FD, FD)).T
    energy, cross = sums[0:CASES, 0:1], sums[CASES:2 * CASES, 0:1]
    lanes = lax.broadcasted_iota(jnp.int32, load.shape, 1)
    load = jnp.where(lanes < 3 * AGGREGATES, load, 0.0)
    if not first:
        scale = state_ref[REST, 0:FD]
        beta = norm / scale[:, 0:1]
        energy = energy + beta * cross + beta * beta * scale[:, 1:2]
        applied = applied + beta * state_ref[APPLIED, :]
        search = search + beta * state_ref[SEARCH, :]
        load = load + beta * state_ref[LOAD, 0:COARSE]
    coarse = dot_split(load, kh_ref, kl_ref)
    step = norm / (energy + jnp.sum(load * coarse, axis=1, keepdims=True))
    corner = dot_exact(coarse, pick_ref[...])
    correction = dot_split(corner, gh_ref, gl_ref) * mask
    residual = state_ref[RESIDUAL, :] - step * (applied + correction)
    moved = step * search
    if last:
        multipliers_ref, left_ref = rest
        for d in range(3):
            before = state_ref[REST, (d + 1) * FD:(d + 2) * FD]
            multipliers_ref[d] = before + face(moved, 2 * d + 1)
            left_ref[d] = face(residual, 2 * d + 1)
        return
    dh_ref, dl_ref, new_ref, down_ref, up_ref = rest
    new_ref[RESIDUAL, :] = residual
    shown = apply_dense(residual, state_ref, dh_ref, dl_ref)
    new_ref[SHOWN, :] = shown
    down_ref[...] = face(shown, 4)
    up_ref[...] = face(shown, 5)
    new_ref[SEARCH, :] = search
    new_ref[APPLIED, :] = applied
    new_ref[LOAD, 0:COARSE] = load
    new_ref[LOAD, COARSE:] = jnp.zeros((CASES, WIDE - COARSE), F32)
    lanes = lax.broadcasted_iota(jnp.int32, (CASES, FD), 1)
    scale = jnp.where(lanes == 0, norm, energy)
    parts = [scale]
    for d in range(3):
        parts.append(state_ref[REST, (d + 1) * FD:(d + 2) * FD] + face(moved, 2 * d + 1))
    new_ref[REST, :] = jnp.concatenate(parts + [scale, scale], axis=1)
    new_ref[ORDERS:ORDERS + 8, :] = state_ref[ORDERS:ORDERS + 8, :]


def passed_along(shard, axis, by):
    peers = lax.axis_size(axis)
    pairs = [(i, i + by) for i in range(peers) if 0 <= i + by < peers]
    return lax.ppermute(shard, axis, pairs)


def swapped(slots, axes):
    return lax.all_to_all(slots, axes, 0, 0)


def body(
    jump_rhs,
    flex_diag,
    flex_couple,
    dirichlet_diag,
    dirichlet_couple,
    face_pairs,
    corner_coupling,
    coarse_ids,
    partner,
    coarse_inverse,
):
    gx, gy, gz = (lax.axis_size(a) for a in AXES)
    plane = gx * gy
    rhs = jump_rhs.reshape(3, CASES, FD)
    coupling = corner_coupling.reshape(24, WIDE)
    square = (WIDE, WIDE)
    wide = (CASES, WIDE)

    width = ((0, 0),) * 4
    table = jnp.concatenate(
        [
            jnp.swapaxes(partner, 2, 3),
            jnp.pad(coarse_ids[:, :, :, None, :], width + ((0, FD - 8),)),
            jnp.pad(jnp.transpose(face_pairs, (0, 1, 4, 2, 3)), width + ((0, FD - 6),)),
        ],
        axis=2,
    )
    *ups, dx, dy, dz = call(
        prep_kernel, [((56, FD), F32)] * 3 + [((32, FD), F32)] * 3,
        [table, rhs, coupling],
    )
    messages = [passed_along(m, a, 1) for m, a in zip(ups, AXES)]
    above = [passed_along(m, a, -1) for m, a in zip((dx, dy), AXES)]
    blocks = [b.reshape(6, FD, FD) for b in (dirichlet_diag, dirichlet_couple, flex_diag, flex_couple)]
    dirichlet = call(
        dense_kernel, [(square, BF16)] * 2, [table] + blocks[:2], specs=[SMEM]
    )
    state, down, up = call(
        start_kernel,
        [(STATE, F32), ((CASES + 32, FD), F32), ((CASES, FD), F32)],
        [*ups, *messages, dz, *dirichlet],
    )
    stacked = (plane, 5, 4, FD)

    for iteration in range(ITERS):
        first, last = iteration == 0, iteration + 1 == ITERS
        below = passed_along(up, "gz", 1)
        over = passed_along(down, "gz", -1)
        if first:
            *joint, slots = call(
                joint_kernel,
                [((CORNERS, WIDE), BF16)] * 2 + [((COARSE, CORNERS), BF16), (stacked, F32)],
                [*ups, *messages, dx, dy, dz, *above, over, state],
                scratch=[pltpu.VMEM((CORNERS, WIDE), F32)],
            )
        else:
            (slots,) = call(sum_kernel, [(stacked, F32)], [state, *joint])
        if not last:
            slots, below, over = lax.optimization_barrier((slots, below, over))
        slots = swapped(slots, PLANE)
        if first:
            late = call(
                late_kernel,
                [(square, BF16)] * 2 + [((COARSE, COARSE), BF16)] * 2
                + [((CORNERS, WIDE), BF16)] * 2 + [((COARSE, CORNERS), BF16)],
                [table] + blocks[2:] + [coarse_inverse, *joint, slots],
                specs=[SMEM] + [VMEM] * 6 + [pl.BlockSpec(memory_space=pl.ANY)],
            )
            flex, inverse, again = late[:2], late[2:4], late[4:]
        z, flexed, layers = call(
            functools.partial(flex_kernel, first),
            [(wide, F32), (wide, F32), ((gz, 5, 4, FD), F32)],
            [state, slots, below, over, *flex],
            scratch=[pltpu.VMEM((FD, FD), F32)],
        )
        layers = swapped(layers, "gz")
        (slots,) = call(share_kernel, [(stacked, F32)], [layers, flexed])
        slots = swapped(slots, PLANE)
        common = [slots, layers, flexed, z, state, *inverse, *(again if last else joint)]
        kernel = functools.partial(step_kernel, first, last)
        scratch = [pltpu.VMEM((CASES, COARSE), F32)]
        if last:
            multipliers, left = call(kernel, [((3, CASES, FD), F32)] * 2, common, scratch=scratch)
            break
        state, down, up = call(
            kernel, [(STATE, F32)] + [((CASES, FD), F32)] * 2, common + [*dirichlet], scratch=scratch
        )
    return multipliers.reshape(jump_rhs.shape), left.reshape(jump_rhs.shape)


def solution(mesh):
    placed = (
        P("gx", "gy", "gz", None, None, None),
        P("gx", "gy", "gz", None, None, None),
        P("gx", "gy", "gz", None, None, None),
        P("gx", "gy", "gz", None, None, None),
        P("gx", "gy", "gz", None, None, None),
        P("gx", "gy", "gz", None, None),
        P("gx", "gy", "gz", None, None),
        P("gx", "gy", "gz", None),
        P("gx", "gy", "gz", None, None),
        P(),
    )
    return jax.shard_map(
        body,
        mesh=mesh,
        in_specs=placed,
        out_specs=(P("gx", "gy", "gz", None, None, None), P("gx", "gy", "gz", None, None, None)),
        check_vma=False,
    )
```

```python
import functools

import jax
import jax.numpy as jnp
from jax import lax
from jax.experimental import pallas as pl
from jax.experimental.pallas import tpu as pltpu
from jax.sharding import PartitionSpec as P

ITERS = 3
CASES = 16
FD = 128
WIDE = 6 * FD
AGGREGATES = 192
COARSE = 640
SUBS = 32
CORNERS = 256
AXES = ("gx", "gy", "gz")
PLANE = ("gx", "gy")
F32 = jnp.float32
BF16 = jnp.bfloat16
VMEM = pl.BlockSpec(memory_space=pltpu.VMEM)
SMEM = pl.BlockSpec(memory_space=pltpu.SMEM)


def call(kernel, outs, args, specs=(), scratch=()):
    return pl.pallas_call(
        kernel,
        out_shape=[jax.ShapeDtypeStruct(shape, dtype) for shape, dtype in outs],
        in_specs=list(specs) + [VMEM] * (len(args) - len(specs)),
        out_specs=[VMEM] * len(outs),
        scratch_shapes=list(scratch),
        compiler_params=pltpu.CompilerParams(vmem_limit_bytes=40 * 1024 * 1024),
    )(*args)


def halves(x):
    high = x.astype(BF16)
    return high, (x - high.astype(F32)).astype(BF16)


def dot_exact(x, selector):
    rows = x.shape[0]
    high, low = halves(x)
    both = jnp.dot(jnp.concatenate([high, low], 0), selector, preferred_element_type=F32)
    return both[:rows] + both[rows:]


def dot_across(x, matrix):
    return lax.dot_general(x, matrix, (((1,), (1,)), ((), ())), preferred_element_type=F32)


def dot_split(x, high_ref, low_ref):
    rows = x.shape[0]
    high, low = halves(x)
    both = jnp.dot(jnp.concatenate([high, low], 0), high_ref[...], preferred_element_type=F32)
    rest = jnp.dot(high, low_ref[...], preferred_element_type=F32)
    return both[:rows] + both[rows:] + rest


def face(x, f):
    return x[:, f * FD:(f + 1) * FD]


def take(x, row):
    index = jnp.broadcast_to(row.astype(jnp.int32), x.shape)
    return jnp.take_along_axis(x, index, axis=1, mode="promise_in_bounds")


def lower_changed(x, rows):
    parts = []
    for d in range(3):
        parts.append(-take(face(x, 2 * d), rows[d]))
        parts.append(face(x, 2 * d + 1))
    return jnp.concatenate(parts, axis=1)


RESIDUAL, SHOWN, SEARCH, APPLIED, LOAD, REST = (slice(CASES * i, CASES * (i + 1)) for i in range(6))
ORDERS = 6 * CASES
STATE = (ORDERS + 8, WIDE)


def apply_dense(field, state_ref, high_ref, low_ref):
    orders = state_ref[ORDERS:ORDERS + 8, :]
    partner = [face(orders[0:1, :], d) for d in range(3)]
    inverse = [face(orders[1:2, :], d) for d in range(3)]
    loads = lower_changed(field, inverse)
    return lower_changed(dot_split(loads, high_ref, low_ref), partner)


def position():
    gy = lax.axis_size("gy")
    places = [(lax.axis_index(a), lax.axis_size(a)) for a in ("gx", "gy", "gz")]
    there = []
    for place, size in places:
        there += [place > 0, place < size - 1]
    return places[0][0] * gy + places[1][0], places[2][0], there


def steps():
    gy = lax.axis_size("gy")
    return (-gy, gy, -1, 1)


def mask_row(there):
    return jnp.concatenate([jnp.full((1, FD), t.astype(F32)) for t in there], axis=1)


def put_rows(slots_ref, spot, rows):
    for q in range(4):
        slots_ref[spot, q] = rows[4 * q:4 * q + 4, :]


def take_rows(slots_ref, spot):
    return jnp.concatenate([slots_ref[spot, q] for q in range(4)], axis=0)


def target_rows(ids_row):
    row = lax.broadcasted_iota(jnp.int32, (8, FD), 1) % SUBS
    ids = take(jnp.broadcast_to(ids_row.astype(F32), (8, FD)), jnp.minimum(row // 3, 7))
    return jnp.where(row < 24, ids + (row % 3 * AGGREGATES).astype(F32), -1.0)


def prep_kernel(table_ref, rhs_ref, coupling_ref, *message_refs):
    _, _, there = position()
    target = target_rows(table_ref[0, 0, 3])
    for d in range(3):
        up_ref, down_ref = message_refs[d], message_refs[3 + d]
        row = table_ref[0, 0, d]
        up_ref[0:CASES, :] = rhs_ref[d] * there[2 * d + 1].astype(F32)
        wanted = lax.broadcasted_iota(jnp.int32, (FD, FD), 0)
        hits = (wanted == jnp.broadcast_to(row, (FD, FD))).astype(F32).astype(BF16)
        count = lax.broadcasted_iota(jnp.int32, (16, FD), 1).astype(F32).astype(BF16)
        up_ref[CASES:CASES + 8, :] = jnp.zeros((8, FD), F32)
        up_ref[CASES:CASES + 1, :] = row.astype(F32)
        up_ref[CASES + 1:CASES + 2, :] = dot_across(count, hits)[0:1, :]
        up_ref[24:48, :] = coupling_ref[:, (2 * d + 1) * FD:(2 * d + 2) * FD]
        up_ref[48:56, :] = target
        down_ref[0:24, :] = coupling_ref[:, 2 * d * FD:(2 * d + 1) * FD]
        down_ref[24:32, :] = target


def put_dense(table, diag_ref, couple_ref, high_ref, low_ref):
    high_ref[...] = jnp.zeros_like(high_ref)
    low_ref[...] = jnp.zeros_like(low_ref)

    def put(rows, cols, block):
        high, low = halves(block)
        high_ref[pl.ds(rows, FD), pl.ds(cols, FD)] = high
        low_ref[pl.ds(rows, FD), pl.ds(cols, FD)] = low

    for f in range(6):
        put(f * FD, f * FD, diag_ref[f])
    for k in range(6):
        first = pl.multiple_of(table[0, 0, 4, 0, k] * FD, FD)
        second = pl.multiple_of(table[0, 0, 5, 0, k] * FD, FD)
        block = couple_ref[k]
        put(second, first, block)
        put(first, second, block.T)


def dense_kernel(table, diag_ref, couple_ref, high_ref, low_ref):
    put_dense(table, diag_ref, couple_ref, high_ref, low_ref)


def start_kernel(ux_ref, uy_ref, uz_ref, mx_ref, my_ref, mz_ref, dz_ref, dh_ref, dl_ref, state_ref,
                 down_ref, up_ref):
    own, messages = (ux_ref, uy_ref, uz_ref), (mx_ref, my_ref, mz_ref)
    state_ref[...] = jnp.zeros_like(state_ref)
    parts = []
    for d in range(3):
        parts += [messages[d][0:CASES, :], own[d][0:CASES, :]]
        state_ref[ORDERS:ORDERS + 8, d * FD:(d + 1) * FD] = messages[d][CASES:CASES + 8, :]
    field = jnp.concatenate(parts, axis=1)
    state_ref[RESIDUAL, :] = field
    shown = apply_dense(field, state_ref, dh_ref, dl_ref)
    state_ref[SHOWN, :] = shown
    down_ref[0:CASES, :] = face(shown, 4)
    down_ref[CASES:CASES + 32, :] = dz_ref[...]
    up_ref[...] = face(shown, 5)


def joint_kernel(ux_ref, uy_ref, uz_ref, mx_ref, my_ref, mz_ref, dx_ref, dy_ref, dz_ref, nx_ref, ny_ref,
                 over_ref, state_ref, gh_ref, gl_ref, pick_ref, out_ref, pad):
    _, _, there = position()
    own, messages, lower = (ux_ref, uy_ref, uz_ref), (mx_ref, my_ref, mz_ref), (dx_ref, dy_ref, dz_ref)
    above = (nx_ref[...], ny_ref[...], over_ref[CASES:CASES + 32, :])
    pad[...] = jnp.zeros_like(pad)
    targets = [own[0][48:56, :]]
    for d in range(3):
        row = own[d][CASES:CASES + 1, :]
        low, high = slice(2 * d * FD, (2 * d + 1) * FD), slice((2 * d + 1) * FD, (2 * d + 2) * FD)
        pad[0:24, low] = -take(lower[d][0:24, :], messages[d][CASES:CASES + 1, :])
        pad[0:24, high] = own[d][24:48, :]
        sides = (
            (low, messages[d][24:48, :], messages[d][48:56, :]),
            (high, -take(above[d][0:24, :], row), above[d][24:32, :]),
        )
        for f, (lanes, rows, target) in zip((2 * d, 2 * d + 1), sides):
            exists = there[f].astype(F32)
            pad[SUBS * (f + 1):SUBS * (f + 1) + 24, lanes] = rows * exists
            targets.append(target * exists)
    high, low = halves(pad[...])
    gh_ref[...] = high
    gl_ref[...] = low
    lanes = lax.broadcasted_iota(jnp.int32, (8, FD), 1)
    rows = lax.broadcasted_iota(jnp.int32, (COARSE, FD), 0)
    for half in range(2):
        wanted = jnp.full((8, FD), -1.0, F32)
        for n in range(4 * half, min(4 * half + 4, 7)):
            wanted = jnp.where(lanes // SUBS == n % 4, targets[n], wanted)
        wanted = jnp.broadcast_to(wanted[0:1, :].astype(jnp.int32), (COARSE, FD))
        pick_ref[:, half * FD:(half + 1) * FD] = (rows == wanted).astype(F32).astype(BF16)
    sum_kernel(state_ref, gh_ref, gl_ref, pick_ref, out_ref)


def late_kernel(table, diag_ref, couple_ref, inverse_ref, gh_ref, gl_ref, pick_ref, _, fh_ref, fl_ref, kh_ref,
                kl_ref, gh2_ref, gl2_ref, pick2_ref):
    for ref, again_ref in ((gh_ref, gh2_ref), (gl_ref, gl2_ref), (pick_ref, pick2_ref)):
        again_ref[...] = ref[...]
    put_dense(table, diag_ref, couple_ref, fh_ref, fl_ref)
    count = inverse_ref.shape[0]
    high, low = halves(inverse_ref[...])
    for ref, piece in ((kh_ref, high), (kl_ref, low)):
        ref[...] = jnp.zeros_like(ref)
        ref[0:count, 0:count] = piece


def face_sum(x, faces=range(6)):
    total = None
    for f in faces:
        total = face(x, f) if total is None else total + face(x, f)
    return total


def payload_places():
    for c in range(CASES):
        for b in range(COARSE // FD):
            spot, row = divmod(c * (COARSE // FD) + b, 3)
            yield c, b, spot, slice(row, row + 1)


def put_payload(out_ref, gathered, norm):
    lanes = lax.broadcasted_iota(jnp.int32, (CASES, FD), 1)
    blocks = [face(gathered, b) for b in range(COARSE // FD)]
    blocks[-1] = jnp.where(lanes == 64, norm, blocks[-1])
    for c, b, spot, row in payload_places():
        out_ref[spot, 4, row, :] = blocks[b][c:c + 1, :]


def sum_kernel(state_ref, gh_ref, gl_ref, pick_ref, out_ref):
    here, _, there = position()
    shown = state_ref[SHOWN, :]
    share = 0.25 * shown * mask_row(there)
    high, low = halves(share)
    both = dot_across(jnp.concatenate([high, low], 0), gh_ref[...])
    corner = both[:CASES] + both[CASES:] + dot_across(high, gl_ref[...])
    high, low = halves(corner)
    both = dot_across(jnp.concatenate([high, low], 0), pick_ref[...])
    norm = jnp.sum(face_sum(share * state_ref[RESIDUAL, :]), axis=1, keepdims=True)
    out_ref[...] = jnp.zeros_like(out_ref)
    put_payload(out_ref, both[:CASES] + both[CASES:], norm)
    for f, by in enumerate(steps()):
        @pl.when(there[f])
        def _():
            put_rows(out_ref, here + by, face(shown, f))


def put_layers(out_ref, total, flexed_ref, layer, there):
    out_ref[...] = jnp.zeros_like(out_ref)
    for i in range(out_ref.shape[0]):
        out_ref[i, 4] = total
    for f, by in ((4, -1), (5, 1)):
        @pl.when(there[f])
        def _():
            put_rows(out_ref, layer + by, flexed_ref[:, f * FD:(f + 1) * FD])


def flex_kernel(first, last, state_ref, slots_ref, below_ref, above_ref, fh_ref, fl_ref, z_ref, flexed_ref,
                out_ref, turn, *apart):
    here, layer, there = position()
    spots = [jnp.where(there[f], here + by, here) for f, by in enumerate(steps())]
    if last:
        faces, shares, sems = apart
        copies = [
            pltpu.make_async_copy(slots_ref.at[spot, pl.ds(0, 4)], faces.at[f], sems.at[f])
            for f, spot in enumerate(spots)
        ]
        copies.append(pltpu.make_async_copy(slots_ref.at[:, 4], shares, sems.at[4]))
        for copy in copies:
            copy.start()
        for copy in copies:
            copy.wait()
        across = [take_rows(faces, f) for f in range(4)]
    else:
        across = [take_rows(slots_ref, spot) for spot in spots]
    across += [below_ref[...], above_ref[0:CASES, :]]
    z = 0.25 * (state_ref[SHOWN, :] + jnp.concatenate(across, axis=1)) * mask_row(there)
    z_ref[...] = z
    flexed = apply_dense(z, state_ref, fh_ref, fl_ref)
    flexed_ref[...] = flexed
    turn[...] = jnp.zeros_like(turn)
    turn[0:CASES, :] = face_sum(z * flexed)
    if not first:
        turn[CASES:2 * CASES, :] = (
            face_sum(z * state_ref[APPLIED, :], (1, 3, 5))
            + face_sum(state_ref[SEARCH, :] * flexed)
        )
    sums = jnp.sum(turn[...].T, axis=0, keepdims=True)
    total = jnp.sum(shares[...] if last else slots_ref[:, 4], axis=0)
    rows = lax.broadcasted_iota(jnp.int32, total.shape, 0)
    total = jnp.where(rows == 3, jnp.broadcast_to(sums, total.shape), total)
    put_layers(out_ref, total, flexed_ref, layer, there)


def share_kernel(layers_ref, flexed_ref, out_ref):
    here, _, there = position()
    total = jnp.sum(layers_ref[:, 4], axis=0)
    out_ref[...] = jnp.zeros_like(out_ref)
    for i in range(out_ref.shape[0]):
        out_ref[i, 4] = total
    for f, by in enumerate(steps()):
        @pl.when(there[f])
        def _():
            put_rows(out_ref, here + by, flexed_ref[:, f * FD:(f + 1) * FD])


def step_kernel(first, last, slots_ref, layers_ref, flexed_ref, z_ref, state_ref, kh_ref, kl_ref,
                gh_ref, gl_ref, pick_ref, *rest):
    rest, whole = rest[:-1], rest[-1]
    here, layer, there = position()
    across = []
    for f, by in enumerate(steps()):
        across.append(take_rows(slots_ref, jnp.where(there[f], here + by, here)))
    for f, by in ((4, -1), (5, 1)):
        across.append(take_rows(layers_ref, jnp.where(there[f], layer + by, layer)))
    mask = mask_row(there)
    applied = (flexed_ref[...] + jnp.concatenate(across, axis=1)) * mask
    search = z_ref[...]
    for c, b, spot, row in payload_places():
        whole[c:c + 1, b * FD:(b + 1) * FD] = slots_ref[spot, 4, row, :]
    load = whole[...]
    norm = load[:, COARSE - 64:COARSE - 63]
    sums = jnp.sum(slots_ref[:, 4], axis=0)[3:4, :]
    sums = jnp.broadcast_to(sums, (FD, FD)).T
    energy, cross = sums[0:CASES, 0:1], sums[CASES:2 * CASES, 0:1]
    lanes = lax.broadcasted_iota(jnp.int32, load.shape, 1)
    load = jnp.where(lanes < 3 * AGGREGATES, load, 0.0)
    if not first:
        scale = state_ref[REST, 0:FD]
        beta = norm / scale[:, 0:1]
        energy = energy + beta * cross + beta * beta * scale[:, 1:2]
        applied = applied + beta * state_ref[APPLIED, :]
        search = search + beta * state_ref[SEARCH, :]
        load = load + beta * state_ref[LOAD, 0:COARSE]
    coarse = dot_split(load, kh_ref, kl_ref)
    step = norm / (energy + jnp.sum(load * coarse, axis=1, keepdims=True))
    corner = dot_exact(coarse, pick_ref[...])
    correction = dot_split(corner, gh_ref, gl_ref) * mask
    residual = state_ref[RESIDUAL, :] - step * (applied + correction)
    moved = step * search
    if last:
        multipliers_ref, left_ref = rest
        for d in range(3):
            before = state_ref[REST, (d + 1) * FD:(d + 2) * FD]
            multipliers_ref[d] = before + face(moved, 2 * d + 1)
            left_ref[d] = face(residual, 2 * d + 1)
        return
    dh_ref, dl_ref, new_ref, down_ref, up_ref = rest
    new_ref[RESIDUAL, :] = residual
    shown = apply_dense(residual, state_ref, dh_ref, dl_ref)
    new_ref[SHOWN, :] = shown
    down_ref[...] = face(shown, 4)
    up_ref[...] = face(shown, 5)
    new_ref[SEARCH, :] = search
    new_ref[APPLIED, :] = applied
    new_ref[LOAD, 0:COARSE] = load
    new_ref[LOAD, COARSE:] = jnp.zeros((CASES, WIDE - COARSE), F32)
    lanes = lax.broadcasted_iota(jnp.int32, (CASES, FD), 1)
    scale = jnp.where(lanes == 0, norm, energy)
    parts = [scale]
    for d in range(3):
        parts.append(state_ref[REST, (d + 1) * FD:(d + 2) * FD] + face(moved, 2 * d + 1))
    new_ref[REST, :] = jnp.concatenate(parts + [scale, scale], axis=1)
    new_ref[ORDERS:ORDERS + 8, :] = state_ref[ORDERS:ORDERS + 8, :]


def passed_along(shard, axis, by):
    peers = lax.axis_size(axis)
    pairs = [(i, i + by) for i in range(peers) if 0 <= i + by < peers]
    return lax.ppermute(shard, axis, pairs)


def swapped(slots, axes):
    return lax.all_to_all(slots, axes, 0, 0)


def body(
    jump_rhs,
    flex_diag,
    flex_couple,
    dirichlet_diag,
    dirichlet_couple,
    face_pairs,
    corner_coupling,
    coarse_ids,
    partner,
    coarse_inverse,
):
    gx, gy, gz = (lax.axis_size(a) for a in AXES)
    plane = gx * gy
    rhs = jump_rhs.reshape(3, CASES, FD)
    coupling = corner_coupling.reshape(24, WIDE)
    square = (WIDE, WIDE)
    wide = (CASES, WIDE)

    width = ((0, 0),) * 4
    table = jnp.concatenate(
        [
            jnp.swapaxes(partner, 2, 3),
            jnp.pad(coarse_ids[:, :, :, None, :], width + ((0, FD - 8),)),
            jnp.pad(jnp.transpose(face_pairs, (0, 1, 4, 2, 3)), width + ((0, FD - 6),)),
        ],
        axis=2,
    )
    *ups, dx, dy, dz = call(
        prep_kernel, [((56, FD), F32)] * 3 + [((32, FD), F32)] * 3,
        [table, rhs, coupling],
    )
    messages = [passed_along(m, a, 1) for m, a in zip(ups, AXES)]
    above = [passed_along(m, a, -1) for m, a in zip((dx, dy), AXES)]
    blocks = [b.reshape(6, FD, FD) for b in (dirichlet_diag, dirichlet_couple, flex_diag, flex_couple)]
    dirichlet = call(
        dense_kernel, [(square, BF16)] * 2, [table] + blocks[:2], specs=[SMEM]
    )
    state, down, up = call(
        start_kernel,
        [(STATE, F32), ((CASES + 32, FD), F32), ((CASES, FD), F32)],
        [*ups, *messages, dz, *dirichlet],
    )
    stacked = (plane, 5, 4, FD)

    for iteration in range(ITERS):
        first, last = iteration == 0, iteration + 1 == ITERS
        below = passed_along(up, "gz", 1)
        over = passed_along(down, "gz", -1)
        if first:
            *joint, slots = call(
                joint_kernel,
                [((CORNERS, WIDE), BF16)] * 2 + [((COARSE, CORNERS), BF16), (stacked, F32)],
                [*ups, *messages, dx, dy, dz, *above, over, state],
                scratch=[pltpu.VMEM((CORNERS, WIDE), F32)],
            )
        else:
            (slots,) = call(sum_kernel, [(stacked, F32)], [state, *joint])
        if not last:
            slots, below, over = lax.optimization_barrier((slots, below, over))
        slots = swapped(slots, PLANE)
        if first:
            late = call(
                late_kernel,
                [(square, BF16)] * 2 + [((COARSE, COARSE), BF16)] * 2
                + [((CORNERS, WIDE), BF16)] * 2 + [((COARSE, CORNERS), BF16)],
                [table] + blocks[2:] + [coarse_inverse, *joint, slots],
                specs=[SMEM] + [VMEM] * 6 + [pl.BlockSpec(memory_space=pl.ANY)],
            )
            flex, inverse, again = late[:2], late[2:4], late[4:]
        z, flexed, layers = call(
            functools.partial(flex_kernel, first, last),
            [(wide, F32), (wide, F32), ((gz, 5, 4, FD), F32)],
            [state, slots, below, over, *flex],
            specs=[VMEM, pl.BlockSpec(memory_space=pl.ANY)] if last else (),
            scratch=[pltpu.VMEM((FD, FD), F32)]
            + [pltpu.VMEM((4, 4, 4, FD), F32), pltpu.VMEM((plane, 4, FD), F32),
               pltpu.SemaphoreType.DMA((5,))] * last,
        )
        layers = swapped(layers, "gz")
        (slots,) = call(share_kernel, [(stacked, F32)], [layers, flexed])
        slots = swapped(slots, PLANE)
        common = [slots, layers, flexed, z, state, *inverse, *(again if last else joint)]
        kernel = functools.partial(step_kernel, first, last)
        scratch = [pltpu.VMEM((CASES, COARSE), F32)]
        if last:
            multipliers, left = call(kernel, [((3, CASES, FD), F32)] * 2, common, scratch=scratch)
            break
        state, down, up = call(
            kernel, [(STATE, F32)] + [((CASES, FD), F32)] * 2, common + [*dirichlet], scratch=scratch
        )
    return multipliers.reshape(jump_rhs.shape), left.reshape(jump_rhs.shape)


def solution(mesh):
    placed = (
        P("gx", "gy", "gz", None, None, None),
        P("gx", "gy", "gz", None, None, None),
        P("gx", "gy", "gz", None, None, None),
        P("gx", "gy", "gz", None, None, None),
        P("gx", "gy", "gz", None, None, None),
        P("gx", "gy", "gz", None, None),
        P("gx", "gy", "gz", None, None),
        P("gx", "gy", "gz", None),
        P("gx", "gy", "gz", None, None),
        P(),
    )
    return jax.shard_map(
        body,
        mesh=mesh,
        in_specs=placed,
        out_specs=(P("gx", "gy", "gz", None, None, None), P("gx", "gy", "gz", None, None, None)),
        check_vma=False,
    )
```

```python
import functools

import jax
import jax.numpy as jnp
from jax import lax
from jax.experimental import pallas as pl
from jax.experimental.pallas import tpu as pltpu
from jax.sharding import PartitionSpec as P

ITERS = 3
CASES = 16
FD = 128
WIDE = 6 * FD
AGGREGATES = 192
COARSE = 640
SUBS = 32
CORNERS = 256
AXES = ("gx", "gy", "gz")
PLANE = ("gx", "gy")
F32 = jnp.float32
BF16 = jnp.bfloat16
VMEM = pl.BlockSpec(memory_space=pltpu.VMEM)
SMEM = pl.BlockSpec(memory_space=pltpu.SMEM)


def call(kernel, outs, args, specs=(), scratch=()):
    return pl.pallas_call(
        kernel,
        out_shape=[jax.ShapeDtypeStruct(shape, dtype) for shape, dtype in outs],
        in_specs=list(specs) + [VMEM] * (len(args) - len(specs)),
        out_specs=[VMEM] * len(outs),
        scratch_shapes=list(scratch),
        compiler_params=pltpu.CompilerParams(vmem_limit_bytes=40 * 1024 * 1024),
    )(*args)


def halves(x):
    high = x.astype(BF16)
    return high, (x - high.astype(F32)).astype(BF16)


def dot_exact(x, selector):
    rows = x.shape[0]
    high, low = halves(x)
    both = jnp.dot(jnp.concatenate([high, low], 0), selector, preferred_element_type=F32)
    return both[:rows] + both[rows:]


def dot_across(x, matrix):
    return lax.dot_general(x, matrix, (((1,), (1,)), ((), ())), preferred_element_type=F32)


def dot_split(x, high_ref, low_ref):
    rows = x.shape[0]
    high, low = halves(x)
    both = jnp.dot(jnp.concatenate([high, low], 0), high_ref[...], preferred_element_type=F32)
    rest = jnp.dot(high, low_ref[...], preferred_element_type=F32)
    return both[:rows] + both[rows:] + rest


def face(x, f):
    return x[:, f * FD:(f + 1) * FD]


def take(x, row):
    index = jnp.broadcast_to(row.astype(jnp.int32), x.shape)
    return jnp.take_along_axis(x, index, axis=1, mode="promise_in_bounds")


def lower_changed(x, rows):
    parts = []
    for d in range(3):
        parts.append(-take(face(x, 2 * d), rows[d]))
        parts.append(face(x, 2 * d + 1))
    return jnp.concatenate(parts, axis=1)


RESIDUAL, SHOWN, SEARCH, APPLIED, LOAD, REST = (slice(CASES * i, CASES * (i + 1)) for i in range(6))
ORDERS = 6 * CASES
STATE = (ORDERS + 8, WIDE)


def apply_dense(field, state_ref, high_ref, low_ref):
    orders = state_ref[ORDERS:ORDERS + 8, :]
    partner = [face(orders[0:1, :], d) for d in range(3)]
    inverse = [face(orders[1:2, :], d) for d in range(3)]
    loads = lower_changed(field, inverse)
    return lower_changed(dot_split(loads, high_ref, low_ref), partner)


def position():
    gy = lax.axis_size("gy")
    places = [(lax.axis_index(a), lax.axis_size(a)) for a in ("gx", "gy", "gz")]
    there = []
    for place, size in places:
        there += [place > 0, place < size - 1]
    return places[0][0] * gy + places[1][0], places[2][0], there


def steps():
    gy = lax.axis_size("gy")
    return (-gy, gy, -1, 1)


def mask_row(there):
    return jnp.concatenate([jnp.full((1, FD), t.astype(F32)) for t in there], axis=1)


def put_rows(slots_ref, spot, rows):
    for q in range(4):
        slots_ref[spot, q] = rows[4 * q:4 * q + 4, :]


def take_rows(slots_ref, spot):
    return jnp.concatenate([slots_ref[spot, q] for q in range(4)], axis=0)


def target_rows(ids_row):
    row = lax.broadcasted_iota(jnp.int32, (8, FD), 1) % SUBS
    ids = take(jnp.broadcast_to(ids_row.astype(F32), (8, FD)), jnp.minimum(row // 3, 7))
    return jnp.where(row < 24, ids + (row % 3 * AGGREGATES).astype(F32), -1.0)


def prep_kernel(table_ref, rhs_ref, coupling_ref, *message_refs):
    _, _, there = position()
    target = target_rows(table_ref[0, 0, 3])
    for d in range(3):
        up_ref, down_ref = message_refs[d], message_refs[3 + d]
        row = table_ref[0, 0, d]
        up_ref[0:CASES, :] = rhs_ref[d] * there[2 * d + 1].astype(F32)
        wanted = lax.broadcasted_iota(jnp.int32, (FD, FD), 0)
        hits = (wanted == jnp.broadcast_to(row, (FD, FD))).astype(F32).astype(BF16)
        count = lax.broadcasted_iota(jnp.int32, (16, FD), 1).astype(F32).astype(BF16)
        up_ref[CASES:CASES + 8, :] = jnp.zeros((8, FD), F32)
        up_ref[CASES:CASES + 1, :] = row.astype(F32)
        up_ref[CASES + 1:CASES + 2, :] = dot_across(count, hits)[0:1, :]
        up_ref[24:48, :] = coupling_ref[:, (2 * d + 1) * FD:(2 * d + 2) * FD]
        up_ref[48:56, :] = target
        down_ref[0:24, :] = coupling_ref[:, 2 * d * FD:(2 * d + 1) * FD]
        down_ref[24:32, :] = target


def put_dense(table, diag_ref, couple_ref, high_ref, low_ref):
    high_ref[...] = jnp.zeros_like(high_ref)
    low_ref[...] = jnp.zeros_like(low_ref)

    def put(rows, cols, block):
        high, low = halves(block)
        high_ref[pl.ds(rows, FD), pl.ds(cols, FD)] = high
        low_ref[pl.ds(rows, FD), pl.ds(cols, FD)] = low

    for f in range(6):
        put(f * FD, f * FD, diag_ref[f])
    for k in range(6):
        first = pl.multiple_of(table[0, 0, 4, 0, k] * FD, FD)
        second = pl.multiple_of(table[0, 0, 5, 0, k] * FD, FD)
        block = couple_ref[k]
        put(second, first, block)
        put(first, second, block.T)


def dense_kernel(table, diag_ref, couple_ref, high_ref, low_ref):
    put_dense(table, diag_ref, couple_ref, high_ref, low_ref)


def start_kernel(ux_ref, uy_ref, uz_ref, mx_ref, my_ref, mz_ref, dz_ref, dh_ref, dl_ref, state_ref,
                 down_ref, up_ref):
    own, messages = (ux_ref, uy_ref, uz_ref), (mx_ref, my_ref, mz_ref)
    state_ref[...] = jnp.zeros_like(state_ref)
    parts = []
    for d in range(3):
        parts += [messages[d][0:CASES, :], own[d][0:CASES, :]]
        state_ref[ORDERS:ORDERS + 8, d * FD:(d + 1) * FD] = messages[d][CASES:CASES + 8, :]
    field = jnp.concatenate(parts, axis=1)
    state_ref[RESIDUAL, :] = field
    shown = apply_dense(field, state_ref, dh_ref, dl_ref)
    state_ref[SHOWN, :] = shown
    down_ref[0:CASES, :] = face(shown, 4)
    down_ref[CASES:CASES + 32, :] = dz_ref[...]
    up_ref[...] = face(shown, 5)


def joint_kernel(ux_ref, uy_ref, uz_ref, mx_ref, my_ref, mz_ref, dx_ref, dy_ref, dz_ref, nx_ref, ny_ref,
                 over_ref, state_ref, gh_ref, gl_ref, pick_ref, out_ref, pad):
    _, _, there = position()
    own, messages, lower = (ux_ref, uy_ref, uz_ref), (mx_ref, my_ref, mz_ref), (dx_ref, dy_ref, dz_ref)
    above = (nx_ref[...], ny_ref[...], over_ref[CASES:CASES + 32, :])
    pad[...] = jnp.zeros_like(pad)
    targets = [own[0][48:56, :]]
    for d in range(3):
        row = own[d][CASES:CASES + 1, :]
        low, high = slice(2 * d * FD, (2 * d + 1) * FD), slice((2 * d + 1) * FD, (2 * d + 2) * FD)
        pad[0:24, low] = -take(lower[d][0:24, :], messages[d][CASES:CASES + 1, :])
        pad[0:24, high] = own[d][24:48, :]
        sides = (
            (low, messages[d][24:48, :], messages[d][48:56, :]),
            (high, -take(above[d][0:24, :], row), above[d][24:32, :]),
        )
        for f, (lanes, rows, target) in zip((2 * d, 2 * d + 1), sides):
            exists = there[f].astype(F32)
            pad[SUBS * (f + 1):SUBS * (f + 1) + 24, lanes] = rows * exists
            targets.append(target * exists)
    high, low = halves(pad[...])
    gh_ref[...] = high
    gl_ref[...] = low
    lanes = lax.broadcasted_iota(jnp.int32, (8, FD), 1)
    rows = lax.broadcasted_iota(jnp.int32, (COARSE, FD), 0)
    for half in range(2):
        wanted = jnp.full((8, FD), -1.0, F32)
        for n in range(4 * half, min(4 * half + 4, 7)):
            wanted = jnp.where(lanes // SUBS == n % 4, targets[n], wanted)
        wanted = jnp.broadcast_to(wanted[0:1, :].astype(jnp.int32), (COARSE, FD))
        pick_ref[:, half * FD:(half + 1) * FD] = (rows == wanted).astype(F32).astype(BF16)
    sum_kernel(state_ref, gh_ref, gl_ref, pick_ref, out_ref)


def late_kernel(table, diag_ref, couple_ref, inverse_ref, gh_ref, gl_ref, pick_ref, _, fh_ref, fl_ref, kh_ref,
                kl_ref, gh2_ref, gl2_ref, pick2_ref):
    for ref, again_ref in ((gh_ref, gh2_ref), (gl_ref, gl2_ref), (pick_ref, pick2_ref)):
        again_ref[...] = ref[...]
    put_dense(table, diag_ref, couple_ref, fh_ref, fl_ref)
    count = inverse_ref.shape[0]
    high, low = halves(inverse_ref[...])
    for ref, piece in ((kh_ref, high), (kl_ref, low)):
        ref[...] = jnp.zeros_like(ref)
        ref[0:count, 0:count] = piece


def face_sum(x, faces=range(6)):
    total = None
    for f in faces:
        total = face(x, f) if total is None else total + face(x, f)
    return total


def payload_places():
    for c in range(CASES):
        for b in range(COARSE // FD):
            spot, row = divmod(c * (COARSE // FD) + b, 3)
            yield c, b, spot, slice(row, row + 1)


def put_payload(out_ref, gathered, norm):
    lanes = lax.broadcasted_iota(jnp.int32, (CASES, FD), 1)
    blocks = [face(gathered, b) for b in range(COARSE // FD)]
    blocks[-1] = jnp.where(lanes == 64, norm, blocks[-1])
    for c, b, spot, row in payload_places():
        out_ref[spot, 4, row, :] = blocks[b][c:c + 1, :]


def sum_kernel(state_ref, gh_ref, gl_ref, pick_ref, out_ref):
    here, _, there = position()
    shown = state_ref[SHOWN, :]
    share = 0.25 * shown * mask_row(there)
    high, low = halves(share)
    both = dot_across(jnp.concatenate([high, low], 0), gh_ref[...])
    corner = both[:CASES] + both[CASES:] + dot_across(high, gl_ref[...])
    high, low = halves(corner)
    both = dot_across(jnp.concatenate([high, low], 0), pick_ref[...])
    norm = jnp.sum(face_sum(share * state_ref[RESIDUAL, :]), axis=1, keepdims=True)
    out_ref[...] = jnp.zeros_like(out_ref)
    put_payload(out_ref, both[:CASES] + both[CASES:], norm)
    for f, by in enumerate(steps()):
        @pl.when(there[f])
        def _():
            put_rows(out_ref, here + by, face(shown, f))


def put_layers(out_ref, total, flexed_ref, layer, there):
    out_ref[...] = jnp.zeros_like(out_ref)
    for i in range(out_ref.shape[0]):
        out_ref[i, 4] = total
    for f, by in ((4, -1), (5, 1)):
        @pl.when(there[f])
        def _():
            put_rows(out_ref, layer + by, flexed_ref[:, f * FD:(f + 1) * FD])


def flex_kernel(first, last, state_ref, slots_ref, below_ref, above_ref, fh_ref, fl_ref, z_ref, flexed_ref,
                out_ref, turn, *apart):
    here, layer, there = position()
    spots = [jnp.where(there[f], here + by, here) for f, by in enumerate(steps())]
    if last:
        faces, shares, sems = apart
        copies = [
            pltpu.make_async_copy(slots_ref.at[spot, pl.ds(0, 4)], faces.at[f], sems.at[f])
            for f, spot in enumerate(spots)
        ]
        copies.append(pltpu.make_async_copy(slots_ref.at[:, 4], shares, sems.at[4]))
        for copy in copies:
            copy.start()
        for copy in copies[:4]:
            copy.wait()
        across = [take_rows(faces, f) for f in range(4)]
    else:
        across = [take_rows(slots_ref, spot) for spot in spots]
    across += [below_ref[...], above_ref[0:CASES, :]]
    z = 0.25 * (state_ref[SHOWN, :] + jnp.concatenate(across, axis=1)) * mask_row(there)
    z_ref[...] = z
    flexed = apply_dense(z, state_ref, fh_ref, fl_ref)
    flexed_ref[...] = flexed
    turn[...] = jnp.zeros_like(turn)
    turn[0:CASES, :] = face_sum(z * flexed)
    if not first:
        turn[CASES:2 * CASES, :] = (
            face_sum(z * state_ref[APPLIED, :], (1, 3, 5))
            + face_sum(state_ref[SEARCH, :] * flexed)
        )
    sums = jnp.sum(turn[...].T, axis=0, keepdims=True)
    if last:
        copies[4].wait()
    total = jnp.sum(shares[...] if last else slots_ref[:, 4], axis=0)
    rows = lax.broadcasted_iota(jnp.int32, total.shape, 0)
    total = jnp.where(rows == 3, jnp.broadcast_to(sums, total.shape), total)
    put_layers(out_ref, total, flexed_ref, layer, there)


def share_kernel(layers_ref, flexed_ref, out_ref):
    here, _, there = position()
    total = jnp.sum(layers_ref[:, 4], axis=0)
    out_ref[...] = jnp.zeros_like(out_ref)
    for i in range(out_ref.shape[0]):
        out_ref[i, 4] = total
    for f, by in enumerate(steps()):
        @pl.when(there[f])
        def _():
            put_rows(out_ref, here + by, flexed_ref[:, f * FD:(f + 1) * FD])


def step_kernel(first, last, slots_ref, layers_ref, flexed_ref, z_ref, state_ref, kh_ref, kl_ref,
                gh_ref, gl_ref, pick_ref, *rest):
    rest, whole = rest[:-1], rest[-1]
    here, layer, there = position()
    across = []
    for f, by in enumerate(steps()):
        across.append(take_rows(slots_ref, jnp.where(there[f], here + by, here)))
    for f, by in ((4, -1), (5, 1)):
        across.append(take_rows(layers_ref, jnp.where(there[f], layer + by, layer)))
    mask = mask_row(there)
    applied = (flexed_ref[...] + jnp.concatenate(across, axis=1)) * mask
    search = z_ref[...]
    for c, b, spot, row in payload_places():
        whole[c:c + 1, b * FD:(b + 1) * FD] = slots_ref[spot, 4, row, :]
    load = whole[...]
    norm = load[:, COARSE - 64:COARSE - 63]
    sums = jnp.sum(slots_ref[:, 4], axis=0)[3:4, :]
    sums = jnp.broadcast_to(sums, (FD, FD)).T
    energy, cross = sums[0:CASES, 0:1], sums[CASES:2 * CASES, 0:1]
    lanes = lax.broadcasted_iota(jnp.int32, load.shape, 1)
    load = jnp.where(lanes < 3 * AGGREGATES, load, 0.0)
    if not first:
        scale = state_ref[REST, 0:FD]
        beta = norm / scale[:, 0:1]
        energy = energy + beta * cross + beta * beta * scale[:, 1:2]
        applied = applied + beta * state_ref[APPLIED, :]
        search = search + beta * state_ref[SEARCH, :]
        load = load + beta * state_ref[LOAD, 0:COARSE]
    coarse = dot_split(load, kh_ref, kl_ref)
    step = norm / (energy + jnp.sum(load * coarse, axis=1, keepdims=True))
    corner = dot_exact(coarse, pick_ref[...])
    correction = dot_split(corner, gh_ref, gl_ref) * mask
    residual = state_ref[RESIDUAL, :] - step * (applied + correction)
    moved = step * search
    if last:
        multipliers_ref, left_ref = rest
        for d in range(3):
            before = state_ref[REST, (d + 1) * FD:(d + 2) * FD]
            multipliers_ref[d] = before + face(moved, 2 * d + 1)
            left_ref[d] = face(residual, 2 * d + 1)
        return
    dh_ref, dl_ref, new_ref, down_ref, up_ref = rest
    new_ref[RESIDUAL, :] = residual
    shown = apply_dense(residual, state_ref, dh_ref, dl_ref)
    new_ref[SHOWN, :] = shown
    down_ref[...] = face(shown, 4)
    up_ref[...] = face(shown, 5)
    new_ref[SEARCH, :] = search
    new_ref[APPLIED, :] = applied
    new_ref[LOAD, 0:COARSE] = load
    new_ref[LOAD, COARSE:] = jnp.zeros((CASES, WIDE - COARSE), F32)
    lanes = lax.broadcasted_iota(jnp.int32, (CASES, FD), 1)
    scale = jnp.where(lanes == 0, norm, energy)
    parts = [scale]
    for d in range(3):
        parts.append(state_ref[REST, (d + 1) * FD:(d + 2) * FD] + face(moved, 2 * d + 1))
    new_ref[REST, :] = jnp.concatenate(parts + [scale, scale], axis=1)
    new_ref[ORDERS:ORDERS + 8, :] = state_ref[ORDERS:ORDERS + 8, :]


def passed_along(shard, axis, by):
    peers = lax.axis_size(axis)
    pairs = [(i, i + by) for i in range(peers) if 0 <= i + by < peers]
    return lax.ppermute(shard, axis, pairs)


def swapped(slots, axes):
    return lax.all_to_all(slots, axes, 0, 0)


def body(
    jump_rhs,
    flex_diag,
    flex_couple,
    dirichlet_diag,
    dirichlet_couple,
    face_pairs,
    corner_coupling,
    coarse_ids,
    partner,
    coarse_inverse,
):
    gx, gy, gz = (lax.axis_size(a) for a in AXES)
    plane = gx * gy
    rhs = jump_rhs.reshape(3, CASES, FD)
    coupling = corner_coupling.reshape(24, WIDE)
    square = (WIDE, WIDE)
    wide = (CASES, WIDE)

    width = ((0, 0),) * 4
    table = jnp.concatenate(
        [
            jnp.swapaxes(partner, 2, 3),
            jnp.pad(coarse_ids[:, :, :, None, :], width + ((0, FD - 8),)),
            jnp.pad(jnp.transpose(face_pairs, (0, 1, 4, 2, 3)), width + ((0, FD - 6),)),
        ],
        axis=2,
    )
    *ups, dx, dy, dz = call(
        prep_kernel, [((56, FD), F32)] * 3 + [((32, FD), F32)] * 3,
        [table, rhs, coupling],
    )
    messages = [passed_along(m, a, 1) for m, a in zip(ups, AXES)]
    above = [passed_along(m, a, -1) for m, a in zip((dx, dy), AXES)]
    blocks = [b.reshape(6, FD, FD) for b in (dirichlet_diag, dirichlet_couple, flex_diag, flex_couple)]
    dirichlet = call(
        dense_kernel, [(square, BF16)] * 2, [table] + blocks[:2], specs=[SMEM]
    )
    state, down, up = call(
        start_kernel,
        [(STATE, F32), ((CASES + 32, FD), F32), ((CASES, FD), F32)],
        [*ups, *messages, dz, *dirichlet],
    )
    stacked = (plane, 5, 4, FD)

    for iteration in range(ITERS):
        first, last = iteration == 0, iteration + 1 == ITERS
        below = passed_along(up, "gz", 1)
        over = passed_along(down, "gz", -1)
        if first:
            *joint, slots = call(
                joint_kernel,
                [((CORNERS, WIDE), BF16)] * 2 + [((COARSE, CORNERS), BF16), (stacked, F32)],
                [*ups, *messages, dx, dy, dz, *above, over, state],
                scratch=[pltpu.VMEM((CORNERS, WIDE), F32)],
            )
        else:
            (slots,) = call(sum_kernel, [(stacked, F32)], [state, *joint])
        if not last:
            slots, below, over = lax.optimization_barrier((slots, below, over))
        slots = swapped(slots, PLANE)
        if first:
            late = call(
                late_kernel,
                [(square, BF16)] * 2 + [((COARSE, COARSE), BF16)] * 2
                + [((CORNERS, WIDE), BF16)] * 2 + [((COARSE, CORNERS), BF16)],
                [table] + blocks[2:] + [coarse_inverse, *joint, slots],
                specs=[SMEM] + [VMEM] * 6 + [pl.BlockSpec(memory_space=pl.ANY)],
            )
            flex, inverse, again = late[:2], late[2:4], late[4:]
        z, flexed, layers = call(
            functools.partial(flex_kernel, first, last),
            [(wide, F32), (wide, F32), ((gz, 5, 4, FD), F32)],
            [state, slots, below, over, *flex],
            specs=[VMEM, pl.BlockSpec(memory_space=pl.ANY)] if last else (),
            scratch=[pltpu.VMEM((FD, FD), F32)]
            + [pltpu.VMEM((4, 4, 4, FD), F32), pltpu.VMEM((plane, 4, FD), F32),
               pltpu.SemaphoreType.DMA((5,))] * last,
        )
        layers = swapped(layers, "gz")
        (slots,) = call(share_kernel, [(stacked, F32)], [layers, flexed])
        slots = swapped(slots, PLANE)
        common = [slots, layers, flexed, z, state, *inverse, *(again if last else joint)]
        kernel = functools.partial(step_kernel, first, last)
        scratch = [pltpu.VMEM((CASES, COARSE), F32)]
        if last:
            multipliers, left = call(kernel, [((3, CASES, FD), F32)] * 2, common, scratch=scratch)
            break
        state, down, up = call(
            kernel, [(STATE, F32)] + [((CASES, FD), F32)] * 2, common + [*dirichlet], scratch=scratch
        )
    return multipliers.reshape(jump_rhs.shape), left.reshape(jump_rhs.shape)


def solution(mesh):
    placed = (
        P("gx", "gy", "gz", None, None, None),
        P("gx", "gy", "gz", None, None, None),
        P("gx", "gy", "gz", None, None, None),
        P("gx", "gy", "gz", None, None, None),
        P("gx", "gy", "gz", None, None, None),
        P("gx", "gy", "gz", None, None),
        P("gx", "gy", "gz", None, None),
        P("gx", "gy", "gz", None),
        P("gx", "gy", "gz", None, None),
        P(),
    )
    return jax.shard_map(
        body,
        mesh=mesh,
        in_specs=placed,
        out_specs=(P("gx", "gy", "gz", None, None, None), P("gx", "gy", "gz", None, None, None)),
        check_vma=False,
    )
```
